32 devices in a mesh: section: 2 (over core), dp: 4 (over z), seq: 4 (over y, x).
Axes of the slice: x: 2, y: 2, z: 4, core: 2. Of those that a mesh axis runs over, the one named last changes fastest.
Arguments:
- patches: bfloat16 [8, 96, 12, 768], P('dp', 'seq'), may hold values from -6 to 6
- queries: bfloat16 [8, 128, 768], P('dp'), may hold values from -6 to 6
- page_rows: int32 [8], P('dp'), may hold values from 1 to 8, as said below
- window_mask: int32 [8, 8, 1], P('dp', 'seq'), may hold values from 0 to 1, as said below
- query_lengths: int32 [8], P('dp'), may hold values from 1 to 128, as said below
- plan: int32 [4, 2], P('dp'), may hold values from 0 to 1, each once within a row
- norm_attn: bfloat16 [2, 768], P('section', ('dp', 'seq')), may hold values from 0.099609375 to 1.8984375
- norm_mlp: bfloat16 [2, 768], P('section', ('dp', 'seq')), may hold values from 0.099609375 to 1.8984375
- norm_query: bfloat16 [2, 768], P('section', ('dp', 'seq')), may hold values from 0.099609375 to 1.8984375
- attn_input: bfloat16 [2, 768, 2304], P('section', ('dp', 'seq')), may hold values from -0.21875 to 0.21875
- attn_output: bfloat16 [2, 768, 768], P('section', ('dp', 'seq')), may hold values from -1.5 to 1.5
- mlp_up: bfloat16 [2, 768, 3072], P('section', ('dp', 'seq')), may hold values from -0.21875 to 0.21875
- mlp_down: bfloat16 [2, 3072, 768], P('section', ('dp', 'seq')), may hold values from -0.109375 to 0.109375
- cross_query: bfloat16 [2, 768, 768], P('section', ('dp', 'seq')), may hold values from -0.21875 to 0.21875
- cross_pair: bfloat16 [2, 768, 1536], P('section', ('dp', 'seq')), may hold values from -0.21875 to 0.21875
- cross_output: bfloat16 [2, 768, 768], P('section', ('dp', 'seq')), may hold values from -4 to 4
- patch_cotangent: bfloat16 [8, 96, 12, 768], P('dp', 'seq'), may hold values from -6 to 6
- query_cotangent: bfloat16 [8, 128, 768], P('dp'), may hold values from -6 to 6
Outputs:
- patch_ends: bfloat16 [2, 8, 96, 12, 768], P('section', 'dp', 'seq')
- query_ends: bfloat16 [2, 8, 128, 768], P('section', 'dp')
- grad_norm_attn: float32 [2, 768], P('section', ('dp', 'seq'))
- grad_norm_mlp: float32 [2, 768], P('section', ('dp', 'seq'))
- grad_norm_query: float32 [2, 768], P('section', ('dp', 'seq'))
- grad_attn_input: float32 [2, 768, 2304], P('section', ('dp', 'seq'))
- grad_attn_output: float32 [2, 768, 768], P('section', ('dp', 'seq'))
- grad_mlp_up: float32 [2, 768, 3072], P('section', ('dp', 'seq'))
- grad_mlp_down: float32 [2, 3072, 768], P('section', ('dp', 'seq'))
- grad_cross_query: float32 [2, 768, 768], P('section', ('dp', 'seq'))
- grad_cross_pair: float32 [2, 768, 1536], P('section', ('dp', 'seq'))
- grad_cross_output: float32 [2, 768, 768], P('section', ('dp', 'seq'))
The draws below stay inside these ranges and needn't reach their ends.
Inputs may be any that keep to these rules, and one draw needn't show every extreme that they name: `page_rows`: among the 2 pages of each dp index one holds content in all 8 window rows. `window_mask`: window 0 of window row 0 of every page is 1. `query_lengths`: among the 2 query sets of each dp index one has all 128 tokens live. `plan`: each row is a permutation of the numbers below 2.
All inputs are finite; a program needn't handle non-finite values.
Results may differ from the reference program's by a relative error of at most 0.025.
Values may be sent and summed in bfloat16 or wider, within the bound.
No kernel may reach another device: no remote copies, remote signals or barrier semaphores. Data moves between devices by JAX's collectives and lax.ppermute only.
A program may use at most 320 MiB of HBM per device.

```python
import math
import jax
import jax.numpy as jnp
from jax import lax

D = 768
HEADS = 12
HDIM = 64
FF = 3072
WIN = 12
NQ = 128
MB = 2
LAYERS = 2
WCOLS = 1
WROWS = 8
PH = 96
PW = 12
GROUPS = 4
PAGES = 8
QSETS = 8


def draw_page_rows(key, part):
    key = jax.random.fold_in(key, 11)
    first_key, second_key = jax.random.split(key)
    counts_drawn = jax.random.randint(first_key, (GROUPS, MB), 1, WROWS + 1)
    chosen = jax.random.randint(second_key, (GROUPS, 1), 0, MB)
    full_slot = jnp.arange(MB)[None, :] == chosen
    return jnp.where(full_slot, WROWS, counts_drawn).reshape(PAGES).astype(jnp.int32)


def draw_window_mask(key, part):
    key = jax.random.fold_in(key, 12)
    levels = jax.random.randint(key, (PAGES, WROWS, WCOLS), 0, 4)
    marks_drawn = jnp.minimum(levels, 1)
    corner = (jnp.arange(WROWS)[:, None] == 0) & (jnp.arange(WCOLS)[None, :] == 0)
    return jnp.where(corner[None], 1, marks_drawn).astype(jnp.int32)


def draw_query_lengths(key, part):
    key = jax.random.fold_in(key, 13)
    first_key, second_key = jax.random.split(key)
    lengths = jax.random.randint(first_key, (GROUPS, MB), 1, NQ + 1)
    chosen = jax.random.randint(second_key, (GROUPS, 1), 0, MB)
    full_slot = jnp.arange(MB)[None, :] == chosen
    return jnp.where(full_slot, NQ, lengths).reshape(QSETS).astype(jnp.int32)


def shard_levels(key, dims, pieces, low, largest):
    loudness = 1.0
    for position, shards_of in pieces:
        draws = jax.random.uniform(jax.random.fold_in(jax.random.fold_in(key, 6), position), (shards_of,), jnp.float32, low / len(pieces), largest / len(pieces))
        loudness = loudness * jnp.repeat(jnp.exp(draws), dims[position] // shards_of).reshape((-1,) + (1,) * (len(dims) - 1 - position))
    return loudness


def centred(own_key, shape, width, reach, cuts=(), kind=jnp.bfloat16):
    values = jax.random.normal(own_key, shape, jnp.float32) * width
    if len(cuts) > 0:
        values = shard_levels(own_key, shape, cuts, -0.22, 0.18) * values
    return jnp.clip(values, min=-reach, max=reach).astype(kind)


def setup_inputs(seed: int = 0) -> dict:
    key_list = jax.random.split(jax.random.key(seed), 19)
    return {
        "patches": centred(key_list[0], (PAGES, PH, PW, D), 1.0, 6.0, ((0, 4), (1, 4))),
        "queries": centred(key_list[1], (QSETS, NQ, D), 1.0, 6.0, ((0, 4),)),
        "page_rows": draw_page_rows(jax.random.fold_in(key_list[18], 71), 0),
        "window_mask": draw_window_mask(jax.random.fold_in(key_list[18], 71), 0),
        "query_lengths": draw_query_lengths(jax.random.fold_in(key_list[18], 71), 0),
        "plan": jax.vmap(lambda own: jax.random.permutation(own, MB))(jax.random.split(key_list[5], GROUPS)).reshape((GROUPS, MB)).astype(jnp.int32),
        "norm_attn": jnp.clip(1.0 + 0.18 * jax.random.normal(key_list[6], (LAYERS, D), jnp.float32), 0.099609375, 1.8984375).astype(jnp.bfloat16),
        "norm_mlp": jnp.clip(1.0 + 0.18 * jax.random.normal(key_list[7], (LAYERS, D), jnp.float32), 0.099609375, 1.8984375).astype(jnp.bfloat16),
        "norm_query": jnp.clip(1.0 + 0.18 * jax.random.normal(key_list[8], (LAYERS, D), jnp.float32), 0.099609375, 1.8984375).astype(jnp.bfloat16),
        "attn_input": centred(key_list[9], (LAYERS, D, 3 * D), D ** -0.5, 0.21875, ((0, 2), (1, 16))),
        "attn_output": centred(key_list[10], (LAYERS, D, D), (D // 48) ** -0.5, 1.5, ((0, 2), (1, 16))),
        "mlp_up": centred(key_list[11], (LAYERS, D, FF), D ** -0.5, 0.21875, ((0, 2), (1, 16))),
        "mlp_down": centred(key_list[12], (LAYERS, FF, D), FF ** -0.5, 0.109375, ((0, 2), (1, 16))),
        "cross_query": centred(key_list[13], (LAYERS, D, D), D ** -0.5, 0.21875, ((0, 2), (1, 16))),
        "cross_pair": centred(key_list[14], (LAYERS, D, 2 * D), D ** -0.5, 0.21875, ((0, 2), (1, 16))),
        "cross_output": centred(key_list[15], (LAYERS, D, D), (max(D // 384, 1)) ** -0.5, 4.0, ((0, 2), (1, 16))),
        "patch_cotangent": centred(key_list[16], (PAGES, PH, PW, D), 1.0, 6.0, ((0, 4), (1, 4))),
        "query_cotangent": centred(key_list[17], (QSETS, NQ, D), 1.0, 6.0, ((0, 4),)),
    }


epsilon = 1e-05
hidden_value = -1e+30
highest = lax.Precision.HIGHEST

@jax.custom_vjp
def low(v):
    return lax.optimization_barrier(v.astype(jnp.bfloat16)).astype(jnp.float32)

@jax.custom_vjp
def low_back(v):
    return v

def low_keep(v):
    return (low(v), None)

def low_pass(kept, grad):
    return (grad,)

def back_keep(v):
    return (v, None)

def back_low(kept, grad):
    return (low(grad),)
low.defvjp(low_keep, low_pass)
low_back.defvjp(back_keep, back_low)

def product(left_side, right_side):
    return jnp.dot(left_side, right_side, precision=highest, preferred_element_type=jnp.float32)

def layer_norm(values, gain):
    center = values - lax.optimization_barrier(jnp.mean(values, axis=-1, keepdims=True))
    spread = lax.optimization_barrier(jnp.mean(center * center, axis=-1, keepdims=True))
    return center * lax.rsqrt(spread + epsilon) * gain

def heads_view(values):
    return values.reshape(values.shape[:-1] + (HEADS, HDIM))

def to_windows(grid_view):
    row_count, col_count, features = grid_view.shape
    blocks = grid_view.reshape(row_count // WIN, WIN, col_count // WIN, WIN, features)
    return blocks.transpose(0, 2, 1, 3, 4).reshape(-1, WIN * WIN, features)

def from_windows(blocks, row_count, col_count):
    features = blocks.shape[-1]
    grid_view = blocks.reshape(row_count // WIN, col_count // WIN, WIN, WIN, features)
    return grid_view.transpose(0, 2, 1, 3, 4).reshape(row_count, col_count, features)

def window_attend(packed, present):
    scaling = 1.0 / math.sqrt(HDIM)
    query_heads = heads_view(packed[..., :D])
    key_heads = heads_view(packed[..., D:2 * D])
    value_heads = heads_view(packed[..., 2 * D:])
    scores = low_back(jnp.einsum('nqhe,nkhe->nhqk', query_heads, key_heads, precision=highest) * scaling)
    scores = jnp.where(present[:, None, None, :], scores, hidden_value)
    softmaxed = jax.nn.softmax(scores, axis=-1)
    mixed_out = jnp.einsum('nhqk,nkhe->nqhe', low(softmaxed), value_heads, precision=highest)
    return low(low_back(mixed_out.reshape(packed.shape[0], packed.shape[1], D)))

def layer(weights, patch_in, query_in, key_valid, query_live, shifted):
    gain_attn, gain_mlp, gain_query, w_input, w_output, w_up, w_down, w_query, w_pair, w_cross = weights
    row_count, col_count = (patch_in.shape[0], patch_in.shape[1])
    half_win = WIN // 2
    flat_patch = patch_in.reshape(row_count * col_count, D)
    normed = low(layer_norm(flat_patch, gain_attn))
    packed = low(low_back(product(normed, w_input))).reshape(row_count, col_count, 3 * D)
    present = jnp.ones((row_count, col_count), dtype=bool)
    if shifted:
        packed = jnp.pad(packed, ((half_win, half_win), (half_win, half_win), (0, 0)))
        present = jnp.pad(present, half_win)
    frame_rows, frame_cols = (packed.shape[0], packed.shape[1])
    mixed_out = window_attend(to_windows(packed), to_windows(present[..., None])[..., 0])
    mixed_out = from_windows(mixed_out, frame_rows, frame_cols)
    if shifted:
        mixed_out = mixed_out[half_win:half_win + row_count, half_win:half_win + col_count]
    first_sum = flat_patch + low_back(product(mixed_out.reshape(row_count * col_count, D), w_output))
    normed_mlp = low(layer_norm(first_sum, gain_mlp))
    lifted = low_back(product(normed_mlp, w_up))
    active = low(jax.nn.gelu(lifted, approximate=False))
    second_sum = first_sum + product(active, w_down)
    normed_query = low(layer_norm(query_in, gain_query))
    query_proj = low(low_back(product(normed_query, w_query)))
    pair_proj = low(low_back(product(normed_mlp, w_pair)))
    scaling = 1.0 / math.sqrt(HDIM)
    scores = low_back(jnp.einsum('qhe,khe->hqk', heads_view(query_proj), heads_view(pair_proj[:, :D]), precision=highest) * scaling)
    scores = jnp.where(key_valid[None, None, :], scores, hidden_value)
    softmaxed = jax.nn.softmax(scores, axis=-1)
    attended = jnp.einsum('hqk,khe->qhe', low(softmaxed), heads_view(pair_proj[:, D:]), precision=highest)
    attended = low(low_back(attended.reshape(-1, D)))
    query_out = query_in + query_live[:, None] * product(attended, w_cross)
    return (second_sum.reshape(row_count, col_count, D), query_out)

def reference(patches, queries, page_rows, window_mask, query_lengths, plan, norm_attn, norm_mlp, norm_query, attn_input, attn_output, mlp_up, mlp_down, cross_query, cross_pair, cross_output, patch_cotangent, query_cotangent):
    stacked = [weight.astype(jnp.float32) for weight in (norm_attn, norm_mlp, norm_query, attn_input, attn_output, mlp_up, mlp_down, cross_query, cross_pair, cross_output)]
    layer_one = tuple((weight[0] for weight in stacked))
    layer_two = tuple((weight[1] for weight in stacked))
    batch_total = GROUPS * MB
    page_index = (jnp.arange(GROUPS, dtype=jnp.int32)[:, None] * MB + plan).reshape(-1).astype(jnp.int32)
    row_marks = jnp.arange(WROWS, dtype=jnp.int32)[None, :] < page_rows[:, None]
    window_valid = row_marks[:, :, None] & (window_mask == 1)
    cell_valid = jnp.repeat(jnp.repeat(window_valid, WIN, axis=1), WIN, axis=2).reshape(PAGES, PH * PW)
    live_all = (jnp.arange(NQ, dtype=jnp.int32)[None, :] < query_lengths[:, None]).astype(jnp.float32)

    def one_batch(totals, batch_id):
        page_id = page_index[batch_id]
        patch_in = patches[page_id].astype(jnp.float32)
        query_in = queries[batch_id].astype(jnp.float32)
        key_valid = cell_valid[page_id]
        query_live = live_all[batch_id]

        def two_layers(patch_val, query_val, first_weights, second_weights):
            middle_patch, middle_query = layer(first_weights, patch_val, query_val, key_valid, query_live, False)
            middle_patch = low(low_back(middle_patch))
            middle_query = low(low_back(middle_query))
            return layer(second_weights, middle_patch, middle_query, key_valid, query_live, True)
        outputs, pullback = jax.vjp(two_layers, patch_in, query_in, layer_one, layer_two)
        grad_patch, grad_query, grad_one, grad_two = pullback((patch_cotangent[page_id].astype(jnp.float32), query_cotangent[batch_id].astype(jnp.float32)))
        totals = jax.tree.map(lambda total_val, part_val: total_val + part_val, totals, (grad_one, grad_two))
        return (totals, (outputs[0].astype(jnp.bfloat16), outputs[1].astype(jnp.bfloat16), grad_patch.astype(jnp.bfloat16), grad_query.astype(jnp.bfloat16)))
    zero_grads = jax.tree.map(jnp.zeros_like, (layer_one, layer_two))
    totals, (out_patches, out_queries, grad_patches, grad_queries) = lax.scan(one_batch, zero_grads, jnp.arange(batch_total, dtype=jnp.int32))
    out_pages = jnp.zeros((PAGES, PH, PW, D), jnp.bfloat16).at[page_index].set(out_patches)
    grad_pages = jnp.zeros((PAGES, PH, PW, D), jnp.bfloat16).at[page_index].set(grad_patches)
    patch_ends = jnp.stack([grad_pages, out_pages])
    query_ends = jnp.stack([grad_queries, out_queries])
    grads = tuple((jnp.stack([totals[0][slot], totals[1][slot]]) for slot in range(10)))
    return (patch_ends, query_ends, grads[0], grads[1], grads[2], grads[3], grads[4], grads[5], grads[6], grads[7], grads[8], grads[9])
```

```python
from functools import partial
import math

import jax
import jax.numpy as jnp
from jax import lax
from jax.experimental import pallas as pl
from jax.experimental.pallas import tpu as pltpu
from jax.sharding import PartitionSpec as P

D = 768
HEADS = 12
HDIM = 64
WIN = 12
NQ = 128
CELLS = WIN * WIN
HALF = D // 2
HH = HEADS // 2
PAIRS = HH // 2
RIM = WIN // 2 * WIN

epsilon = 1e-05
hidden_value = -1e30
scaling = 1.0 / math.sqrt(HDIM)
bf16 = jnp.bfloat16
f32 = jnp.float32
SWAP = [(0, 1), (1, 0)]
ANY = pl.BlockSpec(memory_space=pl.ANY)
SMEM = pl.BlockSpec(memory_space=pltpu.SMEM)


def whole(shape):
    return pl.BlockSpec(shape, lambda *_: (0,) * len(shape))


def per_batch(shape):
    return pl.BlockSpec((1,) + tuple(shape[1:]), lambda m: (m,) + (0,) * (len(shape) - 1))


def run(kernel, name, grid, ins, outs, scratch, flops):
    arrays = [a for a, _ in ins]
    nbytes = sum(a.size * a.dtype.itemsize for a in arrays)
    return pl.pallas_call(
        kernel,
        grid=grid,
        in_specs=[s for _, s in ins],
        out_specs=[s for _, _, s in outs],
        out_shape=[jax.ShapeDtypeStruct(sh, dt) for sh, dt, _ in outs],
        scratch_shapes=scratch,
        compiler_params=pltpu.CompilerParams(vmem_limit_bytes=52 * 1024 * 1024),
        cost_estimate=pl.CostEstimate(flops=int(flops), bytes_accessed=int(nbytes), transcendentals=0),
        name=name,
    )(*arrays)


def start_fetch(dst, pieces, order, rows, row0, col0, sem):
    cols = dst.shape[1]
    for p, piece in enumerate(pieces):
        slots = piece.shape[0]
        for s in range(slots):
            at = pl.multiple_of(order[p * slots + s] * rows, 16)
            pltpu.make_async_copy(
                piece.at[s, pl.ds(row0, rows), pl.ds(col0, cols)], dst.at[pl.ds(at, rows), :], sem
            ).start()


def end_fetch(dst, sem):
    pltpu.make_async_copy(dst, dst, sem).wait()


def spread_rows(values, outs, order, rows, row0, col0):
    cols = values.shape[1]
    for p, out in enumerate(outs):
        slots = out.shape[0]
        for s in range(slots):
            at = pl.multiple_of(order[p * slots + s] * rows, 8)
            out[s, row0 : row0 + rows, col0 : col0 + cols] = values[pl.ds(at, rows), :].astype(bf16)


def nn(a, b):
    return jnp.dot(a, b, preferred_element_type=f32)


def nt(a, b):
    return lax.dot_general(a, b, (((1,), (1,)), ((), ())), preferred_element_type=f32)


def tn(a, b):
    return lax.dot_general(a, b, (((0,), (0,)), ((), ())), preferred_element_type=f32)


def norm_parts(values):
    center = values - jnp.mean(values, axis=-1, keepdims=True)
    inv = lax.rsqrt(jnp.mean(center * center, axis=-1, keepdims=True) + epsilon)
    return center * inv, inv


def norm_back(unit, inv, gain, grad):
    scaled = grad * gain
    return inv * (
        scaled
        - jnp.mean(scaled, axis=-1, keepdims=True)
        - unit * jnp.mean(scaled * unit, axis=-1, keepdims=True)
    )


def lane_halves(rows):
    lane = lax.broadcasted_iota(jnp.int32, (rows, 128), 1)
    return lane < HDIM


def half_masks():
    lane = lax.broadcasted_iota(jnp.int32, (1, 128), 1)
    low = (lane < HDIM).astype(f32)
    return low.astype(bf16), (1.0 - low).astype(bf16)


def attn_forward(n, shifted, *refs):
    order_c, order_r, x_ref = refs[:3]
    refs = refs[3:]
    if shifted:
        mask_ref, refs = refs[0], refs[1:]
    u0, u1, refs = refs[:n], refs[n : 2 * n], refs[2 * n :]
    h_ref, qkv_ref, p_ref, o_ref, part_ref, gain_ref, w_in, w_out, mixed, hidden, sem0, sem1 = refs
    tokens = x_ref.shape[1]
    own = o_ref.shape[1]
    lo = (tokens - own) // 2

    @pl.when(pl.program_id(0) == 0)
    def _():
        start_fetch(w_in, u0, order_c, w_in.shape[0] // (n * u0[0].shape[0]), 0, 0, sem0)
        start_fetch(w_out, u1, order_r, w_out.shape[0] // (n * u1[0].shape[0]), 0, 0, sem1)
        end_fetch(w_in, sem0)
        end_fetch(w_out, sem1)
        gain_ref[...] = w_in[:, :128].astype(f32).T[0:8]

    unit, _ = norm_parts(x_ref[0].astype(f32))
    hidden[...] = unit * gain_ref[0:1]
    h_ref[0] = hidden[lo : lo + own].astype(bf16)
    qkv_ref[0] = nn(hidden[...].astype(bf16), w_in[:, 128:]).astype(bf16)
    first_half = lane_halves(CELLS)
    masks = half_masks()
    for block in range(tokens // CELLS):
        rows = slice(block * CELLS, (block + 1) * CELLS)
        for pair in range(PAIRS):
            q2 = qkv_ref[0, rows, pair * 128 : pair * 128 + 128]
            k2 = qkv_ref[0, rows, HALF + pair * 128 : HALF + pair * 128 + 128]
            v2 = qkv_ref[0, rows, 2 * HALF + pair * 128 : 2 * HALF + pair * 128 + 128]
            mixed_two = []
            for side in range(2):
                scores = nt(q2 * masks[side], k2) * scaling
                if shifted:
                    scores = scores + mask_ref[block]
                weights = jnp.exp(scores - jnp.max(scores, axis=-1, keepdims=True))
                probs = (weights / jnp.sum(weights, axis=-1, keepdims=True)).astype(bf16)
                p_ref[0, block * HH + pair * 2 + side] = probs
                mixed_two.append(nn(probs, v2))
            mixed[rows, pair * 128 : pair * 128 + 128] = jnp.where(
                first_half, mixed_two[0], mixed_two[1]
            )
    out = mixed[lo : lo + own].astype(bf16)
    o_ref[0] = out
    part_ref[0] = nn(out, w_out[...]).astype(bf16)


def mlp_forward(n, *refs):
    order_c, order_r, x_ref, pa_ref, pb_ref, gain_ref, cq_ref, valid_ref = refs[:8]
    refs = refs[8:]
    u2, u3, refs = refs[:n], refs[n : 2 * n], refs[2 * n :]
    first_ref, h_ref, slope_ref, act_ref, part_ref, ckv_ref, e_ref, o_ref, stat_ref = refs[:9]
    w_up, w_down, sem0, sem1 = refs[9:]
    hid = slope_ref.shape[2]
    tokens = x_ref.shape[1]

    @pl.when(pl.program_id(0) == 0)
    def _():
        start_fetch(w_up, u2, order_c, w_up.shape[0] // (n * u2[0].shape[0]), 0, 0, sem0)
        start_fetch(w_down, u3, order_r, w_down.shape[0] // (n * u3[0].shape[0]), 0, 0, sem1)
        end_fetch(w_up, sem0)
        end_fetch(w_down, sem1)

    first = x_ref[0].astype(f32) + (pa_ref[0].astype(f32) + pb_ref[0].astype(f32))
    first_ref[0] = first
    unit, _ = norm_parts(first)
    hidden = (unit * gain_ref[1:2]).astype(bf16)
    h_ref[0] = hidden
    ckv_ref[0] = nn(hidden, w_up[:, hid:]).astype(bf16)
    step = 512
    for at in range(0, hid, step):
        lifted = nn(hidden, w_up[:, at : at + step])
        cdf = 0.5 + 0.5 * lax.erf(lifted * math.sqrt(0.5))
        act_ref[0, :, at : at + step] = (lifted * cdf).astype(bf16)
        pdf = jnp.exp(lifted * lifted * -0.5) * (1.0 / math.sqrt(2.0 * math.pi))
        slope_ref[0, :, at : at + step] = (cdf + lifted * pdf).astype(bf16)
    part_ref[0] = nn(act_ref[0], w_down[...]).astype(bf16)

    valid = jnp.broadcast_to(valid_ref[0], (NQ, tokens)) > 0.5
    first_half = lane_halves(NQ)
    masks = half_masks()
    lane = lax.broadcasted_iota(jnp.int32, (NQ, 128), 1)
    stats = jnp.zeros((NQ, 128), f32)
    for pair in range(PAIRS):
        q2 = cq_ref[0, :, pair * 128 : pair * 128 + 128]
        k2 = ckv_ref[0, :, pair * 128 : pair * 128 + 128]
        v2 = ckv_ref[0, :, HALF + pair * 128 : HALF + pair * 128 + 128]
        mixed_two = []
        for side in range(2):
            head = pair * 2 + side
            scores = jnp.where(valid, nt(q2 * masks[side], k2) * scaling, hidden_value)
            peak = jnp.max(scores, axis=-1, keepdims=True)
            weights = jnp.where(valid, jnp.exp(scores - peak), 0.0)
            total = jnp.sum(weights, axis=-1, keepdims=True)
            stats = jnp.where(lane == head, peak, stats)
            stats = jnp.where(lane == 8 + head, total, stats)
            low = weights.astype(bf16)
            e_ref[0, head] = low
            mixed_two.append(nn(low, v2))
        o_ref[0, :, pair * 128 : pair * 128 + 128] = jnp.where(
            first_half, mixed_two[0], mixed_two[1]
        ).astype(bf16)
    stat_ref[0] = stats.T[0:16]


def query_in(n, has_parts, *refs):
    order_c, q_ref, gain_ref = refs[:3]
    refs = refs[3:]
    if has_parts:
        pa_ref, pb_ref, live_ref, refs = refs[0], refs[1], refs[2], refs[3:]
    u2, refs = refs[:n], refs[n:]
    if has_parts:
        new_ref, refs = refs[0], refs[1:]
    h_ref, cq_ref, w_q, sem = refs
    start_fetch(
        w_q, u2, order_c, w_q.shape[0] // (n * u2[0].shape[0]), 0, u2[0].shape[2] - HALF, sem
    )
    end_fetch(w_q, sem)
    for m in range(q_ref.shape[0]):
        query = q_ref[m].astype(f32)
        if has_parts:
            query = query + live_ref[m] * (pa_ref[m].astype(f32) + pb_ref[m].astype(f32))
            low = query.astype(bf16)
            new_ref[m] = low
            query = low.astype(f32)
        unit, _ = norm_parts(query)
        hidden = (unit * gain_ref[2:3]).astype(bf16)
        h_ref[m] = hidden
        cq_ref[m] = nn(hidden, w_q[...]).astype(bf16)


def query_out(n, ns, *refs):
    order_r, order_s = refs[:2]
    refs = refs[2:]
    os, ss, refs = refs[:ns], refs[ns : 2 * ns], refs[2 * ns :]
    u3, refs = refs[:n], refs[n:]
    att_ref, low_ref, coef_ref, part_ref, w_co, o_all, s_all, sem = refs
    rows = w_co.shape[0] // (n * u3[0].shape[0])
    start_fetch(w_co, u3, order_r, rows, u3[0].shape[1] - rows, 0, sem)
    for p in range(ns):
        o_all[order_s[p]] = os[p][...]
        s_all[order_s[p]] = ss[p][...]
    first_half = lane_halves(NQ)
    end_fetch(w_co, sem)
    for m in range(att_ref.shape[0]):
        peak = s_all[0, m, 0:8]
        for s in range(1, ns):
            peak = jnp.maximum(peak, s_all[s, m, 0:8])
        scales = [jnp.exp(s_all[s, m, 0:8] - peak) for s in range(ns)]
        total = scales[0] * s_all[0, m, 8:16]
        for s in range(1, ns):
            total = total + scales[s] * s_all[s, m, 8:16]
        inverse = 1.0 / jnp.where(total > 0.0, total, 1.0)
        blocks = [scale * inverse for scale in scales]
        if ns * 8 < 128:
            blocks.append(jnp.zeros((128 - ns * 8, 128), f32))
        columns = jnp.concatenate(blocks, axis=0).T
        mine = jnp.exp(ss[0][m, 0:8] - peak) * inverse
        coef_ref[m] = jnp.concatenate([mine, jnp.zeros((120, 128), f32)], axis=0).T
        for pair in range(PAIRS):
            mixed = jnp.zeros((NQ, 128), f32)
            for s in range(ns):
                at = s * 8 + pair * 2
                factor = jnp.where(first_half, columns[:, at : at + 1], columns[:, at + 1 : at + 2])
                mixed = mixed + factor * o_all[s, m, :, pair * 128 : pair * 128 + 128].astype(f32)
            att_ref[m, :, pair * 128 : pair * 128 + 128] = mixed
        low = att_ref[m].astype(bf16)
        low_ref[m] = low
        part_ref[m] = nn(low, w_co[...]).astype(bf16)


def mlp_backward(n, *refs):
    order_c, order_r, ds_ref, slope_ref, e_ref, coef_ref, dq_ref, live_ref, att_ref, cq_ref, ckv_ref = refs[:11]
    refs = refs[11:]
    u2, u3, refs = refs[:n], refs[n : 2 * n], refs[2 * n :]
    du_ref, dckv_ref, dcq_ref, part_ref, dc_ref, w_up, w_down, w_co, sem0, sem1, sem2 = refs
    hid = slope_ref.shape[2]
    tokens = ds_ref.shape[1]

    @pl.when(pl.program_id(0) == 0)
    def _():
        down_rows = w_down.shape[0] // (n * u3[0].shape[0])
        start_fetch(w_down, u3, order_r, down_rows, 0, 0, sem1)
        start_fetch(w_co, u3, order_r, w_co.shape[0] // (n * u3[0].shape[0]), down_rows, 0, sem2)
        start_fetch(w_up, u2, order_c, w_up.shape[0] // (n * u2[0].shape[0]), 0, 0, sem0)
        end_fetch(w_down, sem1)
        end_fetch(w_co, sem2)
        end_fetch(w_up, sem0)

    grad_second = ds_ref[0]
    step = 512
    for at in range(0, hid, step):
        grad_act = nt(grad_second, w_down[at : at + step, :])
        du_ref[0, :, at : at + step] = (
            grad_act * slope_ref[0, :, at : at + step].astype(f32)
        ).astype(bf16)

    grad_cross = (live_ref[0] * dq_ref[0].astype(f32)).astype(bf16)
    dc_ref[0] = grad_cross
    grad_att = nt(grad_cross, w_co[...]).astype(bf16)
    first_q = lane_halves(NQ)
    first_k = lane_halves(tokens)
    masks = half_masks()
    for pair in range(PAIRS):
        lanes = slice(pair * 128, pair * 128 + 128)
        upper = slice(HALF + pair * 128, HALF + pair * 128 + 128)
        a2 = grad_att[:, lanes]
        q2 = cq_ref[0, :, lanes]
        k2 = ckv_ref[0, :, lanes]
        v2 = ckv_ref[0, :, upper]
        inner = a2.astype(f32) * att_ref[0, :, lanes]
        dq_two, dk_two, dv_two = [], [], []
        for side in range(2):
            head = pair * 2 + side
            keep = first_q if side == 0 else jnp.logical_not(first_q)
            delta = jnp.sum(jnp.where(keep, inner, 0.0), axis=-1, keepdims=True)
            probs = e_ref[0, head].astype(f32) * coef_ref[0, :, head : head + 1]
            grad_probs = nt(a2 * masks[side], v2)
            grad_scores = (probs * (grad_probs - delta)).astype(bf16)
            dq_two.append(nn(grad_scores, k2))
            dk_two.append(tn(grad_scores, q2))
            dv_two.append(tn(probs.astype(bf16), a2))
        dcq_ref[0, :, lanes] = (jnp.where(first_q, dq_two[0], dq_two[1]) * scaling).astype(bf16)
        dckv_ref[0, :, lanes] = (jnp.where(first_k, dk_two[0], dk_two[1]) * scaling).astype(bf16)
        dckv_ref[0, :, upper] = jnp.where(first_k, dv_two[0], dv_two[1]).astype(bf16)
    part_ref[0] = (
        nt(du_ref[0], w_up[:, :hid]) + nt(dckv_ref[0], w_up[:, hid:])
    ).astype(bf16)


def first_backward(n, *refs):
    order_r, ds_ref, da_ref, db_ref, first_ref, gain_ref = refs[:6]
    u1, refs = refs[6 : 6 + n], refs[6 + n :]
    df_ref, low_ref, do_ref, dg_ref, w_out, sem = refs

    @pl.when(pl.program_id(0) == 0)
    def _():
        start_fetch(w_out, u1, order_r, w_out.shape[0] // (n * u1[0].shape[0]), 0, 0, sem)
        dg_ref[...] = jnp.zeros_like(dg_ref)
        end_fetch(w_out, sem)

    grad = da_ref[0].astype(f32) + db_ref[0].astype(f32)
    unit, inv = norm_parts(first_ref[0])
    dg_ref[0:1] += jnp.sum(grad * unit, axis=0, keepdims=True)
    grad_first = ds_ref[0].astype(f32) + norm_back(unit, inv, gain_ref[1:2], grad)
    df_ref[0] = grad_first
    low = grad_first.astype(bf16)
    low_ref[0] = low
    do_ref[0] = nt(low, w_out[...]).astype(bf16)


def attn_backward(n, *refs):
    order_c, do_ref, qkv_ref, p_ref = refs[:4]
    u0, refs = refs[4 : 4 + n], refs[4 + n :]
    dqkv_ref, part_ref, w_in, wide, sem = refs
    tokens = do_ref.shape[1]
    own = dqkv_ref.shape[1]
    lo = (tokens - own) // 2

    @pl.when(pl.program_id(0) == 0)
    def _():
        start_fetch(w_in, u0, order_c, w_in.shape[0] // (n * u0[0].shape[0]), 0, 128, sem)
        end_fetch(w_in, sem)

    first_half = lane_halves(CELLS)
    masks = half_masks()
    for block in range(tokens // CELLS):
        rows = slice(block * CELLS, (block + 1) * CELLS)
        for pair in range(PAIRS):
            lanes = slice(pair * 128, pair * 128 + 128)
            q2 = qkv_ref[0, rows, lanes]
            k2 = qkv_ref[0, rows, HALF + pair * 128 : HALF + pair * 128 + 128]
            v2 = qkv_ref[0, rows, 2 * HALF + pair * 128 : 2 * HALF + pair * 128 + 128]
            g2 = do_ref[0, rows, lanes]
            dq_two, dk_two, dv_two = [], [], []
            for side in range(2):
                probs = p_ref[0, block * HH + pair * 2 + side]
                wide_probs = probs.astype(f32)
                grad_probs = nt(g2 * masks[side], v2)
                delta = jnp.sum(wide_probs * grad_probs, axis=-1, keepdims=True)
                grad_scores = (wide_probs * (grad_probs - delta)).astype(bf16)
                dq_two.append(nn(grad_scores, k2))
                dk_two.append(tn(grad_scores, q2))
                dv_two.append(tn(probs, g2))
            wide[rows, lanes] = jnp.where(first_half, dq_two[0], dq_two[1]) * scaling
            wide[rows, HALF + pair * 128 : HALF + pair * 128 + 128] = (
                jnp.where(first_half, dk_two[0], dk_two[1]) * scaling
            )
            wide[rows, 2 * HALF + pair * 128 : 2 * HALF + pair * 128 + 128] = jnp.where(
                first_half, dv_two[0], dv_two[1]
            )
    low = wide[lo : lo + own].astype(bf16)
    dqkv_ref[0] = low
    part_ref[0] = nt(low, w_in[...]).astype(bf16)


def input_backward(x_ref, df_ref, da_ref, db_ref, gain_ref, dx_ref, dg_ref):
    @pl.when(pl.program_id(0) == 0)
    def _():
        dg_ref[...] = jnp.zeros_like(dg_ref)

    grad = da_ref[0].astype(f32) + db_ref[0].astype(f32)
    unit, inv = norm_parts(x_ref[0].astype(f32))
    dg_ref[0:1] += jnp.sum(grad * unit, axis=0, keepdims=True)
    dx_ref[0] = (df_ref[0] + norm_back(unit, inv, gain_ref[0:1], grad)).astype(bf16)


def query_back_one(n, ns, *refs):
    order_c, order_s = refs[:2]
    parts, refs = refs[2 : 2 + ns], refs[2 + ns :]
    u2, refs = refs[:n], refs[n:]
    dcq_ref, part_ref, w_q, all_parts, sem = refs
    start_fetch(
        w_q, u2, order_c, w_q.shape[0] // (n * u2[0].shape[0]), 0, u2[0].shape[2] - HALF, sem
    )
    for p in range(ns):
        all_parts[order_s[p]] = parts[p][...]
    end_fetch(w_q, sem)
    for m in range(dcq_ref.shape[0]):
        total = all_parts[0, m].astype(f32)
        for s in range(1, ns):
            total = total + all_parts[s, m].astype(f32)
        low = total.astype(bf16)
        dcq_ref[m] = low
        part_ref[m] = nt(low, w_q[...]).astype(bf16)


def query_back_two(q_ref, dq_ref, da_ref, db_ref, gain_ref, out_ref, dg_ref):
    total = jnp.zeros((1, D), f32)
    for m in range(q_ref.shape[0]):
        grad = da_ref[m].astype(f32) + db_ref[m].astype(f32)
        unit, inv = norm_parts(q_ref[m].astype(f32))
        total = total + jnp.sum(grad * unit, axis=0, keepdims=True)
        out_ref[m] = (dq_ref[m].astype(f32) + norm_back(unit, inv, gain_ref[2:3], grad)).astype(bf16)
    dg_ref[...] = jnp.broadcast_to(total, dg_ref.shape)


def weight_grads(n, plan, order_by, *refs):
    order_c, order_r = refs[:2]
    count = 1 + max(max(item[0], item[1]) for item in plan)
    sides, refs = refs[2 : 2 + count], refs[2 + count :]
    units = len(order_by)
    outs, acc = [refs[u * n : (u + 1) * n] for u in range(units)], refs[units * n]
    for left, right, unit, rows, row0, col0 in plan:
        order = order_c if order_by[unit] == "c" else order_r
        height, width = sides[left].shape[1], sides[right].shape[1]
        step = 384
        for at in range(0, width, step):
            acc[0:height] = tn(sides[left][...], sides[right][:, at : at + step])
            spread_rows(acc, outs[unit], order, rows, row0, col0 + at)


def per_device(
    patches,
    queries,
    page_rows,
    window_mask,
    query_lengths,
    plan,
    norm_attn,
    norm_mlp,
    norm_query,
    attn_input,
    attn_output,
    mlp_up,
    mlp_down,
    cross_query,
    cross_pair,
    cross_output,
    patch_cotangent,
    query_cotangent,
):
    core = lax.axis_index("section")
    zi = lax.axis_index("dp")
    qi = lax.axis_index("seq")
    nz, ns = lax.axis_size("dp"), lax.axis_size("seq")
    rows = attn_input.shape[1]
    hid = mlp_up.shape[2] // 2
    manual = rows % 16 == 0 and ns == 4 and nz & (nz - 1) == 0
    near = nz // 2
    batches, row_count, col_count = patches.shape[:3]
    tokens = row_count * col_count
    core_zero = core == 0

    def swap(x):
        return lax.ppermute(x, "section", SWAP)

    def across(x, r):
        return lax.ppermute(x, "seq", [(j, j ^ r) for j in range(ns)])

    if manual:
        n = ns
        far = (zi // near) ^ core
        order_c = jnp.stack([((zi ^ r) * ns + (qi ^ p)) for p in range(ns) for r in range(nz)])
        order_r = jnp.stack(
            [
                (((zi ^ (far * near + k)) - core * near) * ns + (qi ^ p))
                for p in range(ns)
                for k in range(near)
            ]
        )
    else:
        n = 1
        order_c = jnp.zeros((1,), jnp.int32)
        order_r = jnp.zeros((1,), jnp.int32)
    order_s = jnp.stack([qi ^ p for p in range(ns)])
    order_c, order_r, order_s = (o.astype(jnp.int32) for o in (order_c, order_r, order_s))

    gain_block = jnp.stack([norm_attn[0], norm_mlp[0], norm_query[0]], axis=1)
    gain_block = jnp.pad(gain_block, ((0, 0), (0, 125)))

    def columns(arrays, half):
        return [a[:, half * w : (half + 1) * w] for a, w in arrays]

    win, up, cq, cp = attn_input[0], mlp_up[0], cross_query[0], cross_pair[0]
    col_parts = [
        [(win[:, :D], HALF), (win[:, D : 2 * D], HALF), (win[:, 2 * D :], HALF)],
        [(up, hid), (cp[:, :D], HALF), (cp[:, D:], HALF), (cq, HALF)],
    ]
    row_units = [attn_output[0], jnp.concatenate([mlp_down[0], cross_output[0]], axis=0)]
    halves = []
    for index, parts in enumerate(col_parts):
        lead = [gain_block] if index == 0 else []
        halves.append([jnp.concatenate(lead + columns(parts, h), axis=1) for h in range(2)])

    def spread_xy(own, by_y):
        one = across(own, 1)
        two = across(own, 2)
        three = across(one, 2) if by_y else across(two, 1)
        return [own, one, two, three]

    def gather_col(mine, theirs, layer, by_y):
        unit = jnp.where(core == layer, mine, theirs)
        stack = jnp.stack(
            [unit]
            + [lax.ppermute(unit, "dp", [(j, j ^ r) for j in range(nz)]) for r in range(1, nz)]
        )
        return spread_xy(stack, by_y)

    def gather_row(mine, theirs, layer, by_y):
        unit = jnp.where(core == layer, mine, theirs)
        got = [unit]
        for r in range(1, nz):
            pairs = [
                (c * nz + j, c * nz + (j ^ r))
                for c in range(2)
                for j in range(c * near, (c + 1) * near)
            ]
            got.append(lax.ppermute(unit, ("section", "dp"), pairs))
        stack = jnp.where(far == 0, jnp.stack(got[:near]), jnp.stack(got[near:]))
        return spread_xy(stack, by_y)

    units = [[None] * 4 for _ in range(2)]
    if manual:
        col_mine = [jnp.where(core_zero, h[0], h[1]) for h in halves]
        col_send = [jnp.where(core_zero, h[1], h[0]) for h in halves]
        col_recv = [swap(s) for s in col_send]
        row_recv = [swap(s) for s in row_units]
        for layer in range(2):
            units[layer][0] = gather_col(col_mine[0], col_recv[0], layer, True)
            units[layer][1] = gather_row(row_units[0], row_recv[0], layer, False)
            units[layer][2] = gather_col(col_mine[1], col_recv[1], layer, False)
            units[layer][3] = gather_row(row_units[1], row_recv[1], layer, True)
    else:

        def gather_all(x):
            return lax.all_gather(
                lax.all_gather(x, ("dp", "seq"), axis=0, tiled=True), "section", axis=0
            )

        whole_cols = [[gather_all(half) for half in h] for h in halves]
        whole_rows = [gather_all(x) for x in (attn_output[0], mlp_down[0], cross_output[0])]
        for layer in range(2):
            for index in range(2):
                units[layer][2 * index] = [
                    jnp.where(core_zero, whole_cols[index][0][layer], whole_cols[index][1][layer])[None]
                ]
            mine = [
                lax.dynamic_slice_in_dim(w[layer], core * (w.shape[1] // 2), w.shape[1] // 2, 0)
                for w in whole_rows
            ]
            units[layer][1] = [mine[0][None]]
            units[layer][3] = [jnp.concatenate(mine[1:], axis=0)[None]]

    order = jnp.arange(batches)
    inverse = jnp.sum(jnp.where(plan[0][None, :] == order[:, None], order[None, :], 0), axis=1)
    query_start = jnp.take(queries, inverse, axis=0)
    query_given = jnp.take(query_cotangent, inverse, axis=0)
    lengths = jnp.take(query_lengths, inverse)
    live = (jnp.arange(NQ)[None, :] < lengths[:, None]).astype(f32)[:, :, None]
    window_rows = qi * (row_count // WIN) + jnp.arange(row_count // WIN)
    marks = (window_rows[None, :, None] < page_rows[:, None, None]) & (window_mask == 1)
    valid = jnp.repeat(jnp.repeat(marks, WIN, axis=1), WIN, axis=2)
    valid = valid.reshape(batches, 1, tokens).astype(f32)
    blocks_wide = (row_count + WIN) // WIN
    cell = jnp.arange(CELLS)
    frame_row = qi * row_count - WIN // 2 + jnp.arange(blocks_wide)[:, None] * WIN + cell // WIN
    inside = (frame_row >= 0) & (frame_row < row_count * ns)
    side_of = (cell % WIN) < WIN // 2
    same = side_of[:, None] == side_of[None, :]
    mask = jnp.where(inside[:, None, :] & same[None], 0.0, hidden_value).astype(f32)

    pages = patches.reshape(batches, tokens, D)
    given = patch_cotangent.reshape(batches, tokens, D)

    def widened(edge_source):
        top = lax.ppermute(
            edge_source[:, tokens - RIM :], "seq", [(j, j + 1) for j in range(ns - 1)]
        )
        bottom = lax.ppermute(edge_source[:, :RIM], "seq", [(j + 1, j) for j in range(ns - 1)])
        return jnp.concatenate([top, edge_source, bottom], axis=1)

    def pieces(unit):
        return [(piece, ANY) for piece in unit]

    def shaped(shape, dtype, batched=True):
        return (shape, dtype, per_batch(shape) if batched else whole(shape))

    def batched(a):
        return (a, per_batch(a.shape))

    def full(a):
        return (a, whole(a.shape))

    dma = pltpu.SemaphoreType.DMA

    def forward(layer, x, query, query_parts):
        u = units[layer]
        shifted = layer == 1
        wide_x = widened(x) if shifted else x
        wide = wide_x.shape[1]
        blocks = wide // CELLS
        ins = [(order_c, SMEM), (order_r, SMEM), batched(wide_x)]
        if shifted:
            ins.append(full(mask))
        h1, qkv, probs, mixed, part, gains = run(
            partial(attn_forward, n, shifted),
            "attn_forward",
            (batches,),
            ins + pieces(u[0]) + pieces(u[1]),
            [
                shaped((batches, tokens, D), bf16),
                shaped((batches, wide, 3 * HALF), bf16),
                shaped((batches, blocks * HH, CELLS, CELLS), bf16),
                shaped((batches, tokens, HALF), bf16),
                shaped((batches, tokens, D), bf16),
                shaped((8, D), f32, False),
            ],
            [
                pltpu.VMEM((D, 128 + 3 * HALF), bf16),
                pltpu.VMEM((HALF, D), bf16),
                pltpu.VMEM((wide, HALF), f32),
                pltpu.VMEM((wide, D), f32),
                dma,
                dma,
            ],
            2e9,
        )
        other = swap(part)
        q_ins = [(order_c, SMEM), full(query), full(gains)]
        q_outs = [
            shaped((batches, NQ, D), bf16, False),
            shaped((batches, NQ, HALF), bf16, False),
        ]
        if query_parts is not None:
            q_ins += [full(query_parts[0]), full(query_parts[1]), full(live)]
            q_outs = [shaped((batches, NQ, D), bf16, False)] + q_outs
        got = run(
            partial(query_in, n, query_parts is not None),
            "query_in",
            (),
            q_ins + pieces(u[2]),
            q_outs,
            [pltpu.VMEM((D, HALF), bf16), dma],
            2e8,
        )
        if query_parts is not None:
            query, got = got[0], got[1:]
        hq, cq_now = got
        first, h2, slope, act, second_part, ckv, e, o, stat = run(
            partial(mlp_forward, n),
            "mlp_forward",
            (batches,),
            [
                (order_c, SMEM),
                (order_r, SMEM),
                batched(x),
                batched(part),
                batched(other),
                full(gains),
                batched(cq_now),
                batched(valid),
            ]
            + pieces(u[2])
            + pieces(u[3]),
            [
                shaped((batches, tokens, D), f32),
                shaped((batches, tokens, D), bf16),
                shaped((batches, tokens, hid), bf16),
                shaped((batches, tokens, hid), bf16),
                shaped((batches, tokens, D), bf16),
                shaped((batches, tokens, D), bf16),
                shaped((batches, HH, NQ, tokens), bf16),
                shaped((batches, NQ, HALF), bf16),
                shaped((batches, 16, NQ), f32),
            ],
            [pltpu.VMEM((D, hid + D), bf16), pltpu.VMEM((hid, D), bf16), dma, dma],
            4e9,
        )
        second_other = swap(second_part)
        os = [o] + [across(o, r) for r in range(1, ns)]
        stats = [stat] + [across(stat, r) for r in range(1, ns)]
        att, att_low, coef, q_part = run(
            partial(query_out, n, ns),
            "query_out",
            (),
            [(order_r, SMEM), (order_s, SMEM)]
            + [full(a) for a in os]
            + [full(a) for a in stats]
            + pieces(u[3]),
            [
                shaped((batches, NQ, HALF), f32, False),
                shaped((batches, NQ, HALF), bf16, False),
                shaped((batches, NQ, 128), f32, False),
                shaped((batches, NQ, D), bf16, False),
            ],
            [
                pltpu.VMEM((HALF, D), bf16),
                pltpu.VMEM((ns, batches, NQ, HALF), bf16),
                pltpu.VMEM((ns, batches, 16, NQ), f32),
                dma,
            ],
            2e8,
        )
        q_other = swap(q_part)
        x_next = (first + (second_part.astype(f32) + second_other.astype(f32))).astype(bf16)
        kept = dict(
            x=x, query=query, h1=h1, qkv=qkv, probs=probs, mixed=mixed, gains=gains, hq=hq,
            cq=cq_now, first=first, h2=h2, slope=slope, act=act, ckv=ckv, e=e, att=att,
            att_low=att_low, coef=coef,
        )
        return x_next, (q_part, q_other), kept

    def sums(kernel_plan, order_by, sides, shapes, height, name):
        outs = [shaped(shape, bf16, False) for shape in shapes for _ in range(n)]
        flat = run(
            partial(weight_grads, n, kernel_plan, order_by),
            name,
            (),
            [(order_c, SMEM), (order_r, SMEM)] + [full(s) for s in sides],
            outs,
            [pltpu.VMEM((height, 384), f32)],
            4e9,
        )
        return [flat[k * n : (k + 1) * n] for k in range(len(shapes))]

    def reduce_xy(parts, by_y):
        own, one, two, three = parts
        if by_y:
            got_one, got_three = across(one, 1), across(three, 1)
            got_two = across(two + got_three, 2)
        else:
            got_two, got_three = across(two, 2), across(three, 2)
            got_one = across(one + got_three, 1)
        return own.astype(f32) + got_one.astype(f32) + got_two.astype(f32)

    def reduce_col(parts, by_y):
        if not manual:
            return lax.psum_scatter(
                parts[0][0], ("dp", "seq"), scatter_dimension=0, tiled=True
            ).astype(f32)
        mine = reduce_xy(parts, by_y)
        total = mine[0]
        for r in range(1, nz):
            total = total + lax.ppermute(
                mine[r].astype(bf16), "dp", [(j, j ^ r) for j in range(nz)]
            ).astype(f32)
        return total

    def reduce_row(parts, by_y, splits):
        if not manual:
            out = []
            at = 0
            for height in splits:
                part = parts[0][0][at : at + height * nz * ns // 2]
                at += height * nz * ns // 2
                both = lax.all_gather(part, "section", axis=0, tiled=True)
                out.append(
                    lax.psum_scatter(both, ("dp", "seq"), scatter_dimension=0, tiled=True).astype(f32)
                )
            return out
        mine = reduce_xy(parts, by_y)
        total = mine[0]
        for r in range(1, nz):
            pairs = [
                (c * nz + (j ^ r), c * nz + j)
                for c in range(2)
                for j in range(c * near, (c + 1) * near)
            ]
            total = total + lax.ppermute(
                mine[r % near].astype(bf16), ("section", "dp"), pairs
            ).astype(f32)
        out = []
        at = 0
        for height in splits:
            out.append(total[at : at + height])
            at += height
        return out

    share = 1.0 / ns
    height_down = hid // (nz * ns // 2) if manual else hid
    height_out = HALF // (nz * ns // 2) if manual else HALF
    slots_c, rows_c = (nz, rows) if manual else (1, D)
    slots_r = near if manual else 1

    def backward(layer, grad_patch, grad_query, kept):
        u = units[layer]
        shifted = layer == 1
        gains = kept["gains"]
        du, dckv, dcq_part, part, dcross = run(
            partial(mlp_backward, n),
            "mlp_backward",
            (batches,),
            [(order_c, SMEM), (order_r, SMEM)]
            + [
                batched(a)
                for a in (
                    grad_patch, kept["slope"], kept["e"], kept["coef"], grad_query, live,
                    kept["att"], kept["cq"], kept["ckv"],
                )
            ]
            + pieces(u[2])
            + pieces(u[3]),
            [
                shaped((batches, tokens, hid), bf16),
                shaped((batches, tokens, D), bf16),
                shaped((batches, NQ, HALF), bf16),
                shaped((batches, tokens, D), bf16),
                shaped((batches, NQ, D), bf16),
            ],
            [
                pltpu.VMEM((D, hid + D), bf16),
                pltpu.VMEM((hid, D), bf16),
                pltpu.VMEM((HALF, D), bf16),
                dma,
                dma,
                dma,
            ],
            4e9,
        )
        other = swap(part)
        dcq_all = [dcq_part] + [across(dcq_part, r) for r in range(1, ns)]

        def flat(a):
            return a.reshape(-1, a.shape[-1])

        early_c, early_r = sums(
            (
                (0, 1, 0, rows_c, 0, 0),
                (0, 2, 0, rows_c, 0, hid),
                (3, 4, 1, height_down, 0, 0),
                (5, 6, 1, height_out, height_down, 0),
            ),
            "cr",
            [
                flat(kept["h2"]), flat(du), flat(dckv), flat(kept["act"]), flat(grad_patch),
                flat(kept["att_low"]), flat(dcross * jnp.asarray(share, bf16)),
            ],
            [(slots_c, rows_c, hid + D), (slots_r, height_down + height_out, D)],
            hid,
            "early_grads",
        )
        grad_first, first_low, grad_mixed, dg_mlp = run(
            partial(first_backward, n),
            "first_backward",
            (batches,),
            [(order_r, SMEM)]
            + [batched(a) for a in (grad_patch, part, other, kept["first"])]
            + [full(gains)]
            + pieces(u[1]),
            [
                shaped((batches, tokens, D), f32),
                shaped((batches, tokens, D), bf16),
                shaped((batches, tokens, HALF), bf16),
                shaped((8, D), f32, False),
            ],
            [pltpu.VMEM((HALF, D), bf16), dma],
            4e8,
        )
        wide_grad = widened(grad_mixed) if shifted else grad_mixed
        wide = wide_grad.shape[1]
        dqkv, part = run(
            partial(attn_backward, n),
            "attn_backward",
            (batches,),
            [(order_c, SMEM)]
            + [batched(a) for a in (wide_grad, kept["qkv"], kept["probs"])]
            + pieces(u[0]),
            [shaped((batches, tokens, 3 * HALF), bf16), shaped((batches, tokens, D), bf16)],
            [pltpu.VMEM((D, 3 * HALF), bf16), pltpu.VMEM((wide, 3 * HALF), f32), dma],
            2e9,
        )
        other = swap(part)
        dcq, q_part = run(
            partial(query_back_one, n, ns),
            "query_back_one",
            (),
            [(order_c, SMEM), (order_s, SMEM)] + [full(a) for a in dcq_all] + pieces(u[2]),
            [shaped((batches, NQ, HALF), bf16, False), shaped((batches, NQ, D), bf16, False)],
            [pltpu.VMEM((D, HALF), bf16), pltpu.VMEM((ns, batches, NQ, HALF), bf16), dma],
            2e8,
        )
        q_other = swap(q_part)
        late_c, late_r = sums(
            (
                (0, 1, 0, rows_c, 0, 0),
                (2, 3, 0, rows_c, 0, 3 * HALF),
                (4, 5, 1, height_out, 0, 0),
            ),
            "cr",
            [
                flat(kept["h1"]), flat(dqkv), flat(kept["hq"]), flat(dcq * jnp.asarray(share, bf16)),
                flat(kept["mixed"]), flat(first_low),
            ],
            [(slots_c, rows_c, 4 * HALF), (slots_r, height_out, D)],
            D,
            "late_grads",
        )
        dx, dg_attn = run(
            input_backward,
            "input_backward",
            (batches,),
            [batched(a) for a in (kept["x"], grad_first, part, other)] + [full(gains)],
            [shaped((batches, tokens, D), bf16), shaped((8, D), f32, False)],
            [],
            1e8,
        )
        dq, dg_query = run(
            query_back_two,
            "query_back_two",
            (),
            [full(a) for a in (kept["query"], grad_query, q_part, q_other, gains)],
            [shaped((batches, NQ, D), bf16, False), shaped((8, D), f32, False)],
            [],
            1e8,
        )
        dgains = jnp.concatenate([dg_attn[0:1], dg_mlp[0:1], dg_query[0:1] * share], axis=0)
        return dx, dq, dgains, (early_c, early_r, late_c, late_r)

    x1, q_parts, kept0 = forward(0, pages, query_start, None)
    x2, q_parts_two, kept1 = forward(1, x1, query_start, q_parts)
    query_last = (
        kept1["query"].astype(f32)
        + live * (q_parts_two[0].astype(f32) + q_parts_two[1].astype(f32))
    ).astype(bf16)
    dx1, dq1, dgains1, raw1 = backward(1, given, query_given, kept1)
    down_rows, out_rows = mlp_down.shape[1], attn_output.shape[1]

    def reduced(raw):
        early_c, early_r, late_c, late_r = raw
        return (
            [reduce_col(early_c, True)]
            + reduce_row(early_r, False, (down_rows, out_rows))
            + [reduce_col(late_c, False)]
            + reduce_row(late_r, True, (out_rows,))
        )

    res1 = reduced(raw1)
    sent1 = [lax.ppermute(r, "section", [(0, 1)]) for r in res1]
    dx0, dq0, dgains0, raw0 = backward(0, dx1, dq1, kept0)
    res0 = reduced(raw0)
    sent0 = [lax.ppermute(r, "section", [(1, 0)]) for r in res0]

    def col_halves(k):
        low = jnp.where(core_zero, res0[k], sent1[k])
        high = jnp.where(core_zero, sent0[k], res1[k])
        return low, high

    holder = zi // near if manual else core

    def row_block(k):
        own = jnp.where(core_zero, res0[k], res1[k])
        sent = jnp.where(core_zero, sent0[k], sent1[k])
        return jnp.where(holder == core, own, sent)

    low, high = col_halves(0)
    grad_up = jnp.concatenate([low[:, :hid], high[:, :hid]], axis=1)
    grad_pair = jnp.concatenate(
        [
            low[:, hid : hid + HALF], high[:, hid : hid + HALF],
            low[:, hid + HALF :], high[:, hid + HALF :],
        ],
        axis=1,
    )
    low, high = col_halves(3)
    grad_in = jnp.concatenate(
        [side[:, k * HALF : (k + 1) * HALF] for k in range(3) for side in (low, high)], axis=1
    )
    grad_cq = jnp.concatenate([low[:, 3 * HALF :], high[:, 3 * HALF :]], axis=1)
    grad_down, grad_co, grad_out = row_block(1), row_block(2), row_block(4)

    gain_sums = jnp.concatenate([dgains0, dgains1, jnp.zeros((2, D), f32)], axis=0)
    if manual:
        for axis, count in (("seq", ns), ("dp", nz)):
            base = gain_sums
            for r in range(1, count):
                gain_sums = gain_sums + lax.ppermute(
                    base, axis, [(j, j ^ r) for j in range(count)]
                )
    else:
        gain_sums = lax.psum(gain_sums, ("dp", "seq"))
    mine = jnp.where(core_zero, gain_sums[0:3], gain_sums[3:6])
    mine = lax.dynamic_slice_in_dim(mine, (zi * ns + qi) * rows, rows, axis=1)

    patch_ends = jnp.where(core_zero, dx0, x2).reshape(1, batches, row_count, col_count, D)
    query_ends = jnp.take(jnp.where(core_zero, dq0, query_last), plan[0], axis=0)[None]
    return (
        patch_ends,
        query_ends,
        mine[0:1],
        mine[1:2],
        mine[2:3],
        grad_in[None],
        grad_out[None],
        grad_up[None],
        grad_down[None],
        grad_cq[None],
        grad_pair[None],
        grad_co[None],
    )


def solution(mesh):
    return jax.shard_map(
        per_device,
        mesh=mesh,
        in_specs=(
            P("dp", "seq", None, None),
            P("dp", None, None),
            P("dp"),
            P("dp", "seq", None),
            P("dp"),
            P("dp", None),
            P("section", ("dp", "seq")),
            P("section", ("dp", "seq")),
            P("section", ("dp", "seq")),
            P("section", ("dp", "seq"), None),
            P("section", ("dp", "seq"), None),
            P("section", ("dp", "seq"), None),
            P("section", ("dp", "seq"), None),
            P("section", ("dp", "seq"), None),
            P("section", ("dp", "seq"), None),
            P("section", ("dp", "seq"), None),
            P("dp", "seq", None, None),
            P("dp", None, None),
        ),
        out_specs=(
            P("section", "dp", "seq", None, None),
            P("section", "dp", None, None),
            P("section", ("dp", "seq")),
            P("section", ("dp", "seq")),
            P("section", ("dp", "seq")),
            P("section", ("dp", "seq"), None),
            P("section", ("dp", "seq"), None),
            P("section", ("dp", "seq"), None),
            P("section", ("dp", "seq"), None),
            P("section", ("dp", "seq"), None),
            P("section", ("dp", "seq"), None),
            P("section", ("dp", "seq"), None),
        ),
        check_vma=False,
    )
```

```python
from functools import partial
import itertools
import math

import jax
import jax.numpy as jnp
from jax import lax
from jax.experimental import pallas as pl
from jax.experimental.pallas import tpu as pltpu
from jax.sharding import PartitionSpec as P

D = 768
HEADS = 12
HDIM = 64
WIN = 12
NQ = 128
CELLS = WIN * WIN
HALF = D // 2
HH = HEADS // 2
PAIRS = HH // 2
RIM = WIN // 2 * WIN
CQ_AT = 128 + 3 * HALF
OUT_AT = CQ_AT + HALF

epsilon = 1e-05
hidden_value = -1e30
scaling = 1.0 / math.sqrt(HDIM)
bf16 = jnp.bfloat16
f32 = jnp.float32
SWAP = [(0, 1), (1, 0)]
ANY = pl.BlockSpec(memory_space=pl.ANY)
SMEM = pl.BlockSpec(memory_space=pltpu.SMEM)


def whole(shape):
    return pl.BlockSpec(shape, lambda *_: (0,) * len(shape))


def per_batch(shape):
    return pl.BlockSpec((1,) + tuple(shape[1:]), lambda m: (m,) + (0,) * (len(shape) - 1))


def run(kernel, name, grid, ins, outs, scratch, micros):
    arrays = [a for a, _ in ins]
    return pl.pallas_call(
        kernel,
        grid=grid,
        in_specs=[s for _, s in ins],
        out_specs=[s for _, _, s in outs],
        out_shape=[jax.ShapeDtypeStruct(sh, dt) for sh, dt, _ in outs],
        scratch_shapes=scratch,
        compiler_params=pltpu.CompilerParams(vmem_limit_bytes=52 * 1024 * 1024),
        cost_estimate=pl.CostEstimate(flops=int(micros * 1.15e9 * 1), bytes_accessed=0, transcendentals=0),
        name=name,
    )(*arrays)


def slots_of(pieces):
    near = pieces[3].shape[0]
    spots = [(p, k, p, k) for p in range(3) for k in range(2 * near)]
    return spots + [(3 + h, k, 3, h * near + k) for h in range(2) for k in range(near)]


def segments(unit, layout, col0, cols):
    count, off_x, off_y, cut = layout
    slots = unit[0].shape[0]
    for p, off in enumerate((0, off_x, off_y)):
        for k in range(slots):
            yield p, col0 + off, 0, cols, p, k
    for piece, low, high in ((3, 0, cut), (4, cut, col0 + cols)):
        start, end = max(low, col0), min(high, col0 + cols)
        if start < end:
            for k in range(slots):
                yield piece, start - low, start - col0, end - start, 3, k


def fetch_columns(dst, unit, layout, order, col0, sem):
    cols = dst.shape[1]
    if len(unit) < 5:
        pltpu.make_async_copy(unit[0].at[:, pl.ds(col0, cols)], dst, sem).start()
        return
    slots, rows = unit[0].shape[:2]
    for piece, come, off, width, p, k in segments(unit, layout, col0, cols):
        to = pl.multiple_of(order[p * slots + k] * rows, 16)
        pltpu.make_async_copy(
            unit[piece].at[k, :, pl.ds(come, width)], dst.at[pl.ds(to, rows), pl.ds(off, width)], sem
        ).start()


def fetch_rows(dst, unit, layout, order, col0, row0, sem):
    if len(unit) < 5:
        if len(unit[0].shape) == 5:
            slots, spots, sides, rows, _ = unit[0].shape
            each = dst.shape[0] // (slots * spots)
            for k, p, side, b in itertools.product(
                range(slots), range(spots), range(sides), range(each // rows)
            ):
                to = pl.multiple_of(order[p * slots + k] * each + b * rows, 16)
                pltpu.make_async_copy(
                    unit[0].at[k, p, side, :, pl.ds(col0 + b * HALF, HALF)],
                    dst.at[pl.ds(to, rows), pl.ds(side * HALF, HALF)],
                    sem,
                ).start()
            return
        pltpu.make_async_copy(unit[-1].at[pl.ds(row0, dst.shape[0]), :], dst, sem).start()
        return
    slots, rows = unit[0].shape[:2]
    each = dst.shape[0] // (2 * slots)
    for b in range(each // rows):
        for piece, come, off, width, p, k in segments(unit, layout, col0 + b * HALF, HALF):
            base = order[p * (slots // 2) + k // 2] * each
            to = pl.multiple_of(base + b * rows, 16)
            pltpu.make_async_copy(
                unit[piece].at[k, :, pl.ds(come, width)],
                dst.at[pl.ds(to, rows), pl.ds((k % 2) * HALF + off, width)],
                sem,
            ).start()


def end_fetch(dst, sem):
    pltpu.make_async_copy(dst, dst, sem).wait()


def spread_columns(acc, unit, order, col0):
    cols = acc.shape[1]
    if len(unit) < 5:
        unit[0][:, col0 : col0 + cols] = acc[0:D].astype(bf16)
        return
    slots, rows = unit[0].shape[:2]
    for piece, at, p, k in slots_of(unit):
        come = pl.multiple_of(order[p * slots + k] * rows, 8)
        unit[piece][at, :, col0 : col0 + cols] = acc[pl.ds(come, rows), :].astype(bf16)


def spread_rows(acc, unit, order, height, side, col0, row0):
    if len(unit) < 5:
        unit[-1][row0 : row0 + height, side * HALF : side * HALF + HALF] = acc[0:height].astype(bf16)
        return
    slots, rows = unit[0].shape[:2]
    each = height // (2 * slots)
    for piece, at, p, k in slots_of(unit):
        if k % 2 != side:
            continue
        base = order[p * (slots // 2) + k // 2] * each
        for b in range(each // rows):
            come = pl.multiple_of(base + b * rows, 8)
            unit[piece][at, :, col0 + b * HALF : col0 + b * HALF + HALF] = acc[
                pl.ds(come, rows), :
            ].astype(bf16)


def nn(a, b):
    return jnp.dot(a, b, preferred_element_type=f32)


def nt(a, b):
    return lax.dot_general(a, b, (((1,), (1,)), ((), ())), preferred_element_type=f32)


def tn(a, b):
    return lax.dot_general(a, b, (((0,), (0,)), ((), ())), preferred_element_type=f32)


def norm_parts(values):
    center = values - jnp.mean(values, axis=-1, keepdims=True)
    inv = lax.rsqrt(jnp.mean(center * center, axis=-1, keepdims=True) + epsilon)
    return center * inv, inv


def norm_back(unit, inv, gain, grad):
    scaled = grad * gain
    return inv * (
        scaled
        - jnp.mean(scaled, axis=-1, keepdims=True)
        - unit * jnp.mean(scaled * unit, axis=-1, keepdims=True)
    )


def co_at(lower):
    if len(lower[0].shape) == 5:
        return lower[0].shape[4] - HALF, 0
    if len(lower) < 5:
        return 0, lower[-1].shape[0] - HALF
    return lower[0].shape[2] - HALF, 0


def lane_halves(rows):
    lane = lax.broadcasted_iota(jnp.int32, (rows, 128), 1)
    return lane < HDIM


def half_masks():
    lane = lax.broadcasted_iota(jnp.int32, (1, 128), 1)
    low = (lane < HDIM).astype(f32)
    return low.astype(bf16), (1.0 - low).astype(bf16)


def attn_forward(n, shifted, *refs):
    order_c, order_r, x_ref = refs[:3]
    refs = refs[3:]
    if shifted:
        mask_ref, refs = refs[0], refs[1:]
    unit, refs = refs[: n[0][0]], refs[n[0][0] :]
    h_ref, qkv_ref, p_ref, o_ref, part_ref, gain_ref, w_in, w_out, mixed, hidden, sem0, sem1 = refs
    tokens = x_ref.shape[1]
    own = o_ref.shape[1]
    lo = (tokens - own) // 2

    @pl.when(pl.program_id(0) == 0)
    def _():
        fetch_columns(w_in, unit, n[0], order_c, 0, sem0)
        fetch_rows(w_out, unit, n[0], order_r, OUT_AT, 0, sem1)
        end_fetch(w_in, sem0)
        end_fetch(w_out, sem1)
        gain_ref[...] = w_in[:, :128].astype(f32).T[0:8]

    direction, _ = norm_parts(x_ref[0].astype(f32))
    hidden[...] = direction * gain_ref[0:1]
    h_ref[0] = hidden[lo : lo + own].astype(bf16)
    qkv_ref[0] = nn(hidden[...].astype(bf16), w_in[:, 128:]).astype(bf16)
    first_half = lane_halves(CELLS)
    masks = half_masks()
    for block in range(tokens // CELLS):
        rows = slice(block * CELLS, (block + 1) * CELLS)
        for pair in range(PAIRS):
            q2 = qkv_ref[0, rows, pair * 128 : pair * 128 + 128]
            k2 = qkv_ref[0, rows, HALF + pair * 128 : HALF + pair * 128 + 128]
            v2 = qkv_ref[0, rows, 2 * HALF + pair * 128 : 2 * HALF + pair * 128 + 128]
            mixed_two = []
            for side in range(2):
                scores = nt(q2 * masks[side], k2) * scaling
                if shifted:
                    scores = scores + mask_ref[block]
                weights = jnp.exp(scores - jnp.max(scores, axis=-1, keepdims=True))
                probs = (weights / jnp.sum(weights, axis=-1, keepdims=True)).astype(bf16)
                p_ref[0, block * HH + pair * 2 + side] = probs
                mixed_two.append(nn(probs, v2))
            mixed[rows, pair * 128 : pair * 128 + 128] = jnp.where(
                first_half, mixed_two[0], mixed_two[1]
            )
    out = mixed[lo : lo + own].astype(bf16)
    o_ref[0] = out
    part_ref[0] = nn(out, w_out[...]).astype(bf16)


def mlp_forward(n, *refs):
    order_c, order_r, x_ref, pa_ref, pb_ref, gain_ref, cq_ref, valid_ref = refs[:8]
    refs = refs[8:]
    upper, lower, refs = refs[: n[1][0]], refs[n[1][0] : n[1][0] + n[2][0]], refs[n[1][0] + n[2][0] :]
    first_ref, h_ref, slope_ref, act_ref, part_ref, ckv_ref, e_ref, o_ref = refs[:8]
    w_up, w_down, sem0, sem1 = refs[8:]
    hid = slope_ref.shape[2]
    tokens = x_ref.shape[1]

    @pl.when(pl.program_id(0) == 0)
    def _():
        fetch_columns(w_up, upper, n[1], order_c, 0, sem0)
        fetch_rows(w_down, lower, n[2], order_r, 0, 0, sem1)
        end_fetch(w_up, sem0)
        end_fetch(w_down, sem1)

    first = x_ref[0].astype(f32) + (pa_ref[0].astype(f32) + pb_ref[0].astype(f32))
    first_ref[0] = first
    unit, _ = norm_parts(first)
    hidden = (unit * gain_ref[1:2]).astype(bf16)
    h_ref[0] = hidden
    ckv_ref[0] = nn(hidden, w_up[:, hid:]).astype(bf16)
    step = 512
    for at in range(0, hid, step):
        lifted = nn(hidden, w_up[:, at : at + step])
        cdf = 0.5 + 0.5 * lax.erf(lifted * math.sqrt(0.5))
        act_ref[0, :, at : at + step] = (lifted * cdf).astype(bf16)
        pdf = jnp.exp(lifted * lifted * -0.5) * (1.0 / math.sqrt(2.0 * math.pi))
        slope_ref[0, :, at : at + step] = (cdf + lifted * pdf).astype(bf16)
    part_ref[0] = nn(act_ref[0], w_down[...]).astype(bf16)

    valid = jnp.broadcast_to(valid_ref[0], (NQ, tokens)) > 0.5
    first_half = lane_halves(NQ)
    masks = half_masks()
    lane = lax.broadcasted_iota(jnp.int32, (NQ, 128), 1)
    stats = jnp.zeros((NQ, 128), f32)
    for pair in range(PAIRS):
        q2 = cq_ref[0, :, pair * 128 : pair * 128 + 128]
        k2 = ckv_ref[0, :, pair * 128 : pair * 128 + 128]
        v2 = ckv_ref[0, :, HALF + pair * 128 : HALF + pair * 128 + 128]
        mixed_two = []
        for side in range(2):
            head = pair * 2 + side
            scores = jnp.where(valid, nt(q2 * masks[side], k2) * scaling, hidden_value)
            peak = jnp.max(scores, axis=-1, keepdims=True)
            weights = jnp.where(valid, jnp.exp(scores - peak), 0.0)
            total = jnp.sum(weights, axis=-1, keepdims=True)
            for at, value in ((0, peak), (16, total)):
                high = value.astype(bf16).astype(f32)
                stats = jnp.where(lane == at + head, high, stats)
                stats = jnp.where(lane == at + 8 + head, value - high, stats)
            low = weights.astype(bf16)
            e_ref[0, head] = low
            mixed_two.append(nn(low, v2))
        o_ref[0, :, pair * 128 : pair * 128 + 128] = jnp.where(
            first_half, mixed_two[0], mixed_two[1]
        ).astype(bf16)
    o_ref[0, :, HALF:] = stats.astype(bf16)


def query_in(n, has_parts, *refs):
    order_c, q_ref, gain_ref = refs[:3]
    refs = refs[3:]
    if has_parts:
        pa_ref, pb_ref, live_ref, refs = refs[0], refs[1], refs[2], refs[3:]
    unit, refs = refs[: n[0][0]], refs[n[0][0] :]
    if has_parts:
        new_ref, refs = refs[0], refs[1:]
    h_ref, cq_ref, w_q, sem = refs
    fetch_columns(w_q, unit, n[0], order_c, CQ_AT, sem)
    end_fetch(w_q, sem)
    for m in range(q_ref.shape[0]):
        query = q_ref[m].astype(f32)
        if has_parts:
            query = query + live_ref[m] * (pa_ref[m].astype(f32) + pb_ref[m].astype(f32))
            low = query.astype(bf16)
            new_ref[m] = low
            query = low.astype(f32)
        direction, _ = norm_parts(query)
        hidden = (direction * gain_ref[2:3]).astype(bf16)
        h_ref[m] = hidden
        cq_ref[m] = nn(hidden, w_q[...]).astype(bf16)


def query_out(n, ns, *refs):
    order_r, order_s = refs[:2]
    refs = refs[2:]
    os, refs = refs[:ns], refs[ns:]
    lower, refs = refs[: n[2][0]], refs[n[2][0] :]
    att_ref, low_ref, coef_ref, part_ref, w_co, o_all, sem = refs
    fetch_rows(w_co, lower, n[2], order_r, *co_at(lower), sem)
    for p in range(ns):
        o_all[order_s[p]] = os[p][...]
    first_half = lane_halves(NQ)
    end_fetch(w_co, sem)

    def stat(block, at):
        wide = block.astype(f32)
        return wide[:, at : at + 8] + wide[:, at + 8 : at + 16]

    for m in range(att_ref.shape[0]):
        stats = [o_all[s, m, :, HALF:] for s in range(ns)]
        peaks = [stat(block, 0) for block in stats]
        peak = peaks[0]
        for other in peaks[1:]:
            peak = jnp.maximum(peak, other)
        scales = [jnp.exp(p - peak) for p in peaks]
        total = scales[0] * stat(stats[0], 16)
        for scale, block in zip(scales[1:], stats[1:]):
            total = total + scale * stat(block, 16)
        inverse = 1.0 / jnp.where(total > 0.0, total, 1.0)
        coef_ref[m, :, 0:8] = jnp.exp(stat(os[0][m, :, HALF:], 0) - peak) * inverse
        factors = [scale * inverse for scale in scales]
        for pair in range(PAIRS):
            mixed = jnp.zeros((NQ, 128), f32)
            for s in range(ns):
                at = pair * 2
                factor = jnp.where(
                    first_half, factors[s][:, at : at + 1], factors[s][:, at + 1 : at + 2]
                )
                mixed = mixed + factor * o_all[s, m, :, pair * 128 : pair * 128 + 128].astype(f32)
            att_ref[m, :, pair * 128 : pair * 128 + 128] = mixed
        low = att_ref[m].astype(bf16)
        low_ref[m] = low
        part_ref[m] = nn(low, w_co[...]).astype(bf16)


def mlp_backward(n, *refs):
    order_c, order_r, ds_ref, slope_ref, e_ref, coef_ref, dq_ref, live_ref, att_ref, cq_ref, ckv_ref = refs[:11]
    refs = refs[11:]
    upper, lower, refs = refs[: n[1][0]], refs[n[1][0] : n[1][0] + n[2][0]], refs[n[1][0] + n[2][0] :]
    du_ref, dckv_ref, dcq_ref, part_ref, dc_ref, w_up, w_down, w_co, sem0, sem1, sem2 = refs
    hid = slope_ref.shape[2]
    tokens = ds_ref.shape[1]

    @pl.when(pl.program_id(0) == 0)
    def _():
        fetch_rows(w_down, lower, n[2], order_r, 0, 0, sem1)
        fetch_rows(w_co, lower, n[2], order_r, *co_at(lower), sem2)
        fetch_columns(w_up, upper, n[1], order_c, 0, sem0)
        end_fetch(w_down, sem1)
        end_fetch(w_co, sem2)
        end_fetch(w_up, sem0)

    grad_second = ds_ref[0]
    step = 512
    for at in range(0, hid, step):
        grad_act = nt(grad_second, w_down[at : at + step, :])
        du_ref[0, :, at : at + step] = (
            grad_act * slope_ref[0, :, at : at + step].astype(f32)
        ).astype(bf16)

    grad_cross = (live_ref[0] * dq_ref[0].astype(f32)).astype(bf16)
    dc_ref[0] = grad_cross
    grad_att = nt(grad_cross, w_co[...]).astype(bf16)
    first_q = lane_halves(NQ)
    first_k = lane_halves(tokens)
    masks = half_masks()
    for pair in range(PAIRS):
        lanes = slice(pair * 128, pair * 128 + 128)
        upper = slice(HALF + pair * 128, HALF + pair * 128 + 128)
        a2 = grad_att[:, lanes]
        q2 = cq_ref[0, :, lanes]
        k2 = ckv_ref[0, :, lanes]
        v2 = ckv_ref[0, :, upper]
        inner = a2.astype(f32) * att_ref[0, :, lanes]
        dq_two, dk_two, dv_two = [], [], []
        for side in range(2):
            head = pair * 2 + side
            keep = first_q if side == 0 else jnp.logical_not(first_q)
            delta = jnp.sum(jnp.where(keep, inner, 0.0), axis=-1, keepdims=True)
            probs = e_ref[0, head].astype(f32) * coef_ref[0, :, head : head + 1]
            grad_probs = nt(a2 * masks[side], v2)
            grad_scores = (probs * (grad_probs - delta)).astype(bf16)
            dq_two.append(nn(grad_scores, k2))
            dk_two.append(tn(grad_scores, q2))
            dv_two.append(tn(probs.astype(bf16), a2))
        dcq_ref[0, :, lanes] = (jnp.where(first_q, dq_two[0], dq_two[1]) * scaling).astype(bf16)
        dckv_ref[0, :, lanes] = (jnp.where(first_k, dk_two[0], dk_two[1]) * scaling).astype(bf16)
        dckv_ref[0, :, upper] = jnp.where(first_k, dv_two[0], dv_two[1]).astype(bf16)
    part_ref[0] = (
        nt(du_ref[0], w_up[:, :hid]) + nt(dckv_ref[0], w_up[:, hid:])
    ).astype(bf16)


def first_backward(n, *refs):
    order_r, ds_ref, da_ref, db_ref, first_ref, gain_ref = refs[:6]
    source, refs = refs[6 : 6 + n[0][0]], refs[6 + n[0][0] :]
    df_ref, low_ref, do_ref, dg_ref, w_out, sem = refs

    @pl.when(pl.program_id(0) == 0)
    def _():
        fetch_rows(w_out, source, n[0], order_r, OUT_AT, 0, sem)
        dg_ref[...] = jnp.zeros_like(dg_ref)
        end_fetch(w_out, sem)

    grad = da_ref[0].astype(f32) + db_ref[0].astype(f32)
    unit, inv = norm_parts(first_ref[0])
    dg_ref[0:1] += jnp.sum(grad * unit, axis=0, keepdims=True)
    grad_first = ds_ref[0].astype(f32) + norm_back(unit, inv, gain_ref[1:2], grad)
    df_ref[0] = grad_first
    low = grad_first.astype(bf16)
    low_ref[0] = low
    do_ref[0] = nt(low, w_out[...]).astype(bf16)


def attn_backward(n, *refs):
    order_c, do_ref, qkv_ref, p_ref = refs[:4]
    unit, refs = refs[4 : 4 + n[0][0]], refs[4 + n[0][0] :]
    dqkv_ref, part_ref, w_in, wide, sem = refs
    tokens = do_ref.shape[1]
    own = dqkv_ref.shape[1]
    lo = (tokens - own) // 2

    @pl.when(pl.program_id(0) == 0)
    def _():
        fetch_columns(w_in, unit, n[0], order_c, 128, sem)
        end_fetch(w_in, sem)

    first_half = lane_halves(CELLS)
    masks = half_masks()
    for block in range(tokens // CELLS):
        rows = slice(block * CELLS, (block + 1) * CELLS)
        for pair in range(PAIRS):
            lanes = slice(pair * 128, pair * 128 + 128)
            q2 = qkv_ref[0, rows, lanes]
            k2 = qkv_ref[0, rows, HALF + pair * 128 : HALF + pair * 128 + 128]
            v2 = qkv_ref[0, rows, 2 * HALF + pair * 128 : 2 * HALF + pair * 128 + 128]
            g2 = do_ref[0, rows, lanes]
            dq_two, dk_two, dv_two = [], [], []
            for side in range(2):
                probs = p_ref[0, block * HH + pair * 2 + side]
                wide_probs = probs.astype(f32)
                grad_probs = nt(g2 * masks[side], v2)
                delta = jnp.sum(wide_probs * grad_probs, axis=-1, keepdims=True)
                grad_scores = (wide_probs * (grad_probs - delta)).astype(bf16)
                dq_two.append(nn(grad_scores, k2))
                dk_two.append(tn(grad_scores, q2))
                dv_two.append(tn(probs, g2))
            wide[rows, lanes] = jnp.where(first_half, dq_two[0], dq_two[1]) * scaling
            wide[rows, HALF + pair * 128 : HALF + pair * 128 + 128] = (
                jnp.where(first_half, dk_two[0], dk_two[1]) * scaling
            )
            wide[rows, 2 * HALF + pair * 128 : 2 * HALF + pair * 128 + 128] = jnp.where(
                first_half, dv_two[0], dv_two[1]
            )
    low = wide[lo : lo + own].astype(bf16)
    dqkv_ref[0] = low
    part_ref[0] = nt(low, w_in[...]).astype(bf16)


def input_backward(x_ref, df_ref, da_ref, db_ref, gain_ref, dx_ref, dg_ref):
    @pl.when(pl.program_id(0) == 0)
    def _():
        dg_ref[...] = jnp.zeros_like(dg_ref)

    grad = da_ref[0].astype(f32) + db_ref[0].astype(f32)
    unit, inv = norm_parts(x_ref[0].astype(f32))
    dg_ref[0:1] += jnp.sum(grad * unit, axis=0, keepdims=True)
    dx_ref[0] = (df_ref[0] + norm_back(unit, inv, gain_ref[0:1], grad)).astype(bf16)


def query_back_one(n, *refs):
    order_c, one_ref, two_ref = refs[:3]
    unit, refs = refs[3 : 3 + n[0][0]], refs[3 + n[0][0] :]
    dcq_ref, part_ref, w_q, sem = refs
    fetch_columns(w_q, unit, n[0], order_c, CQ_AT, sem)
    end_fetch(w_q, sem)
    for m in range(dcq_ref.shape[0]):
        low = (one_ref[m].astype(f32) + two_ref[m].astype(f32)).astype(bf16)
        dcq_ref[m] = low
        part_ref[m] = nt(low, w_q[...]).astype(bf16)


def query_back_two(q_ref, dq_ref, da_ref, db_ref, gain_ref, out_ref, dg_ref):
    total = jnp.zeros((1, D), f32)
    for m in range(q_ref.shape[0]):
        grad = da_ref[m].astype(f32) + db_ref[m].astype(f32)
        unit, inv = norm_parts(q_ref[m].astype(f32))
        total = total + jnp.sum(grad * unit, axis=0, keepdims=True)
        out_ref[m] = (dq_ref[m].astype(f32) + norm_back(unit, inv, gain_ref[2:3], grad)).astype(bf16)
    dg_ref[...] = jnp.broadcast_to(total, dg_ref.shape)


def weight_grads(n, plan, *refs):
    order_c, order_r = refs[:2]
    count = 1 + max(max(item[0], item[1]) for item in plan)
    sides, refs = refs[2 : 2 + count], refs[2 + count :]
    outs = []
    for k in n:
        outs.append(refs[:k])
        refs = refs[k:]
    acc = refs[0]
    for left, right, unit, by_rows, col0, row0 in plan:
        height, width = sides[left].shape[1], sides[right].shape[1]
        if left == right:
            turned = jnp.concatenate([sides[left][...], jnp.zeros((120, height), f32)], axis=0).T
            acc[0:height, 0:128] = turned
            spread_columns(acc.at[:, 0:128], outs[unit], order_c, col0)
            continue
        for at in range(0, width, HALF):
            acc[0:height] = tn(sides[left][...], sides[right][:, at : at + HALF])
            if by_rows:
                spread_rows(acc, outs[unit], order_r, height, at // HALF, col0, row0)
            else:
                spread_columns(acc, outs[unit], order_c, col0 + at)


def per_device(
    patches,
    queries,
    page_rows,
    window_mask,
    query_lengths,
    plan,
    norm_attn,
    norm_mlp,
    norm_query,
    attn_input,
    attn_output,
    mlp_up,
    mlp_down,
    cross_query,
    cross_pair,
    cross_output,
    patch_cotangent,
    query_cotangent,
):
    core = lax.axis_index("section")
    zi = lax.axis_index("dp")
    qi = lax.axis_index("seq")
    nz, ns = lax.axis_size("dp"), lax.axis_size("seq")
    rows = attn_input.shape[1]
    hid = mlp_up.shape[2] // 2
    manual = rows % 16 == 0 and ns == 4 and nz & (nz - 1) == 0
    near = nz // 2
    batches, row_count, col_count = patches.shape[:3]
    tokens = row_count * col_count
    core_zero = core == 0

    def swap(x):
        return lax.ppermute(x, "section", SWAP)

    def across(x, r):
        return lax.ppermute(x, "seq", [(j, j ^ r) for j in range(ns)])

    def tied(x, after):
        return x if after is None else lax.optimization_barrier((x, after))[0]

    far = (zi // near) ^ core
    if manual:
        order_c = [((zi ^ r) * ns + (qi ^ p)) for p in range(ns) for r in range(nz)]
        order_r = [
            ((zi ^ (far * near + k)) - core * near) * ns + (qi ^ p)
            for p in range(ns)
            for k in range(near)
        ]
    else:
        order_c = order_r = [zi]
    order_s = [qi ^ p for p in range(ns)]
    order_c, order_r, order_s = (
        jnp.stack(o).astype(jnp.int32) for o in (order_c, order_r, order_s)
    )

    gain_block = jnp.stack([norm_attn[0], norm_mlp[0], norm_query[0]], axis=1)
    gain_block = jnp.pad(gain_block, ((0, 0), (0, 125)))
    win, up, cq, cp = attn_input[0], mlp_up[0], cross_query[0], cross_pair[0]

    def half_columns(side):
        def half(a, w):
            return a[:, side * w : (side + 1) * w]

        first = [half(win[:, k * D : (k + 1) * D], HALF) for k in range(3)]
        return [
            jnp.concatenate([gain_block] + first + [half(cq, HALF)], axis=1),
            jnp.concatenate([half(up, hid), half(cp[:, :D], HALF), half(cp[:, D:], HALF)], axis=1),
        ]

    halves = [half_columns(side) for side in range(2)]

    def fold(w):
        return jnp.stack(
            [
                jnp.concatenate(
                    [
                        w[b * rows : (b + 1) * rows, side * HALF : (side + 1) * HALF]
                        for b in range(w.shape[0] // rows)
                    ],
                    axis=1,
                )
                for side in range(2)
            ]
        )

    down_co = jnp.concatenate([mlp_down[0], cross_output[0]], axis=0)

    def z_pairs(bit):
        return [
            (c * nz + j, c * nz + (j ^ bit))
            for c in range(2)
            for j in range(c * near, (c + 1) * near)
        ]

    def z_step(parts, bit, after):
        out = []
        for stack, by_rows in parts:
            stack = tied(stack, after)
            if not by_rows:
                got = lax.ppermute(stack, "dp", [(j, j ^ bit) for j in range(nz)])
                out.append((jnp.concatenate([stack, got]), False, got))
                continue
            got = lax.ppermute(stack, ("section", "dp"), z_pairs(bit))
            if bit < near:
                stack = jnp.concatenate([stack, got])
            else:
                stack = jnp.where(far == 0, stack, got)
                stack = stack.reshape((nz,) + stack.shape[2:])
            out.append((stack, True, got))
        return [o[:2] for o in out], tuple(o[2] for o in out)

    units = [[None] * 3 for _ in range(2)]
    counts = [[None] * 3 for _ in range(2)]
    if manual:
        col_send = [jnp.where(core_zero, b, a) for a, b in zip(*halves)]
        col_mine = [jnp.where(core_zero, a, b) for a, b in zip(*halves)]
        row_mine = [fold(attn_output[0]), fold(down_co)]
        col_recv = [swap(col_send[0])]
        row_recv = [swap(row_mine[0])]
        col_recv.append(swap(tied(col_send[1], (col_recv[0], row_recv[0]))))
        row_recv.append(swap(tied(row_mine[1], (col_recv[0], row_recv[0]))))

        queue = []
        for layer in range(2):
            own_layer = core == layer
            cols = [jnp.where(own_layer, a, b)[None] for a, b in zip(col_mine, col_recv)]
            folded = [jnp.where(own_layer, a, b)[None] for a, b in zip(row_mine, row_recv)]
            queue += [[(cols[0], False), (folded[0], True)], [(cols[1], False)], [(folded[1], True)]]
        bits = []
        while 2 ** len(bits) < nz:
            bits.append(2 ** len(bits))
        last_rows = queue.pop()[0][0][0]
        count = len(queue)

        def early_steps(k, after):
            tokens_of = ()
            for bit in bits[:-1]:
                queue[k], after = z_step(queue[k], bit, after)
                tokens_of += after
            return tokens_of

        lead = early_steps(0, None)
        queue[0], _ = z_step(queue[0], bits[-1], lead)
        ahead = early_steps(1, lead)
        token = ()
        messages = []
        from_x = from_y = jnp.zeros((nz, rows, 0), bf16)
        cut = 0
        before = None
        for k in range(count + 1):
            low, high = from_x[..., :cut], from_y[..., cut:]
            x_parts, y_parts = [high], [low]
            own = None
            if k < count:
                parts = [stack for stack, _ in queue[k]]
                own = parts[0] if len(parts) == 1 else jnp.concatenate(parts, axis=2)
                own = tied(own, token)
                x_parts.append(own)
                y_parts.append(own)
            sent_x, sent_y = jnp.concatenate(x_parts, axis=2), jnp.concatenate(y_parts, axis=2)
            messages.append((sent_x, sent_y))
            got_x, got_y = across(sent_x, 1), across(sent_y, 2)
            if k + 1 < count:
                queue[k + 1], got = z_step(queue[k + 1], bits[-1], (token, ahead))
                ahead = early_steps(k + 2, got) if k + 2 < count else got
            if before is not None:
                b = k - 1
                units[b // 3][b % 3] = before[0] + [got_y, got_x]
                counts[b // 3][b % 3] = (5,) + before[1] + (cut,)
            if own is None:
                break
            before = ([own, got_x, got_y], (high.shape[2], low.shape[2]))
            from_x, from_y = got_x[..., high.shape[2] :], got_y[..., low.shape[2] :]
            cut = own.shape[2] // 256 * 128
            token = (got_x, got_y)
        stack = jnp.stack([last_rows] + [across(last_rows, r) for r in range(1, ns)])[None]
        stack = tied(stack, ahead)
        for bit in bits:
            got = lax.ppermute(stack, ("section", "dp"), z_pairs(bit))
            stack = jnp.concatenate([stack, got]) if bit < near else jnp.where(far == 0, stack, got)
        units[1][2] = [stack]
        counts[1][2] = (1, 0, 0, 0)
        counts = tuple(tuple(c) for c in counts)
    else:

        def gather_all(x):
            return lax.all_gather(
                lax.all_gather(x, ("dp", "seq"), axis=0, tiled=True), "section", axis=0
            )

        whole_cols = [[gather_all(h[k]) for h in halves] for k in range(2)]
        whole_rows = [gather_all(x) for x in (attn_output[0], mlp_down[0], cross_output[0])]
        for layer in range(2):
            cols = [jnp.where(core_zero, a[layer], b[layer]) for a, b in whole_cols]
            mine = [
                lax.dynamic_slice_in_dim(w[layer], core * (w.shape[1] // 2), w.shape[1] // 2, 0)
                for w in whole_rows
            ]
            units[layer] = [[cols[0], mine[0]], [cols[1]], [jnp.concatenate(mine[1:], axis=0)]]
        counts = (((2, 0, 0, 0), (1, 0, 0, 0), (1, 0, 0, 0)),) * 2
        messages = [()] * 7

    order = jnp.arange(batches)
    inverse = jnp.sum(jnp.where(plan[0][None, :] == order[:, None], order[None, :], 0), axis=1)
    query_start = jnp.take(queries, inverse, axis=0)
    query_given = jnp.take(query_cotangent, inverse, axis=0)
    lengths = jnp.take(query_lengths, inverse)
    live = (jnp.arange(NQ)[None, :] < lengths[:, None]).astype(f32)[:, :, None]
    window_rows = qi * (row_count // WIN) + jnp.arange(row_count // WIN)
    marks = (window_rows[None, :, None] < page_rows[:, None, None]) & (window_mask == 1)
    valid = jnp.repeat(jnp.repeat(marks, WIN, axis=1), WIN, axis=2)
    valid = valid.reshape(batches, 1, tokens).astype(f32)
    blocks_wide = (row_count + WIN) // WIN
    cell = jnp.arange(CELLS)
    frame_row = qi * row_count - WIN // 2 + jnp.arange(blocks_wide)[:, None] * WIN + cell // WIN
    inside = (frame_row >= 0) & (frame_row < row_count * ns)
    side_of = (cell % WIN) < WIN // 2
    same = side_of[:, None] == side_of[None, :]
    mask = jnp.where(inside[:, None, :] & same[None], 0.0, hidden_value).astype(f32)

    pages = patches.reshape(batches, tokens, D)
    given = patch_cotangent.reshape(batches, tokens, D)

    def widened(edge_source):
        top = lax.ppermute(
            edge_source[:, tokens - RIM :], "seq", [(j, j + 1) for j in range(ns - 1)]
        )
        bottom = lax.ppermute(edge_source[:, :RIM], "seq", [(j + 1, j) for j in range(ns - 1)])
        return jnp.concatenate([top, edge_source, bottom], axis=1)

    def pieces(unit):
        return [(piece, ANY) for piece in unit]

    def shaped(shape, dtype, batched=True):
        return (shape, dtype, per_batch(shape) if batched else whole(shape))

    def batched(a):
        return (a, per_batch(a.shape))

    def full(a):
        return (a, whole(a.shape))

    dma = pltpu.SemaphoreType.DMA

    def forward(layer, x, query, query_parts):
        u, n = units[layer], counts[layer]
        shifted = layer == 1
        wide_x = wide_x1 if shifted else x
        wide = wide_x.shape[1]
        blocks = wide // CELLS
        wide_x = tied(wide_x, messages[2 + 3 * layer])
        ins = [(order_c, SMEM), (order_r, SMEM), batched(wide_x)]
        if shifted:
            ins.append(full(mask))
        h1, qkv, probs, mixed, part, gains = run(
            partial(attn_forward, n, shifted),
            "attn_forward",
            (batches,),
            ins + pieces(u[0]),
            [
                shaped((batches, tokens, D), bf16),
                shaped((batches, wide, 3 * HALF), bf16),
                shaped((batches, blocks * HH, CELLS, CELLS), bf16),
                shaped((batches, tokens, HALF), bf16),
                shaped((batches, tokens, D), bf16),
                shaped((8, D), f32, False),
            ],
            [
                pltpu.VMEM((D, 128 + 3 * HALF), bf16),
                pltpu.VMEM((HALF, D), bf16),
                pltpu.VMEM((wide, HALF), f32),
                pltpu.VMEM((wide, D), f32),
                dma,
                dma,
            ],
            10,
        )
        other = swap(part)
        q_ins = [(order_c, SMEM), full(query), full(gains)]
        q_outs = [
            shaped((batches, NQ, D), bf16, False),
            shaped((batches, NQ, HALF), bf16, False),
        ]
        if query_parts is not None:
            q_ins += [full(query_parts[0]), full(query_parts[1]), full(live)]
            q_outs = [shaped((batches, NQ, D), bf16, False)] + q_outs
        got = run(
            partial(query_in, n, query_parts is not None),
            "query_in",
            (),
            q_ins + pieces(u[0]),
            q_outs,
            [pltpu.VMEM((D, HALF), bf16), dma],
            2.5,
        )
        if query_parts is not None:
            query, got = got[0], got[1:]
        hq, cq_now = got
        first, h2, slope, act, second_part, ckv, e, o = run(
            partial(mlp_forward, n),
            "mlp_forward",
            (batches,),
            [
                (order_c, SMEM),
                (order_r, SMEM),
                batched(tied(x, messages[min(4 + 2 * layer, len(messages) - 1)])),
                batched(part),
                batched(other),
                full(gains),
                batched(cq_now),
                batched(valid),
            ]
            + pieces(u[1])
            + pieces(u[2]),
            [
                shaped((batches, tokens, D), f32),
                shaped((batches, tokens, D), bf16),
                shaped((batches, tokens, hid), bf16),
                shaped((batches, tokens, hid), bf16),
                shaped((batches, tokens, D), bf16),
                shaped((batches, tokens, D), bf16),
                shaped((batches, HH, NQ, tokens), bf16),
                shaped((batches, NQ, HALF + 128), bf16),
            ],
            [pltpu.VMEM((D, hid + D), bf16), pltpu.VMEM((hid, D), bf16), dma, dma],
            14,
        )
        second_other = swap(second_part)
        os = [o] + [across(o, r) for r in range(1, ns)]
        att, att_low, coef, q_part = run(
            partial(query_out, n, ns),
            "query_out",
            (),
            [(order_r, SMEM), (order_s, SMEM)]
            + [full(a) for a in os]
            + pieces(u[2]),
            [
                shaped((batches, NQ, HALF), f32, False),
                shaped((batches, NQ, HALF), bf16, False),
                shaped((batches, NQ, 128), f32, False),
                shaped((batches, NQ, D), bf16, False),
            ],
            [
                pltpu.VMEM((HALF, D), bf16),
                pltpu.VMEM((ns, batches, NQ, HALF + 128), bf16),
                dma,
            ],
            4.5,
        )
        q_other = swap(q_part)
        x_next = (first + (second_part.astype(f32) + second_other.astype(f32))).astype(bf16)
        kept = dict(
            x=x, query=query, h1=h1, qkv=qkv, probs=probs, mixed=mixed, gains=gains, hq=hq,
            cq=cq_now, first=first, h2=h2, slope=slope, act=act, ckv=ckv, e=e, att=att,
            att_low=att_low, coef=coef,
        )
        return x_next, (q_part, q_other), kept

    def sums(kernel_plan, sides, shapes, height, name, after=None):
        flat = run(
            partial(weight_grads, tuple(len(unit) for unit in shapes), kernel_plan),
            name,
            (),
            [(order_c, SMEM), (order_r, SMEM)] + [full(s) for s in sides],
            [shaped(shape, bf16, False) for unit in shapes for shape in unit],
            [pltpu.VMEM((height, HALF), f32)],
            12 if height > D else 6,
        )
        out = []
        for unit in shapes:
            out.append(flat[: len(unit)])
            flat = flat[len(unit) :]
        return out

    def unit_shapes(cols, row_height):
        if not manual:
            shapes = [(D, cols)] if cols else []
            return shapes + ([(row_height, D)] if row_height else [])
        width = cols + row_height // (rows * nz * ns // 2) * HALF
        return [(nz, rows, width)] * 3 + [(near, rows, width)] * 2

    def reduce_one(unit, after):
        own, one, two, low, high = unit
        low, high = tied((low, high), after)
        low, high = across(low, 2), across(high, 1)
        return (own, one, two, low, high), (low, high)

    def reduce_two(unit, after):
        own, one, two, low, high = tied(unit, after)
        one = jnp.concatenate([one[:near] + low, one[near:]])
        two = jnp.concatenate([two[:near], two[near:] + high])
        one, two = across(one, 1), across(two, 2)
        return (own, one, two), (one, two)

    def reduce_three(unit, cols, after):
        own, one, two = tied(unit, after)
        total = own.astype(f32) + one.astype(f32) + two.astype(f32)
        col, row = total[..., :cols], total[..., cols:]
        sent = col[near:].astype(bf16)
        got_col = lax.ppermute(sent, "dp", [(j, j ^ near) for j in range(nz)])
        sent = row.astype(bf16)
        got_row = lax.ppermute(sent, ("section", "dp"), [(b, a) for a, b in z_pairs(near)])
        return [(col[:near], got_col), (row, got_row)], (got_col, got_row)

    def reduce_four(parts, after):
        out = []
        token = ()
        for by_rows, (total, got) in enumerate(tied(parts, after)):
            total = total + got.astype(f32)
            if by_rows:
                total = total.reshape((near, 2) + total.shape[1:])
            bit = near // 2
            while bit:
                sent = total[bit:].astype(bf16)
                pairs = [(b, a) for a, b in z_pairs(bit)] if by_rows else [
                    (j, j ^ bit) for j in range(nz)
                ]
                got = lax.ppermute(sent, ("section", "dp") if by_rows else "dp", pairs)
                token += (got,)
                total = total[:bit] + got.astype(f32)
                bit //= 2
            out.append(total[0])
        return out, token

    def unfold(row):
        blocks = row.shape[2] // HALF
        return jnp.concatenate(
            [
                jnp.concatenate([row[side, :, b * HALF : (b + 1) * HALF] for side in range(2)], axis=1)
                for b in range(blocks)
            ],
            axis=0,
        )

    def reduce_plain(unit, cols, heights):
        out = []
        if cols:
            out.append(lax.psum_scatter(unit[0], ("dp", "seq"), scatter_dimension=0, tiled=True))
        if len(unit) > 1 or not cols:
            cut = heights[0] * nz * ns // 2
            pieces_of = [unit[-1][:cut], unit[-1][cut:]]
            out += [
                lax.psum_scatter(
                    lax.all_gather(piece, "section", axis=0, tiled=True),
                    ("dp", "seq"),
                    scatter_dimension=0,
                    tiled=True,
                )
                for piece in pieces_of
            ]
        return [o.astype(f32) for o in out]

    share = 1.0 / ns

    def backward(layer, grad_patch, grad_query, kept, emit):
        u, n = units[layer], counts[layer]
        shifted = layer == 1
        gains = kept["gains"]
        du, dckv, dcq_part, part, dcross = run(
            partial(mlp_backward, n),
            "mlp_backward",
            (batches,),
            [(order_c, SMEM), (order_r, SMEM)]
            + [
                batched(a)
                for a in (
                    grad_patch, kept["slope"], kept["e"], kept["coef"], grad_query, live,
                    kept["att"], kept["cq"], kept["ckv"],
                )
            ]
            + pieces(u[1])
            + pieces(u[2]),
            [
                shaped((batches, tokens, hid), bf16),
                shaped((batches, tokens, D), bf16),
                shaped((batches, NQ, HALF), bf16),
                shaped((batches, tokens, D), bf16),
                shaped((batches, NQ, D), bf16),
            ],
            [
                pltpu.VMEM((D, hid + D), bf16),
                pltpu.VMEM((hid, D), bf16),
                pltpu.VMEM((HALF, D), bf16),
                dma,
                dma,
                dma,
            ],
            14,
        )
        emit("mlp", part)
        other = swap(part)
        dcq_got = across(dcq_part, 1)

        def flat(a):
            return a.reshape(-1, a.shape[-1])

        row_at = hid + D if manual else 0
        row_base = hid // (nz * ns // 2) // rows * HALF if manual else 0
        early = sums(
            (
                (0, 1, 0, False, 0, 0),
                (0, 2, 0, False, hid, 0),
                (3, 4, 0, True, row_at, 0),
                (5, 6, 0, True, row_at + row_base, hid),
            ),
            [
                flat(kept["h2"]), flat(du), flat(dckv), flat(kept["act"]), flat(grad_patch),
                flat(kept["att_low"]), flat(dcross * jnp.asarray(share, bf16)),
            ],
            [unit_shapes(hid + D, hid + HALF)],
            hid,
            "early_grads",
        )
        part = tied(part, early[0][0])
        dcq_got = tied(dcq_got, early[0][0])
        bit = 2
        while bit < ns:
            dcq_part = (dcq_part.astype(f32) + dcq_got.astype(f32)).astype(bf16)
            dcq_got = across(dcq_part, bit)
            bit *= 2
        emit("early", (early[0], dcq_part))
        grad_first, first_low, grad_mixed, dg_mlp = run(
            partial(first_backward, n),
            "first_backward",
            (batches,),
            [(order_r, SMEM)]
            + [batched(a) for a in (grad_patch, part, other, kept["first"])]
            + [full(gains)]
            + pieces(u[0]),
            [
                shaped((batches, tokens, D), f32),
                shaped((batches, tokens, D), bf16),
                shaped((batches, tokens, HALF), bf16),
                shaped((8, D), f32, False),
            ],
            [pltpu.VMEM((HALF, D), bf16), dma],
            5.6,
        )
        wide_grad = widened(grad_mixed) if shifted else grad_mixed
        emit("first", grad_mixed)
        wide = wide_grad.shape[1]
        dqkv, part = run(
            partial(attn_backward, n),
            "attn_backward",
            (batches,),
            [(order_c, SMEM)]
            + [batched(a) for a in (wide_grad, kept["qkv"], kept["probs"])]
            + pieces(u[0]),
            [shaped((batches, tokens, 3 * HALF), bf16), shaped((batches, tokens, D), bf16)],
            [pltpu.VMEM((D, 3 * HALF), bf16), pltpu.VMEM((wide, 3 * HALF), f32), dma],
            15,
        )
        emit("attn", part)
        other = swap(part)
        dcq_got = tied(dcq_got, dqkv)
        dcq, q_part = run(
            partial(query_back_one, n),
            "query_back_one",
            (),
            [(order_c, SMEM), full(dcq_part), full(dcq_got)] + pieces(u[0]),
            [shaped((batches, NQ, HALF), bf16, False), shaped((batches, NQ, D), bf16, False)],
            [pltpu.VMEM((D, HALF), bf16), dma],
            2.5,
        )
        q_other = swap(q_part)
        last_x = kept["x"]
        dx, dg_attn = run(
            input_backward,
            "input_backward",
            (batches,),
            [batched(a) for a in (last_x, grad_first, part, other)] + [full(gains)],
            [shaped((batches, tokens, D), bf16), shaped((8, D), f32, False)],
            [],
            3,
        )
        dq, dg_query = run(
            query_back_two,
            "query_back_two",
            (),
            [full(a) for a in (kept["query"], grad_query, q_part, q_other, gains)],
            [shaped((batches, NQ, D), bf16, False), shaped((8, D), f32, False)],
            [],
            1,
        )
        dgains = jnp.concatenate([dg_attn[0:1], dg_mlp[0:1], dg_query[0:1] * share], axis=0)
        emit(
            "late",
            ([
                flat(kept["h1"]), flat(dqkv), flat(kept["hq"]), flat(dcq * jnp.asarray(share, bf16)),
                flat(kept["mixed"]), flat(first_low),
            ], dgains),
        )
        return dx, dq

    x1, q_parts, kept0 = forward(0, pages, query_start, None)
    wide_x1 = widened(x1)
    x2, q_parts_two, kept1 = forward(1, x1, query_start, q_parts)
    query_last = (
        kept1["query"].astype(f32)
        + live * (q_parts_two[0].astype(f32) + q_parts_two[1].astype(f32))
    ).astype(bf16)

    widths = (hid + D, hid + D, 8 * HALF + 128)
    out_rows = attn_output.shape[1]
    heights = [(mlp_down.shape[1], cross_output.shape[1])] * 2 + [(out_rows, out_rows)]
    state = [None] * 3
    late_sides = []

    rounds = [()]

    def one_round(*items, after=()):
        for unit, step in items:
            now = state[unit]
            if not manual:
                if step == 4:
                    now = reduce_plain(now, widths[unit], heights[unit])
            elif step == 1:
                now, got = reduce_one(now, after)
            elif step == 2:
                now, got = reduce_two(now, after)
            elif step == 3:
                now, got = reduce_three(now, widths[unit], after)
            else:
                now, got = reduce_four(now, after)
                rows_of = unfold(now[1])
                cut = heights[unit][0]
                now = [now[0], rows_of[:cut], rows_of[cut:]]
            state[unit] = now
            rounds[unit, step] = got if manual else ()

    rounds = {}

    def emit_late_layer(what, value):
        if what == "early":
            state[1] = value[0]
            one_round((1, 1), after=value[1])
        elif what == "attn":
            one_round((1, 2), after=value)
        elif what == "late":
            late_sides.extend(value)

    def emit_first_layer(what, value):
        if what == "early":
            state[0] = value[0]
            one_round((0, 1), after=value[1])
            one_round((1, 3), after=value[1])
        elif what == "first":
            one_round((0, 2), after=value)
        elif what == "late":
            sides = tied(late_sides[0] + value[0], rounds[1, 3])
            gain_sums = jnp.concatenate(
                [value[1], late_sides[1], jnp.zeros((2, D), f32)], axis=0
            )
            row_at = 8 * HALF + 128
            (state[2],) = sums(
                [
                    item
                    for k in range(2)
                    for item in (
                        (6 * k, 6 * k + 1, 0, False, 4 * HALF * k, 0),
                        (6 * k + 2, 6 * k + 3, 0, False, 4 * HALF * k + 3 * HALF, 0),
                        (6 * k + 4, 6 * k + 5, 0, True, row_at + HALF * k, HALF * k),
                    )
                ]
                + [(12, 12, 0, False, 8 * HALF, 0)],
                sides + [gain_sums],
                [unit_shapes(8 * HALF + 128, 2 * HALF)],
                D,
                "late_grads",
            )
            one_round((2, 1))

    given = tied(given, x2)
    kept1["h2"] = tied(kept1["h2"], query_last)
    dx1, dq1 = backward(1, given, query_given, kept1, emit_late_layer)
    dx0, dq0 = backward(0, dx1, dq1, kept0, emit_first_layer)
    one_round((1, 4), after=state[2][0])
    one_round((0, 3), after=state[2][0])
    one_round((2, 2), after=(rounds[0, 2], state[2][0]))
    one_round((2, 3), after=rounds[0, 3])
    one_round((0, 4), after=rounds[2, 2])

    def handed(low, high):
        return [swap(jnp.where(core_zero, b, a)) for a, b in zip(low, high)]

    got_early = handed(
        [state[0][0], jnp.concatenate(state[0][1:], axis=0)],
        [state[1][0], jnp.concatenate(state[1][1:], axis=0)],
    )
    one_round((2, 4), after=(rounds[0, 4], got_early))
    cols, rows_of = state[2][0], state[2][1:]
    low_cols, high_cols = cols[:, : 4 * HALF], cols[:, 4 * HALF : 8 * HALF]
    got_late = handed([high_cols, rows_of[1]], [low_cols, rows_of[0]])
    own_early = [jnp.where(core_zero, a, b) for a, b in zip(state[0], state[1])]
    own_late = [jnp.where(core_zero, high_cols, low_cols)]
    own_late.append(jnp.where(core_zero, rows_of[1], rows_of[0]))
    cut = heights[0][0]
    mine = own_early + own_late
    theirs = [got_early[0], got_early[1][:cut], got_early[1][cut:]] + got_late

    def col_halves(k):
        low = jnp.where(core_zero, mine[k], theirs[k])
        high = jnp.where(core_zero, theirs[k], mine[k])
        return low, high

    holder = zi // near if manual else core

    def row_block(k):
        return jnp.where(holder == core, mine[k], theirs[k])

    low, high = col_halves(0)
    grad_up = jnp.concatenate([low[:, :hid], high[:, :hid]], axis=1)
    grad_pair = jnp.concatenate(
        [
            low[:, hid : hid + HALF], high[:, hid : hid + HALF],
            low[:, hid + HALF :], high[:, hid + HALF :],
        ],
        axis=1,
    )
    low, high = col_halves(3)
    grad_in = jnp.concatenate(
        [side[:, k * HALF : (k + 1) * HALF] for k in range(3) for side in (low, high)], axis=1
    )
    grad_cq = jnp.concatenate([low[:, 3 * HALF :], high[:, 3 * HALF :]], axis=1)
    grad_down, grad_co, grad_out = row_block(1), row_block(2), row_block(4)

    gain_rows = jnp.where(core_zero, cols[:, 8 * HALF : 8 * HALF + 3], cols[:, 8 * HALF + 3 : 8 * HALF + 6])
    own_gains = gain_rows.T

    patch_ends = jnp.where(core_zero, dx0, x2).reshape(1, batches, row_count, col_count, D)
    query_ends = jnp.take(jnp.where(core_zero, dq0, query_last), plan[0], axis=0)[None]
    return (
        patch_ends,
        query_ends,
        own_gains[0:1],
        own_gains[1:2],
        own_gains[2:3],
        grad_in[None],
        grad_out[None],
        grad_up[None],
        grad_down[None],
        grad_cq[None],
        grad_pair[None],
        grad_co[None],
    )


def solution(mesh):
    return jax.shard_map(
        per_device,
        mesh=mesh,
        in_specs=(
            P("dp", "seq", None, None),
            P("dp", None, None),
            P("dp"),
            P("dp", "seq", None),
            P("dp"),
            P("dp", None),
            P("section", ("dp", "seq")),
            P("section", ("dp", "seq")),
            P("section", ("dp", "seq")),
            P("section", ("dp", "seq"), None),
            P("section", ("dp", "seq"), None),
            P("section", ("dp", "seq"), None),
            P("section", ("dp", "seq"), None),
            P("section", ("dp", "seq"), None),
            P("section", ("dp", "seq"), None),
            P("section", ("dp", "seq"), None),
            P("dp", "seq", None, None),
            P("dp", None, None),
        ),
        out_specs=(
            P("section", "dp", "seq", None, None),
            P("section", "dp", None, None),
            P("section", ("dp", "seq")),
            P("section", ("dp", "seq")),
            P("section", ("dp", "seq")),
            P("section", ("dp", "seq"), None),
            P("section", ("dp", "seq"), None),
            P("section", ("dp", "seq"), None),
            P("section", ("dp", "seq"), None),
            P("section", ("dp", "seq"), None),
            P("section", ("dp", "seq"), None),
            P("section", ("dp", "seq"), None),
        ),
        check_vma=False,
    )
```

```python
from functools import partial
import itertools
import math

import jax
import jax.numpy as jnp
from jax import lax
from jax.experimental import pallas as pl
from jax.experimental.pallas import tpu as pltpu
from jax.sharding import PartitionSpec as P

D = 768
HEADS = 12
HDIM = 64
WIN = 12
NQ = 128
CELLS = WIN * WIN
HALF = D // 2
HH = HEADS // 2
PAIRS = HH // 2
RIM = WIN // 2 * WIN
CQ_AT = 128 + 3 * HALF
OUT_AT = CQ_AT + HALF

epsilon = 1e-05
hidden_value = -1e30
scaling = 1.0 / math.sqrt(HDIM)
bf16 = jnp.bfloat16
f32 = jnp.float32
SWAP = [(0, 1), (1, 0)]
ANY = pl.BlockSpec(memory_space=pl.ANY)
SMEM = pl.BlockSpec(memory_space=pltpu.SMEM)


def whole(shape):
    return pl.BlockSpec(shape, lambda *_: (0,) * len(shape))


def per_batch(shape):
    return pl.BlockSpec((1,) + tuple(shape[1:]), lambda m: (m,) + (0,) * (len(shape) - 1))


def run(kernel, name, grid, ins, outs, scratch, micros):
    arrays = [a for a, _ in ins]
    return pl.pallas_call(
        kernel,
        grid=grid,
        in_specs=[s for _, s in ins],
        out_specs=[s for _, _, s in outs],
        out_shape=[jax.ShapeDtypeStruct(sh, dt) for sh, dt, _ in outs],
        scratch_shapes=scratch,
        compiler_params=pltpu.CompilerParams(vmem_limit_bytes=52 * 1024 * 1024),
        cost_estimate=pl.CostEstimate(flops=int(micros * 1.15e9 * 1), bytes_accessed=0, transcendentals=0),
        name=name,
    )(*arrays)


def slots_of(pieces):
    near = pieces[3].shape[0]
    spots = [(p, k, p, k) for p in range(3) for k in range(2 * near)]
    return spots + [(3 + h, k, 3, h * near + k) for h in range(2) for k in range(near)]


def segments(unit, layout, col0, cols):
    count, off_x, off_y, cut = layout
    slots = unit[0].shape[0]
    for p, off in enumerate((0, off_x, off_y)):
        for k in range(slots):
            yield p, col0 + off, 0, cols, p, k
    for piece, low, high in ((3, 0, cut), (4, cut, col0 + cols)):
        start, end = max(low, col0), min(high, col0 + cols)
        if start < end:
            for k in range(slots):
                yield piece, start - low, start - col0, end - start, 3, k


def fetch_columns(dst, unit, layout, order, col0, sem):
    cols = dst.shape[1]
    if len(unit) < 5:
        pltpu.make_async_copy(unit[0].at[:, pl.ds(col0, cols)], dst, sem).start()
        return
    slots, rows = unit[0].shape[:2]
    for piece, come, off, width, p, k in segments(unit, layout, col0, cols):
        to = pl.multiple_of(order[p * slots + k] * rows, 16)
        pltpu.make_async_copy(
            unit[piece].at[k, :, pl.ds(come, width)], dst.at[pl.ds(to, rows), pl.ds(off, width)], sem
        ).start()


def fetch_rows(dst, unit, layout, order, col0, row0, sem):
    if len(unit) < 5:
        if len(unit[0].shape) == 5:
            slots, spots, sides, rows, _ = unit[0].shape
            each = dst.shape[0] // (slots * spots)
            for k, p, side, b in itertools.product(
                range(slots), range(spots), range(sides), range(each // rows)
            ):
                to = pl.multiple_of(order[p * slots + k] * each + b * rows, 16)
                pltpu.make_async_copy(
                    unit[0].at[k, p, side, :, pl.ds(col0 + b * HALF, HALF)],
                    dst.at[pl.ds(to, rows), pl.ds(side * HALF, HALF)],
                    sem,
                ).start()
            return
        pltpu.make_async_copy(unit[-1].at[pl.ds(row0, dst.shape[0]), :], dst, sem).start()
        return
    slots, rows = unit[0].shape[:2]
    each = dst.shape[0] // (2 * slots)
    for b in range(each // rows):
        for piece, come, off, width, p, k in segments(unit, layout, col0 + b * HALF, HALF):
            base = order[p * (slots // 2) + k // 2] * each
            to = pl.multiple_of(base + b * rows, 16)
            pltpu.make_async_copy(
                unit[piece].at[k, :, pl.ds(come, width)],
                dst.at[pl.ds(to, rows), pl.ds((k % 2) * HALF + off, width)],
                sem,
            ).start()


def end_fetch(dst, sem):
    pltpu.make_async_copy(dst, dst, sem).wait()


def spread_columns(acc, unit, order, col0):
    cols = acc.shape[1]
    if len(unit) < 5:
        unit[0][:, col0 : col0 + cols] = acc[0:D].astype(bf16)
        return
    slots, rows = unit[0].shape[:2]
    for piece, at, p, k in slots_of(unit):
        come = pl.multiple_of(order[p * slots + k] * rows, 8)
        unit[piece][at, :, col0 : col0 + cols] = acc[pl.ds(come, rows), :].astype(bf16)


def spread_rows(acc, unit, order, height, side, col0, row0):
    if len(unit) < 5:
        unit[-1][row0 : row0 + height, side * HALF : side * HALF + HALF] = acc[0:height].astype(bf16)
        return
    slots, rows = unit[0].shape[:2]
    each = height // (2 * slots)
    for piece, at, p, k in slots_of(unit):
        if k % 2 != side:
            continue
        base = order[p * (slots // 2) + k // 2] * each
        for b in range(each // rows):
            come = pl.multiple_of(base + b * rows, 8)
            unit[piece][at, :, col0 + b * HALF : col0 + b * HALF + HALF] = acc[
                pl.ds(come, rows), :
            ].astype(bf16)


def nn(a, b):
    return jnp.dot(a, b, preferred_element_type=f32)


def nt(a, b):
    return lax.dot_general(a, b, (((1,), (1,)), ((), ())), preferred_element_type=f32)


def tn(a, b):
    return lax.dot_general(a, b, (((0,), (0,)), ((), ())), preferred_element_type=f32)


def norm_parts(values):
    center = values - jnp.mean(values, axis=-1, keepdims=True)
    inv = lax.rsqrt(jnp.mean(center * center, axis=-1, keepdims=True) + epsilon)
    return center * inv, inv


def norm_back(unit, inv, gain, grad):
    scaled = grad * gain
    return inv * (
        scaled
        - jnp.mean(scaled, axis=-1, keepdims=True)
        - unit * jnp.mean(scaled * unit, axis=-1, keepdims=True)
    )


def co_at(lower):
    if len(lower[0].shape) == 5:
        return lower[0].shape[4] - HALF, 0
    if len(lower) < 5:
        return 0, lower[-1].shape[0] - HALF
    return lower[0].shape[2] - HALF, 0


def lane_halves(rows):
    lane = lax.broadcasted_iota(jnp.int32, (rows, 128), 1)
    return lane < HDIM


def half_masks():
    lane = lax.broadcasted_iota(jnp.int32, (1, 128), 1)
    low = (lane < HDIM).astype(f32)
    return low.astype(bf16), (1.0 - low).astype(bf16)


def attn_forward(n, shifted, *refs):
    order_c, order_r, x_ref = refs[:3]
    refs = refs[3:]
    if shifted:
        mask_ref, refs = refs[0], refs[1:]
    unit, refs = refs[: n[0][0]], refs[n[0][0] :]
    h_ref, qkv_ref, p_ref, o_ref, part_ref, gain_ref, w_in, w_out, mixed, hidden, sem0, sem1 = refs
    tokens = x_ref.shape[1]
    own = o_ref.shape[1]
    lo = (tokens - own) // 2

    @pl.when(pl.program_id(0) == 0)
    def _():
        fetch_columns(w_in, unit, n[0], order_c, 0, sem0)
        fetch_rows(w_out, unit, n[0], order_r, OUT_AT, 0, sem1)
        end_fetch(w_in, sem0)
        end_fetch(w_out, sem1)
        gain_ref[...] = w_in[:, :128].astype(f32).T[0:8]

    direction, _ = norm_parts(x_ref[0].astype(f32))
    hidden[...] = direction * gain_ref[0:1]
    h_ref[0] = hidden[lo : lo + own].astype(bf16)
    qkv_ref[0] = nn(hidden[...].astype(bf16), w_in[:, 128:]).astype(bf16)
    first_half = lane_halves(CELLS)
    masks = half_masks()
    for block in range(tokens // CELLS):
        rows = slice(block * CELLS, (block + 1) * CELLS)
        for pair in range(PAIRS):
            q2 = qkv_ref[0, rows, pair * 128 : pair * 128 + 128]
            k2 = qkv_ref[0, rows, HALF + pair * 128 : HALF + pair * 128 + 128]
            v2 = qkv_ref[0, rows, 2 * HALF + pair * 128 : 2 * HALF + pair * 128 + 128]
            mixed_two = []
            for side in range(2):
                scores = nt(q2 * masks[side], k2) * scaling
                if shifted:
                    scores = scores + mask_ref[block]
                weights = jnp.exp(scores - jnp.max(scores, axis=-1, keepdims=True))
                probs = (weights / jnp.sum(weights, axis=-1, keepdims=True)).astype(bf16)
                p_ref[0, block * HH + pair * 2 + side] = probs
                mixed_two.append(nn(probs, v2))
            mixed[rows, pair * 128 : pair * 128 + 128] = jnp.where(
                first_half, mixed_two[0], mixed_two[1]
            )
    out = mixed[lo : lo + own].astype(bf16)
    o_ref[0] = out
    part_ref[0] = nn(out, w_out[...]).astype(bf16)


def mlp_forward(n, *refs):
    order_c, order_r, x_ref, pa_ref, pb_ref, gain_ref, cq_ref, valid_ref = refs[:8]
    refs = refs[8:]
    upper, lower, refs = refs[: n[1][0]], refs[n[1][0] : n[1][0] + n[2][0]], refs[n[1][0] + n[2][0] :]
    first_ref, h_ref, slope_ref, act_ref, part_ref, ckv_ref, e_ref, o_ref = refs[:8]
    w_up, w_down, sem0, sem1 = refs[8:]
    hid = slope_ref.shape[2]
    tokens = x_ref.shape[1]

    @pl.when(pl.program_id(0) == 0)
    def _():
        fetch_columns(w_up, upper, n[1], order_c, 0, sem0)
        fetch_rows(w_down, lower, n[2], order_r, 0, 0, sem1)
        end_fetch(w_up, sem0)
        end_fetch(w_down, sem1)

    first = x_ref[0].astype(f32) + (pa_ref[0].astype(f32) + pb_ref[0].astype(f32))
    first_ref[0] = first
    unit, _ = norm_parts(first)
    hidden = (unit * gain_ref[1:2]).astype(bf16)
    h_ref[0] = hidden
    ckv_ref[0] = nn(hidden, w_up[:, hid:]).astype(bf16)
    step = 512
    for at in range(0, hid, step):
        lifted = nn(hidden, w_up[:, at : at + step])
        cdf = 0.5 + 0.5 * lax.erf(lifted * math.sqrt(0.5))
        act_ref[0, :, at : at + step] = (lifted * cdf).astype(bf16)
        pdf = jnp.exp(lifted * lifted * -0.5) * (1.0 / math.sqrt(2.0 * math.pi))
        slope_ref[0, :, at : at + step] = (cdf + lifted * pdf).astype(bf16)
    part_ref[0] = nn(act_ref[0], w_down[...]).astype(bf16)

    valid = jnp.broadcast_to(valid_ref[0], (NQ, tokens)) > 0.5
    first_half = lane_halves(NQ)
    masks = half_masks()
    lane = lax.broadcasted_iota(jnp.int32, (NQ, 128), 1)
    stats = jnp.zeros((NQ, 128), f32)
    for pair in range(PAIRS):
        q2 = cq_ref[0, :, pair * 128 : pair * 128 + 128]
        k2 = ckv_ref[0, :, pair * 128 : pair * 128 + 128]
        v2 = ckv_ref[0, :, HALF + pair * 128 : HALF + pair * 128 + 128]
        mixed_two = []
        for side in range(2):
            head = pair * 2 + side
            scores = jnp.where(valid, nt(q2 * masks[side], k2) * scaling, hidden_value)
            peak = jnp.max(scores, axis=-1, keepdims=True)
            weights = jnp.where(valid, jnp.exp(scores - peak), 0.0)
            total = jnp.sum(weights, axis=-1, keepdims=True)
            for at, value in ((0, peak), (16, total)):
                high = value.astype(bf16).astype(f32)
                stats = jnp.where(lane == at + head, high, stats)
                stats = jnp.where(lane == at + 8 + head, value - high, stats)
            low = weights.astype(bf16)
            e_ref[0, head] = low
            mixed_two.append(nn(low, v2))
        o_ref[0, :, pair * 128 : pair * 128 + 128] = jnp.where(
            first_half, mixed_two[0], mixed_two[1]
        ).astype(bf16)
    o_ref[0, :, HALF:] = stats.astype(bf16)


def query_in(n, has_parts, *refs):
    order_c, q_ref, gain_ref = refs[:3]
    refs = refs[3:]
    if has_parts:
        pa_ref, pb_ref, live_ref, refs = refs[0], refs[1], refs[2], refs[3:]
    unit, refs = refs[: n[0][0]], refs[n[0][0] :]
    if has_parts:
        new_ref, refs = refs[0], refs[1:]
    h_ref, cq_ref, w_q, sem = refs
    fetch_columns(w_q, unit, n[0], order_c, CQ_AT, sem)
    end_fetch(w_q, sem)
    for m in range(q_ref.shape[0]):
        query = q_ref[m].astype(f32)
        if has_parts:
            query = query + live_ref[m] * (pa_ref[m].astype(f32) + pb_ref[m].astype(f32))
            low = query.astype(bf16)
            new_ref[m] = low
            query = low.astype(f32)
        direction, _ = norm_parts(query)
        hidden = (direction * gain_ref[2:3]).astype(bf16)
        h_ref[m] = hidden
        cq_ref[m] = nn(hidden, w_q[...]).astype(bf16)


def query_out(n, ns, *refs):
    order_r, order_s = refs[:2]
    refs = refs[2:]
    os, refs = refs[:ns], refs[ns:]
    lower, refs = refs[: n[2][0]], refs[n[2][0] :]
    att_ref, low_ref, coef_ref, part_ref, w_co, o_all, sem = refs
    fetch_rows(w_co, lower, n[2], order_r, *co_at(lower), sem)
    for p in range(ns):
        o_all[order_s[p]] = os[p][...]
    first_half = lane_halves(NQ)
    end_fetch(w_co, sem)

    def stat(block, at):
        wide = block.astype(f32)
        return wide[:, at : at + 8] + wide[:, at + 8 : at + 16]

    for m in range(att_ref.shape[0]):
        stats = [o_all[s, m, :, HALF:] for s in range(ns)]
        peaks = [stat(block, 0) for block in stats]
        peak = peaks[0]
        for other in peaks[1:]:
            peak = jnp.maximum(peak, other)
        scales = [jnp.exp(p - peak) for p in peaks]
        total = scales[0] * stat(stats[0], 16)
        for scale, block in zip(scales[1:], stats[1:]):
            total = total + scale * stat(block, 16)
        inverse = 1.0 / jnp.where(total > 0.0, total, 1.0)
        coef_ref[m, :, 0:8] = jnp.exp(stat(os[0][m, :, HALF:], 0) - peak) * inverse
        factors = [scale * inverse for scale in scales]
        for pair in range(PAIRS):
            mixed = jnp.zeros((NQ, 128), f32)
            for s in range(ns):
                at = pair * 2
                factor = jnp.where(
                    first_half, factors[s][:, at : at + 1], factors[s][:, at + 1 : at + 2]
                )
                mixed = mixed + factor * o_all[s, m, :, pair * 128 : pair * 128 + 128].astype(f32)
            att_ref[m, :, pair * 128 : pair * 128 + 128] = mixed
        low = att_ref[m].astype(bf16)
        low_ref[m] = low
        part_ref[m] = nn(low, w_co[...]).astype(bf16)


def mlp_backward(n, *refs):
    order_c, order_r, ds_ref, slope_ref = refs[:4]
    refs = refs[4:]
    upper, lower, refs = refs[: n[1][0]], refs[n[1][0] : n[1][0] + n[2][0]], refs[n[1][0] + n[2][0] :]
    du_ref, part_ref, w_up, w_down, sem0, sem1 = refs
    hid = slope_ref.shape[2]

    @pl.when(pl.program_id(0) == 0)
    def _():
        fetch_rows(w_down, lower, n[2], order_r, 0, 0, sem1)
        fetch_columns(w_up, upper, n[1], order_c, 0, sem0)
        end_fetch(w_down, sem1)
        end_fetch(w_up, sem0)

    grad_second = ds_ref[0]
    step = 512
    for at in range(0, hid, step):
        grad_act = nt(grad_second, w_down[at : at + step, :])
        du_ref[0, :, at : at + step] = (
            grad_act * slope_ref[0, :, at : at + step].astype(f32)
        ).astype(bf16)
    part_ref[0] = nt(du_ref[0], w_up[...])


def cross_backward(n, hid, *refs):
    order_c, order_r, before_ref, e_ref, coef_ref, dq_ref, live_ref, att_ref, cq_ref, ckv_ref = refs[:10]
    refs = refs[10:]
    upper, lower, refs = refs[: n[1][0]], refs[n[1][0] : n[1][0] + n[2][0]], refs[n[1][0] + n[2][0] :]
    dckv_ref, dcq_ref, part_ref, dc_ref, w_pair, w_co, sem0, sem1 = refs
    tokens = before_ref.shape[1]

    @pl.when(pl.program_id(0) == 0)
    def _():
        fetch_rows(w_co, lower, n[2], order_r, *co_at(lower), sem1)
        fetch_columns(w_pair, upper, n[1], order_c, hid, sem0)
        end_fetch(w_co, sem1)
        end_fetch(w_pair, sem0)

    grad_cross = (live_ref[0] * dq_ref[0].astype(f32)).astype(bf16)
    dc_ref[0] = grad_cross
    grad_att = nt(grad_cross, w_co[...]).astype(bf16)
    first_q = lane_halves(NQ)
    first_k = lane_halves(tokens)
    masks = half_masks()
    for pair in range(PAIRS):
        lanes = slice(pair * 128, pair * 128 + 128)
        upper = slice(HALF + pair * 128, HALF + pair * 128 + 128)
        a2 = grad_att[:, lanes]
        q2 = cq_ref[0, :, lanes]
        k2 = ckv_ref[0, :, lanes]
        v2 = ckv_ref[0, :, upper]
        inner = a2.astype(f32) * att_ref[0, :, lanes]
        dq_two, dk_two, dv_two = [], [], []
        for side in range(2):
            head = pair * 2 + side
            keep = first_q if side == 0 else jnp.logical_not(first_q)
            delta = jnp.sum(jnp.where(keep, inner, 0.0), axis=-1, keepdims=True)
            probs = e_ref[0, head].astype(f32) * coef_ref[0, :, head : head + 1]
            grad_probs = nt(a2 * masks[side], v2)
            grad_scores = (probs * (grad_probs - delta)).astype(bf16)
            dq_two.append(nn(grad_scores, k2))
            dk_two.append(tn(grad_scores, q2))
            dv_two.append(tn(probs.astype(bf16), a2))
        dcq_ref[0, :, lanes] = (jnp.where(first_q, dq_two[0], dq_two[1]) * scaling).astype(bf16)
        dckv_ref[0, :, lanes] = (jnp.where(first_k, dk_two[0], dk_two[1]) * scaling).astype(bf16)
        dckv_ref[0, :, upper] = jnp.where(first_k, dv_two[0], dv_two[1]).astype(bf16)
    part_ref[0] = (before_ref[0] + nt(dckv_ref[0], w_pair[...])).astype(bf16)


def first_backward(n, *refs):
    order_r, ds_ref, da_ref, db_ref, first_ref, gain_ref = refs[:6]
    source, refs = refs[6 : 6 + n[0][0]], refs[6 + n[0][0] :]
    df_ref, low_ref, do_ref, dg_ref, w_out, sem = refs

    @pl.when(pl.program_id(0) == 0)
    def _():
        fetch_rows(w_out, source, n[0], order_r, OUT_AT, 0, sem)
        dg_ref[...] = jnp.zeros_like(dg_ref)
        end_fetch(w_out, sem)

    grad = da_ref[0].astype(f32) + db_ref[0].astype(f32)
    unit, inv = norm_parts(first_ref[0])
    dg_ref[0:1] += jnp.sum(grad * unit, axis=0, keepdims=True)
    grad_first = ds_ref[0].astype(f32) + norm_back(unit, inv, gain_ref[1:2], grad)
    df_ref[0] = grad_first
    low = grad_first.astype(bf16)
    low_ref[0] = low
    do_ref[0] = nt(low, w_out[...]).astype(bf16)


def attn_backward(n, *refs):
    order_c, do_ref, qkv_ref, p_ref = refs[:4]
    unit, refs = refs[4 : 4 + n[0][0]], refs[4 + n[0][0] :]
    dqkv_ref, part_ref, w_in, wide, sem = refs
    tokens = do_ref.shape[1]
    own = dqkv_ref.shape[1]
    lo = (tokens - own) // 2

    @pl.when(pl.program_id(0) == 0)
    def _():
        fetch_columns(w_in, unit, n[0], order_c, 128, sem)
        end_fetch(w_in, sem)

    first_half = lane_halves(CELLS)
    masks = half_masks()
    for block in range(tokens // CELLS):
        rows = slice(block * CELLS, (block + 1) * CELLS)
        for pair in range(PAIRS):
            lanes = slice(pair * 128, pair * 128 + 128)
            q2 = qkv_ref[0, rows, lanes]
            k2 = qkv_ref[0, rows, HALF + pair * 128 : HALF + pair * 128 + 128]
            v2 = qkv_ref[0, rows, 2 * HALF + pair * 128 : 2 * HALF + pair * 128 + 128]
            g2 = do_ref[0, rows, lanes]
            dq_two, dk_two, dv_two = [], [], []
            for side in range(2):
                probs = p_ref[0, block * HH + pair * 2 + side]
                wide_probs = probs.astype(f32)
                grad_probs = nt(g2 * masks[side], v2)
                delta = jnp.sum(wide_probs * grad_probs, axis=-1, keepdims=True)
                grad_scores = (wide_probs * (grad_probs - delta)).astype(bf16)
                dq_two.append(nn(grad_scores, k2))
                dk_two.append(tn(grad_scores, q2))
                dv_two.append(tn(probs, g2))
            wide[rows, lanes] = jnp.where(first_half, dq_two[0], dq_two[1]) * scaling
            wide[rows, HALF + pair * 128 : HALF + pair * 128 + 128] = (
                jnp.where(first_half, dk_two[0], dk_two[1]) * scaling
            )
            wide[rows, 2 * HALF + pair * 128 : 2 * HALF + pair * 128 + 128] = jnp.where(
                first_half, dv_two[0], dv_two[1]
            )
    low = wide[lo : lo + own].astype(bf16)
    dqkv_ref[0] = low
    part_ref[0] = nt(low, w_in[...]).astype(bf16)


def input_backward(x_ref, df_ref, da_ref, db_ref, gain_ref, dx_ref, dg_ref):
    @pl.when(pl.program_id(0) == 0)
    def _():
        dg_ref[...] = jnp.zeros_like(dg_ref)

    grad = da_ref[0].astype(f32) + db_ref[0].astype(f32)
    unit, inv = norm_parts(x_ref[0].astype(f32))
    dg_ref[0:1] += jnp.sum(grad * unit, axis=0, keepdims=True)
    dx_ref[0] = (df_ref[0] + norm_back(unit, inv, gain_ref[0:1], grad)).astype(bf16)


def query_back_one(n, *refs):
    order_c, one_ref, two_ref = refs[:3]
    unit, refs = refs[3 : 3 + n[0][0]], refs[3 + n[0][0] :]
    dcq_ref, part_ref, w_q, sem = refs
    fetch_columns(w_q, unit, n[0], order_c, CQ_AT, sem)
    end_fetch(w_q, sem)
    for m in range(dcq_ref.shape[0]):
        low = (one_ref[m].astype(f32) + two_ref[m].astype(f32)).astype(bf16)
        dcq_ref[m] = low
        part_ref[m] = nt(low, w_q[...]).astype(bf16)


def query_back_two(q_ref, dq_ref, da_ref, db_ref, gain_ref, out_ref, dg_ref):
    total = jnp.zeros((1, D), f32)
    for m in range(q_ref.shape[0]):
        grad = da_ref[m].astype(f32) + db_ref[m].astype(f32)
        unit, inv = norm_parts(q_ref[m].astype(f32))
        total = total + jnp.sum(grad * unit, axis=0, keepdims=True)
        out_ref[m] = (dq_ref[m].astype(f32) + norm_back(unit, inv, gain_ref[2:3], grad)).astype(bf16)
    dg_ref[...] = jnp.broadcast_to(total, dg_ref.shape)


def weight_grads(n, plan, *refs):
    order_c, order_r = refs[:2]
    count = 1 + max(max(item[0], item[1]) for item in plan)
    sides, refs = refs[2 : 2 + count], refs[2 + count :]
    outs = []
    for k in n:
        outs.append(refs[:k])
        refs = refs[k:]
    acc = refs[0]
    for left, right, unit, by_rows, col0, row0 in plan:
        height, width = sides[left].shape[1], sides[right].shape[1]
        if left == right:
            turned = jnp.concatenate([sides[left][...], jnp.zeros((120, height), f32)], axis=0).T
            acc[0:height, 0:128] = turned
            spread_columns(acc.at[:, 0:128], outs[unit], order_c, col0)
            continue
        for at in range(0, width, HALF):
            acc[0:height] = tn(sides[left][...], sides[right][:, at : at + HALF])
            if by_rows:
                spread_rows(acc, outs[unit], order_r, height, at // HALF, col0, row0)
            else:
                spread_columns(acc, outs[unit], order_c, col0 + at)


def per_device(
    patches,
    queries,
    page_rows,
    window_mask,
    query_lengths,
    plan,
    norm_attn,
    norm_mlp,
    norm_query,
    attn_input,
    attn_output,
    mlp_up,
    mlp_down,
    cross_query,
    cross_pair,
    cross_output,
    patch_cotangent,
    query_cotangent,
):
    core = lax.axis_index("section")
    zi = lax.axis_index("dp")
    qi = lax.axis_index("seq")
    nz, ns = lax.axis_size("dp"), lax.axis_size("seq")
    rows = attn_input.shape[1]
    hid = mlp_up.shape[2] // 2
    manual = rows % 16 == 0 and ns == 4 and nz & (nz - 1) == 0
    near = nz // 2
    batches, row_count, col_count = patches.shape[:3]
    tokens = row_count * col_count
    core_zero = core == 0

    def swap(x):
        return lax.ppermute(x, "section", SWAP)

    def across(x, r):
        return lax.ppermute(x, "seq", [(j, j ^ r) for j in range(ns)])

    def tied(x, after):
        return x if after is None else lax.optimization_barrier((x, after))[0]

    far = (zi // near) ^ core
    if manual:
        order_c = [((zi ^ r) * ns + (qi ^ p)) for p in range(ns) for r in range(nz)]
        order_r = [
            ((zi ^ (far * near + k)) - core * near) * ns + (qi ^ p)
            for p in range(ns)
            for k in range(near)
        ]
    else:
        order_c = order_r = [zi]
    order_s = [qi ^ p for p in range(ns)]
    order_c, order_r, order_s = (
        jnp.stack(o).astype(jnp.int32) for o in (order_c, order_r, order_s)
    )

    gain_block = jnp.stack([norm_attn[0], norm_mlp[0], norm_query[0]], axis=1)
    gain_block = jnp.pad(gain_block, ((0, 0), (0, 125)))
    win, up, cq, cp = attn_input[0], mlp_up[0], cross_query[0], cross_pair[0]

    def half_columns(side):
        def half(a, w):
            return a[:, side * w : (side + 1) * w]

        first = [half(win[:, k * D : (k + 1) * D], HALF) for k in range(3)]
        return [
            jnp.concatenate([gain_block] + first + [half(cq, HALF)], axis=1),
            jnp.concatenate([half(up, hid), half(cp[:, :D], HALF), half(cp[:, D:], HALF)], axis=1),
        ]

    halves = [half_columns(side) for side in range(2)]

    def fold(w):
        return jnp.stack(
            [
                jnp.concatenate(
                    [
                        w[b * rows : (b + 1) * rows, side * HALF : (side + 1) * HALF]
                        for b in range(w.shape[0] // rows)
                    ],
                    axis=1,
                )
                for side in range(2)
            ]
        )

    down_co = jnp.concatenate([mlp_down[0], cross_output[0]], axis=0)

    def z_pairs(bit):
        return [
            (c * nz + j, c * nz + (j ^ bit))
            for c in range(2)
            for j in range(c * near, (c + 1) * near)
        ]

    def z_step(parts, bit, after):
        out = []
        for stack, by_rows in parts:
            stack = tied(stack, after)
            if not by_rows:
                got = lax.ppermute(stack, "dp", [(j, j ^ bit) for j in range(nz)])
                out.append((jnp.concatenate([stack, got]), False, got))
                continue
            got = lax.ppermute(stack, ("section", "dp"), z_pairs(bit))
            if bit < near:
                stack = jnp.concatenate([stack, got])
            else:
                stack = jnp.where(far == 0, stack, got)
                stack = stack.reshape((nz,) + stack.shape[2:])
            out.append((stack, True, got))
        return [o[:2] for o in out], tuple(o[2] for o in out)

    units = [[None] * 3 for _ in range(2)]
    counts = [[None] * 3 for _ in range(2)]
    if manual:
        col_send = [jnp.where(core_zero, b, a) for a, b in zip(*halves)]
        col_mine = [jnp.where(core_zero, a, b) for a, b in zip(*halves)]
        row_mine = [fold(attn_output[0]), fold(down_co)]
        col_recv = [swap(col_send[0])]
        row_recv = [swap(row_mine[0])]
        col_recv.append(swap(tied(col_send[1], (col_recv[0], row_recv[0]))))
        row_recv.append(swap(tied(row_mine[1], (col_recv[0], row_recv[0]))))

        queue = []
        for layer in range(2):
            own_layer = core == layer
            cols = [jnp.where(own_layer, a, b)[None] for a, b in zip(col_mine, col_recv)]
            folded = [jnp.where(own_layer, a, b)[None] for a, b in zip(row_mine, row_recv)]
            queue += [[(cols[0], False), (folded[0], True)], [(cols[1], False)], [(folded[1], True)]]
        bits = []
        while 2 ** len(bits) < nz:
            bits.append(2 ** len(bits))
        last_rows = queue.pop()[0][0][0]
        count = len(queue)

        def early_steps(k, after):
            tokens_of = ()
            for bit in bits[:-1]:
                queue[k], after = z_step(queue[k], bit, after)
                tokens_of += after
            return tokens_of

        lead = early_steps(0, None)
        queue[0], _ = z_step(queue[0], bits[-1], lead)
        ahead = early_steps(1, lead)
        token = ()
        messages = []
        from_x = from_y = jnp.zeros((nz, rows, 0), bf16)
        cut = 0
        before = None
        for k in range(count + 1):
            low, high = from_x[..., :cut], from_y[..., cut:]
            x_parts, y_parts = [high], [low]
            own = None
            if k < count:
                parts = [stack for stack, _ in queue[k]]
                own = parts[0] if len(parts) == 1 else jnp.concatenate(parts, axis=2)
                own = tied(own, token)
                x_parts.append(own)
                y_parts.append(own)
            sent_x, sent_y = jnp.concatenate(x_parts, axis=2), jnp.concatenate(y_parts, axis=2)
            messages.append((sent_x, sent_y))
            got_x, got_y = across(sent_x, 1), across(sent_y, 2)
            if k + 1 < count:
                queue[k + 1], got = z_step(queue[k + 1], bits[-1], (token, ahead))
                ahead = early_steps(k + 2, got) if k + 2 < count else got
            if before is not None:
                b = k - 1
                units[b // 3][b % 3] = before[0] + [got_y, got_x]
                counts[b // 3][b % 3] = (5,) + before[1] + (cut,)
            if own is None:
                break
            before = ([own, got_x, got_y], (high.shape[2], low.shape[2]))
            from_x, from_y = got_x[..., high.shape[2] :], got_y[..., low.shape[2] :]
            cut = own.shape[2] // 256 * 128
            token = (got_x, got_y)
        stack = jnp.stack([last_rows] + [across(last_rows, r) for r in range(1, ns)])[None]
        stack = tied(stack, ahead)
        for bit in bits:
            got = lax.ppermute(stack, ("section", "dp"), z_pairs(bit))
            stack = jnp.concatenate([stack, got]) if bit < near else jnp.where(far == 0, stack, got)
        units[1][2] = [stack]
        counts[1][2] = (1, 0, 0, 0)
        counts = tuple(tuple(c) for c in counts)
    else:

        def gather_all(x):
            return lax.all_gather(
                lax.all_gather(x, ("dp", "seq"), axis=0, tiled=True), "section", axis=0
            )

        whole_cols = [[gather_all(h[k]) for h in halves] for k in range(2)]
        whole_rows = [gather_all(x) for x in (attn_output[0], mlp_down[0], cross_output[0])]
        for layer in range(2):
            cols = [jnp.where(core_zero, a[layer], b[layer]) for a, b in whole_cols]
            mine = [
                lax.dynamic_slice_in_dim(w[layer], core * (w.shape[1] // 2), w.shape[1] // 2, 0)
                for w in whole_rows
            ]
            units[layer] = [[cols[0], mine[0]], [cols[1]], [jnp.concatenate(mine[1:], axis=0)]]
        counts = (((2, 0, 0, 0), (1, 0, 0, 0), (1, 0, 0, 0)),) * 2
        messages = [()] * 7

    order = jnp.arange(batches)
    inverse = jnp.sum(jnp.where(plan[0][None, :] == order[:, None], order[None, :], 0), axis=1)
    query_start = jnp.take(queries, inverse, axis=0)
    query_given = jnp.take(query_cotangent, inverse, axis=0)
    lengths = jnp.take(query_lengths, inverse)
    live = (jnp.arange(NQ)[None, :] < lengths[:, None]).astype(f32)[:, :, None]
    window_rows = qi * (row_count // WIN) + jnp.arange(row_count // WIN)
    marks = (window_rows[None, :, None] < page_rows[:, None, None]) & (window_mask == 1)
    valid = jnp.repeat(jnp.repeat(marks, WIN, axis=1), WIN, axis=2)
    valid = valid.reshape(batches, 1, tokens).astype(f32)
    blocks_wide = (row_count + WIN) // WIN
    cell = jnp.arange(CELLS)
    frame_row = qi * row_count - WIN // 2 + jnp.arange(blocks_wide)[:, None] * WIN + cell // WIN
    inside = (frame_row >= 0) & (frame_row < row_count * ns)
    side_of = (cell % WIN) < WIN // 2
    same = side_of[:, None] == side_of[None, :]
    mask = jnp.where(inside[:, None, :] & same[None], 0.0, hidden_value).astype(f32)

    pages = patches.reshape(batches, tokens, D)
    given = patch_cotangent.reshape(batches, tokens, D)

    def widened(edge_source):
        top = lax.ppermute(
            edge_source[:, tokens - RIM :], "seq", [(j, j + 1) for j in range(ns - 1)]
        )
        bottom = lax.ppermute(edge_source[:, :RIM], "seq", [(j + 1, j) for j in range(ns - 1)])
        return jnp.concatenate([top, edge_source, bottom], axis=1)

    def pieces(unit):
        return [(piece, ANY) for piece in unit]

    def shaped(shape, dtype, batched=True):
        return (shape, dtype, per_batch(shape) if batched else whole(shape))

    def batched(a):
        return (a, per_batch(a.shape))

    def full(a):
        return (a, whole(a.shape))

    dma = pltpu.SemaphoreType.DMA

    def forward(layer, x, query, query_parts):
        u, n = units[layer], counts[layer]
        shifted = layer == 1
        wide_x = wide_x1 if shifted else x
        wide = wide_x.shape[1]
        blocks = wide // CELLS
        wide_x = tied(wide_x, messages[2 + 3 * layer])
        ins = [(order_c, SMEM), (order_r, SMEM), batched(wide_x)]
        if shifted:
            ins.append(full(mask))
        h1, qkv, probs, mixed, part, gains = run(
            partial(attn_forward, n, shifted),
            "attn_forward",
            (batches,),
            ins + pieces(u[0]),
            [
                shaped((batches, tokens, D), bf16),
                shaped((batches, wide, 3 * HALF), bf16),
                shaped((batches, blocks * HH, CELLS, CELLS), bf16),
                shaped((batches, tokens, HALF), bf16),
                shaped((batches, tokens, D), bf16),
                shaped((8, D), f32, False),
            ],
            [
                pltpu.VMEM((D, 128 + 3 * HALF), bf16),
                pltpu.VMEM((HALF, D), bf16),
                pltpu.VMEM((wide, HALF), f32),
                pltpu.VMEM((wide, D), f32),
                dma,
                dma,
            ],
            10,
        )
        other = swap(part)
        if query_parts is not None:
            query_parts = query_parts(wide_x, part)
        q_ins = [(order_c, SMEM), full(query), full(gains)]
        q_outs = [
            shaped((batches, NQ, D), bf16, False),
            shaped((batches, NQ, HALF), bf16, False),
        ]
        if query_parts is not None:
            q_ins += [full(query_parts[0]), full(query_parts[1]), full(live)]
            q_outs = [shaped((batches, NQ, D), bf16, False)] + q_outs
        got = run(
            partial(query_in, n, query_parts is not None),
            "query_in",
            (),
            q_ins + pieces(u[0]),
            q_outs,
            [pltpu.VMEM((D, HALF), bf16), dma],
            2.5,
        )
        if query_parts is not None:
            query, got = got[0], got[1:]
        hq, cq_now = got
        first, h2, slope, act, second_part, ckv, e, o = run(
            partial(mlp_forward, n),
            "mlp_forward",
            (batches,),
            [
                (order_c, SMEM),
                (order_r, SMEM),
                batched(tied(x, messages[min(4 + 2 * layer, len(messages) - 1)])),
                batched(part),
                batched(other),
                full(gains),
                batched(cq_now),
                batched(valid),
            ]
            + pieces(u[1])
            + pieces(u[2]),
            [
                shaped((batches, tokens, D), f32),
                shaped((batches, tokens, D), bf16),
                shaped((batches, tokens, hid), bf16),
                shaped((batches, tokens, hid), bf16),
                shaped((batches, tokens, D), bf16),
                shaped((batches, tokens, D), bf16),
                shaped((batches, HH, NQ, tokens), bf16),
                shaped((batches, NQ, HALF + 128), bf16),
            ],
            [pltpu.VMEM((D, hid + D), bf16), pltpu.VMEM((hid, D), bf16), dma, dma],
            14,
        )
        second_other = swap(second_part)
        x_next = (first + (second_part.astype(f32) + second_other.astype(f32))).astype(bf16)
        kept = dict(
            x=x, query=query, h1=h1, qkv=qkv, probs=probs, mixed=mixed, gains=gains, hq=hq,
            cq=cq_now, first=first, h2=h2, slope=slope, act=act, ckv=ckv, e=e,
        )

        def query_rest(start, finish):
            sent = tied(o, start)
            os = [sent] + [across(sent, r) for r in range(1, ns)]
            os[1:] = tied(os[1:], finish)
            att, att_low, coef, q_part = run(
                partial(query_out, n, ns),
                "query_out",
                (),
                [(order_r, SMEM), (order_s, SMEM)]
                + [full(a) for a in os]
                + pieces(u[2]),
                [
                    shaped((batches, NQ, HALF), f32, False),
                    shaped((batches, NQ, HALF), bf16, False),
                    shaped((batches, NQ, 128), f32, False),
                    shaped((batches, NQ, D), bf16, False),
                ],
                [
                    pltpu.VMEM((HALF, D), bf16),
                    pltpu.VMEM((ns, batches, NQ, HALF + 128), bf16),
                    dma,
                ],
                4.5,
            )
            kept.update(att=att, att_low=att_low, coef=coef)
            return q_part, swap(q_part)

        return x_next, query_rest, kept

    def sums(kernel_plan, sides, shapes, height, name, after=None):
        flat = run(
            partial(weight_grads, tuple(len(unit) for unit in shapes), kernel_plan),
            name,
            (),
            [(order_c, SMEM), (order_r, SMEM)] + [full(s) for s in sides],
            [shaped(shape, bf16, False) for unit in shapes for shape in unit],
            [pltpu.VMEM((height, HALF), f32)],
            12 if height > D else 6,
        )
        out = []
        for unit in shapes:
            out.append(flat[: len(unit)])
            flat = flat[len(unit) :]
        return out

    def unit_shapes(cols, row_height):
        if not manual:
            shapes = [(D, cols)] if cols else []
            return shapes + ([(row_height, D)] if row_height else [])
        width = cols + row_height // (rows * nz * ns // 2) * HALF
        return [(nz, rows, width)] * 3 + [(near, rows, width)] * 2

    operands = {}

    def reduce_one(unit, after):
        own, one, two, low, high = unit
        low, high = tied((low, high), after)
        low, high = across(low, 2), across(high, 1)
        return (own, one, two, low, high), (low, high)

    def reduce_two(unit, after):
        own, one, two, low, high = tied(unit, after)
        one = jnp.concatenate([one[:near] + low, one[near:]])
        two = jnp.concatenate([two[:near], two[near:] + high])
        operands[2] = (one, two)
        one, two = across(one, 1), across(two, 2)
        return (own, one, two), (one, two)

    def reduce_three(unit, cols, after):
        own, one, two = tied(unit, after)
        total = own.astype(f32) + one.astype(f32) + two.astype(f32)
        col, row = total[..., :cols], total[..., cols:]
        sent = col[near:].astype(bf16)
        operands[3] = sent
        got_col = lax.ppermute(sent, "dp", [(j, j ^ near) for j in range(nz)])
        sent = row.astype(bf16)
        got_row = lax.ppermute(sent, ("section", "dp"), [(b, a) for a, b in z_pairs(near)])
        return [(col[:near], got_col), (row, got_row)], (got_col, got_row)

    def reduce_four(parts, after):
        out = []
        token = ()
        for by_rows, (total, got) in enumerate(tied(parts, after)):
            total = total + got.astype(f32)
            if by_rows:
                total = total.reshape((near, 2) + total.shape[1:])
            bit = near // 2
            while bit:
                sent = total[bit:].astype(bf16)
                pairs = [(b, a) for a, b in z_pairs(bit)] if by_rows else [
                    (j, j ^ bit) for j in range(nz)
                ]
                got = lax.ppermute(sent, ("section", "dp") if by_rows else "dp", pairs)
                token += (got,)
                total = total[:bit] + got.astype(f32)
                bit //= 2
            out.append(total[0])
        return out, token

    def unfold(row):
        blocks = row.shape[2] // HALF
        return jnp.concatenate(
            [
                jnp.concatenate([row[side, :, b * HALF : (b + 1) * HALF] for side in range(2)], axis=1)
                for b in range(blocks)
            ],
            axis=0,
        )

    def reduce_plain(unit, cols, heights):
        out = []
        if cols:
            out.append(lax.psum_scatter(unit[0], ("dp", "seq"), scatter_dimension=0, tiled=True))
        if len(unit) > 1 or not cols:
            cut = heights[0] * nz * ns // 2
            pieces_of = [unit[-1][:cut], unit[-1][cut:]]
            out += [
                lax.psum_scatter(
                    lax.all_gather(piece, "section", axis=0, tiled=True),
                    ("dp", "seq"),
                    scatter_dimension=0,
                    tiled=True,
                )
                for piece in pieces_of
            ]
        return [o.astype(f32) for o in out]

    share = 1.0 / ns

    def mlp_gradient(layer, grad_patch, slope):
        u, n = units[layer], counts[layer]
        return run(
            partial(mlp_backward, n),
            "mlp_backward",
            (batches,),
            [(order_c, SMEM), (order_r, SMEM), batched(grad_patch), batched(slope)]
            + pieces(u[1])
            + pieces(u[2]),
            [shaped((batches, tokens, hid), bf16), shaped((batches, tokens, D), f32)],
            [pltpu.VMEM((D, hid), bf16), pltpu.VMEM((hid, D), bf16), dma, dma],
            9,
        )

    def backward(layer, grad_patch, grad_query, kept, emit, mlp_part):
        u, n = units[layer], counts[layer]
        shifted = layer == 1
        gains = kept["gains"]
        du, before = mlp_part
        dckv, dcq_part, part, dcross = run(
            partial(cross_backward, n, hid),
            "cross_backward",
            (batches,),
            [(order_c, SMEM), (order_r, SMEM)]
            + [
                batched(a)
                for a in (
                    before, kept["e"], kept["coef"], grad_query, live, kept["att"], kept["cq"],
                    kept["ckv"],
                )
            ]
            + pieces(u[1])
            + pieces(u[2]),
            [
                shaped((batches, tokens, D), bf16),
                shaped((batches, NQ, HALF), bf16),
                shaped((batches, tokens, D), bf16),
                shaped((batches, NQ, D), bf16),
            ],
            [pltpu.VMEM((D, D), bf16), pltpu.VMEM((HALF, D), bf16), dma, dma],
            6,
        )
        emit("mlp", part)
        other = swap(part)
        dcq_got = across(dcq_part, 1)

        def flat(a):
            return a.reshape(-1, a.shape[-1])

        row_at = hid + D if manual else 0
        row_base = hid // (nz * ns // 2) // rows * HALF if manual else 0
        early = sums(
            (
                (0, 1, 0, False, 0, 0),
                (0, 2, 0, False, hid, 0),
                (3, 4, 0, True, row_at, 0),
                (5, 6, 0, True, row_at + row_base, hid),
            ),
            [
                flat(kept["h2"]), flat(du), flat(dckv), flat(kept["act"]), flat(grad_patch),
                flat(kept["att_low"]), flat(dcross * jnp.asarray(share, bf16)),
            ],
            [unit_shapes(hid + D, hid + HALF)],
            hid,
            "early_grads",
        )
        part = tied(part, early[0][0])
        def dcq_steps(part_of, got, after):
            bit = 2
            while bit < ns:
                got = tied(got, after)
                part_of = (part_of.astype(f32) + got.astype(f32)).astype(bf16)
                got = across(part_of, bit)
                bit *= 2
            return part_of, got

        if shifted:
            dcq_part, dcq_got = dcq_steps(dcq_part, dcq_got, early[0][0])
        emit("early", (early[0], dcq_part if shifted else early[0][0]))
        if not shifted:
            part = tied(part, operands.get(3, ()))
        grad_first, first_low, grad_mixed, dg_mlp = run(
            partial(first_backward, n),
            "first_backward",
            (batches,),
            [(order_r, SMEM)]
            + [batched(a) for a in (grad_patch, part, other, kept["first"])]
            + [full(gains)]
            + pieces(u[0]),
            [
                shaped((batches, tokens, D), f32),
                shaped((batches, tokens, D), bf16),
                shaped((batches, tokens, HALF), bf16),
                shaped((8, D), f32, False),
            ],
            [pltpu.VMEM((HALF, D), bf16), dma],
            5.6,
        )
        wide_grad = widened(grad_mixed) if shifted else grad_mixed
        emit("first", grad_mixed)
        wide = wide_grad.shape[1]
        dqkv, part = run(
            partial(attn_backward, n),
            "attn_backward",
            (batches,),
            [(order_c, SMEM)]
            + [batched(a) for a in (wide_grad, kept["qkv"], kept["probs"])]
            + pieces(u[0]),
            [shaped((batches, tokens, 3 * HALF), bf16), shaped((batches, tokens, D), bf16)],
            [pltpu.VMEM((D, 3 * HALF), bf16), pltpu.VMEM((wide, 3 * HALF), f32), dma],
            15,
        )
        emit("attn", part)
        other = swap(part)
        if not shifted:
            dcq_part, dcq_got = dcq_steps(dcq_part, dcq_got, dqkv)
            emit("dcq", dcq_part)
            dcq_got = tied(dcq_got, operands.get(2, ()))
        dcq_got = tied(dcq_got, dqkv)
        dcq, q_part = run(
            partial(query_back_one, n),
            "query_back_one",
            (),
            [(order_c, SMEM), full(dcq_part), full(dcq_got)] + pieces(u[0]),
            [shaped((batches, NQ, HALF), bf16, False), shaped((batches, NQ, D), bf16, False)],
            [pltpu.VMEM((D, HALF), bf16), dma],
            2.5,
        )
        q_other = swap(q_part)
        last_x = kept["x"]
        dx, dg_attn = run(
            input_backward,
            "input_backward",
            (batches,),
            [batched(a) for a in (last_x, grad_first, part, other)] + [full(gains)],
            [shaped((batches, tokens, D), bf16), shaped((8, D), f32, False)],
            [],
            3,
        )
        dq, dg_query = run(
            query_back_two,
            "query_back_two",
            (),
            [full(a) for a in (kept["query"], grad_query, q_part, q_other, gains)],
            [shaped((batches, NQ, D), bf16, False), shaped((8, D), f32, False)],
            [],
            1,
        )
        dgains = jnp.concatenate([dg_attn[0:1], dg_mlp[0:1], dg_query[0:1] * share], axis=0)
        emit(
            "late",
            ([
                flat(kept["h1"]), flat(dqkv), flat(kept["hq"]), flat(dcq * jnp.asarray(share, bf16)),
                flat(kept["mixed"]), flat(first_low),
            ], dgains),
        )
        return dx, dq

    x1, q_parts, kept0 = forward(0, pages, query_start, None)
    wide_x1 = widened(x1)
    x2, q_rest, kept1 = forward(1, x1, query_start, q_parts)
    mlp_part = mlp_gradient(1, given, kept1["slope"])
    q_parts_two = q_rest((), mlp_part[0])
    query_last = (
        kept1["query"].astype(f32)
        + live * (q_parts_two[0].astype(f32) + q_parts_two[1].astype(f32))
    ).astype(bf16)

    widths = (hid + D, hid + D, 8 * HALF + 128)
    out_rows = attn_output.shape[1]
    heights = [(mlp_down.shape[1], cross_output.shape[1])] * 2 + [(out_rows, out_rows)]
    state = [None] * 3
    late_sides = []

    rounds = [()]

    def one_round(*items, after=()):
        for unit, step in items:
            now = state[unit]
            if not manual:
                if step == 4:
                    now = reduce_plain(now, widths[unit], heights[unit])
            elif step == 1:
                now, got = reduce_one(now, after)
            elif step == 2:
                now, got = reduce_two(now, after)
            elif step == 3:
                now, got = reduce_three(now, widths[unit], after)
            else:
                now, got = reduce_four(now, after)
                rows_of = unfold(now[1])
                cut = heights[unit][0]
                now = [now[0], rows_of[:cut], rows_of[cut:]]
            state[unit] = now
            rounds[unit, step] = got if manual else ()

    rounds = {}

    def emit_late_layer(what, value):
        if what == "early":
            state[1] = value[0]
            one_round((1, 1), after=value[1])
        elif what == "attn":
            one_round((1, 2), after=value)
        elif what == "late":
            late_sides.extend(value)

    def emit_first_layer(what, value):
        if what == "early":
            state[0] = value[0]
            one_round((0, 1), after=value[1])
            one_round((1, 3), after=value[1])
        elif what == "dcq":
            one_round((0, 2), after=value)
        elif what == "late":
            sides = late_sides[0] + value[0]
            gain_sums = jnp.concatenate(
                [value[1], late_sides[1], jnp.zeros((2, D), f32)], axis=0
            )
            row_at = 8 * HALF + 128
            (state[2],) = sums(
                [
                    item
                    for k in range(2)
                    for item in (
                        (6 * k, 6 * k + 1, 0, False, 4 * HALF * k, 0),
                        (6 * k + 2, 6 * k + 3, 0, False, 4 * HALF * k + 3 * HALF, 0),
                        (6 * k + 4, 6 * k + 5, 0, True, row_at + HALF * k, HALF * k),
                    )
                ]
                + [(12, 12, 0, False, 8 * HALF, 0)],
                sides + [gain_sums],
                [unit_shapes(8 * HALF + 128, 2 * HALF)],
                D,
                "late_grads",
            )
            one_round((2, 1))

    query_given = tied(query_given, x2)
    kept1["h2"] = tied(kept1["h2"], query_last)
    dx1, dq1 = backward(1, given, query_given, kept1, emit_late_layer, mlp_part)
    dx0, dq0 = backward(
        0, dx1, dq1, kept0, emit_first_layer, mlp_gradient(0, dx1, kept0["slope"])
    )
    one_round((1, 4), after=state[2][0])
    one_round((0, 3), after=(state[2][0], rounds[1, 3]))
    one_round((2, 2), after=(rounds[0, 2], operands.get(3, ())))
    one_round((2, 3), after=rounds[0, 3])
    one_round((0, 4), after=rounds[2, 2])

    def handed(low, high):
        return [swap(jnp.where(core_zero, b, a)) for a, b in zip(low, high)]

    got_early = handed(
        [state[0][0], jnp.concatenate(state[0][1:], axis=0)],
        [state[1][0], jnp.concatenate(state[1][1:], axis=0)],
    )
    one_round((2, 4), after=(rounds[0, 4], got_early))
    cols, rows_of = state[2][0], state[2][1:]
    low_cols, high_cols = cols[:, : 4 * HALF], cols[:, 4 * HALF : 8 * HALF]
    got_late = handed([high_cols, rows_of[1]], [low_cols, rows_of[0]])
    own_early = [jnp.where(core_zero, a, b) for a, b in zip(state[0], state[1])]
    own_late = [jnp.where(core_zero, high_cols, low_cols)]
    own_late.append(jnp.where(core_zero, rows_of[1], rows_of[0]))
    cut = heights[0][0]
    mine = own_early + own_late
    theirs = [got_early[0], got_early[1][:cut], got_early[1][cut:]] + got_late

    def col_halves(k):
        low = jnp.where(core_zero, mine[k], theirs[k])
        high = jnp.where(core_zero, theirs[k], mine[k])
        return low, high

    holder = zi // near if manual else core

    def row_block(k):
        return jnp.where(holder == core, mine[k], theirs[k])

    low, high = col_halves(0)
    grad_up = jnp.concatenate([low[:, :hid], high[:, :hid]], axis=1)
    grad_pair = jnp.concatenate(
        [
            low[:, hid : hid + HALF], high[:, hid : hid + HALF],
            low[:, hid + HALF :], high[:, hid + HALF :],
        ],
        axis=1,
    )
    low, high = col_halves(3)
    grad_in = jnp.concatenate(
        [side[:, k * HALF : (k + 1) * HALF] for k in range(3) for side in (low, high)], axis=1
    )
    grad_cq = jnp.concatenate([low[:, 3 * HALF :], high[:, 3 * HALF :]], axis=1)
    grad_down, grad_co, grad_out = row_block(1), row_block(2), row_block(4)

    gain_rows = jnp.where(core_zero, cols[:, 8 * HALF : 8 * HALF + 3], cols[:, 8 * HALF + 3 : 8 * HALF + 6])
    own_gains = gain_rows.T

    patch_ends = jnp.where(core_zero, dx0, x2).reshape(1, batches, row_count, col_count, D)
    query_ends = jnp.take(jnp.where(core_zero, dq0, query_last), plan[0], axis=0)[None]
    return (
        patch_ends,
        query_ends,
        own_gains[0:1],
        own_gains[1:2],
        own_gains[2:3],
        grad_in[None],
        grad_out[None],
        grad_up[None],
        grad_down[None],
        grad_cq[None],
        grad_pair[None],
        grad_co[None],
    )


def solution(mesh):
    return jax.shard_map(
        per_device,
        mesh=mesh,
        in_specs=(
            P("dp", "seq", None, None),
            P("dp", None, None),
            P("dp"),
            P("dp", "seq", None),
            P("dp"),
            P("dp", None),
            P("section", ("dp", "seq")),
            P("section", ("dp", "seq")),
            P("section", ("dp", "seq")),
            P("section", ("dp", "seq"), None),
            P("section", ("dp", "seq"), None),
            P("section", ("dp", "seq"), None),
            P("section", ("dp", "seq"), None),
            P("section", ("dp", "seq"), None),
            P("section", ("dp", "seq"), None),
            P("section", ("dp", "seq"), None),
            P("dp", "seq", None, None),
            P("dp", None, None),
        ),
        out_specs=(
            P("section", "dp", "seq", None, None),
            P("section", "dp", None, None),
            P("section", ("dp", "seq")),
            P("section", ("dp", "seq")),
            P("section", ("dp", "seq")),
            P("section", ("dp", "seq"), None),
            P("section", ("dp", "seq"), None),
            P("section", ("dp", "seq"), None),
            P("section", ("dp", "seq"), None),
            P("section", ("dp", "seq"), None),
            P("section", ("dp", "seq"), None),
            P("section", ("dp", "seq"), None),
        ),
        check_vma=False,
    )
```

```python
from functools import partial
import itertools
import math

import jax
import jax.numpy as jnp
from jax import lax
from jax.experimental import pallas as pl
from jax.experimental.pallas import tpu as pltpu
from jax.sharding import PartitionSpec as P

D = 768
HEADS = 12
HDIM = 64
WIN = 12
NQ = 128
CELLS = WIN * WIN
HALF = D // 2
HH = HEADS // 2
PAIRS = HH // 2
RIM = WIN // 2 * WIN
CQ_AT = 128 + 3 * HALF
OUT_AT = CQ_AT + HALF

epsilon = 1e-05
hidden_value = -1e30
scaling = 1.0 / math.sqrt(HDIM)
bf16 = jnp.bfloat16
f32 = jnp.float32
SWAP = [(0, 1), (1, 0)]
ANY = pl.BlockSpec(memory_space=pl.ANY)
SMEM = pl.BlockSpec(memory_space=pltpu.SMEM)


def whole(shape):
    return pl.BlockSpec(shape, lambda *_: (0,) * len(shape))


def per_batch(shape):
    return pl.BlockSpec((1,) + tuple(shape[1:]), lambda m: (m,) + (0,) * (len(shape) - 1))


def run(kernel, name, grid, ins, outs, scratch, micros):
    arrays = [a for a, _ in ins]
    return pl.pallas_call(
        kernel,
        grid=grid,
        in_specs=[s for _, s in ins],
        out_specs=[s for _, _, s in outs],
        out_shape=[jax.ShapeDtypeStruct(sh, dt) for sh, dt, _ in outs],
        scratch_shapes=scratch,
        compiler_params=pltpu.CompilerParams(vmem_limit_bytes=52 * 1024 * 1024),
        cost_estimate=pl.CostEstimate(flops=int(micros * 1.15e9 * 1), bytes_accessed=0, transcendentals=0),
        name=name,
    )(*arrays)


def slots_of(pieces):
    near = pieces[3].shape[0]
    spots = [(p, k, p, k) for p in range(3) for k in range(2 * near)]
    return spots + [(3 + h, k, 3, h * near + k) for h in range(2) for k in range(near)]


def segments(unit, layout, col0, cols):
    count, off_x, off_y, cut = layout
    slots = unit[0].shape[0]
    for p, off in enumerate((0, off_x, off_y)):
        for k in range(slots):
            yield p, col0 + off, 0, cols, p, k
    for piece, low, high in ((3, 0, cut), (4, cut, col0 + cols)):
        start, end = max(low, col0), min(high, col0 + cols)
        if start < end:
            for k in range(slots):
                yield piece, start - low, start - col0, end - start, 3, k


def fetch_columns(dst, unit, layout, order, col0, sem):
    cols = dst.shape[1]
    if len(unit) < 5:
        pltpu.make_async_copy(unit[0].at[:, pl.ds(col0, cols)], dst, sem).start()
        return
    slots, rows = unit[0].shape[:2]
    for piece, come, off, width, p, k in segments(unit, layout, col0, cols):
        to = pl.multiple_of(order[p * slots + k] * rows, 16)
        pltpu.make_async_copy(
            unit[piece].at[k, :, pl.ds(come, width)], dst.at[pl.ds(to, rows), pl.ds(off, width)], sem
        ).start()


def fetch_rows(dst, unit, layout, order, col0, row0, sem):
    if len(unit) < 5:
        if len(unit[0].shape) == 5:
            slots, spots, sides, rows, _ = unit[0].shape
            each = dst.shape[0] // (slots * spots)
            for k, p, side, b in itertools.product(
                range(slots), range(spots), range(sides), range(each // rows)
            ):
                to = pl.multiple_of(order[p * slots + k] * each + b * rows, 16)
                pltpu.make_async_copy(
                    unit[0].at[k, p, side, :, pl.ds(col0 + b * HALF, HALF)],
                    dst.at[pl.ds(to, rows), pl.ds(side * HALF, HALF)],
                    sem,
                ).start()
            return
        pltpu.make_async_copy(unit[-1].at[pl.ds(row0, dst.shape[0]), :], dst, sem).start()
        return
    slots, rows = unit[0].shape[:2]
    each = dst.shape[0] // (2 * slots)
    for b in range(each // rows):
        for piece, come, off, width, p, k in segments(unit, layout, col0 + b * HALF, HALF):
            base = order[p * (slots // 2) + k // 2] * each
            to = pl.multiple_of(base + b * rows, 16)
            pltpu.make_async_copy(
                unit[piece].at[k, :, pl.ds(come, width)],
                dst.at[pl.ds(to, rows), pl.ds((k % 2) * HALF + off, width)],
                sem,
            ).start()


def end_fetch(dst, sem):
    pltpu.make_async_copy(dst, dst, sem).wait()


def spread_columns(acc, unit, order, col0):
    cols = acc.shape[1]
    if len(unit) < 5:
        unit[0][:, col0 : col0 + cols] = acc[0:D].astype(bf16)
        return
    slots, rows = unit[0].shape[:2]
    for piece, at, p, k in slots_of(unit):
        come = pl.multiple_of(order[p * slots + k] * rows, 8)
        unit[piece][at, :, col0 : col0 + cols] = acc[pl.ds(come, rows), :].astype(bf16)


def spread_rows(acc, unit, order, height, side, col0, row0):
    if len(unit) < 5:
        unit[-1][row0 : row0 + height, side * HALF : side * HALF + HALF] = acc[0:height].astype(bf16)
        return
    slots, rows = unit[0].shape[:2]
    each = height // (2 * slots)
    for piece, at, p, k in slots_of(unit):
        if k % 2 != side:
            continue
        base = order[p * (slots // 2) + k // 2] * each
        for b in range(each // rows):
            come = pl.multiple_of(base + b * rows, 8)
            unit[piece][at, :, col0 + b * HALF : col0 + b * HALF + HALF] = acc[
                pl.ds(come, rows), :
            ].astype(bf16)


def nn(a, b):
    return jnp.dot(a, b, preferred_element_type=f32)


def nt(a, b):
    return lax.dot_general(a, b, (((1,), (1,)), ((), ())), preferred_element_type=f32)


def tn(a, b):
    return lax.dot_general(a, b, (((0,), (0,)), ((), ())), preferred_element_type=f32)


def norm_parts(values):
    center = values - jnp.mean(values, axis=-1, keepdims=True)
    inv = lax.rsqrt(jnp.mean(center * center, axis=-1, keepdims=True) + epsilon)
    return center * inv, inv


def norm_back(unit, inv, gain, grad):
    scaled = grad * gain
    return inv * (
        scaled
        - jnp.mean(scaled, axis=-1, keepdims=True)
        - unit * jnp.mean(scaled * unit, axis=-1, keepdims=True)
    )


def co_at(lower):
    if len(lower[0].shape) == 5:
        return lower[0].shape[4] - HALF, 0
    if len(lower) < 5:
        return 0, lower[-1].shape[0] - HALF
    return lower[0].shape[2] - HALF, 0


def lane_halves(rows):
    lane = lax.broadcasted_iota(jnp.int32, (rows, 128), 1)
    return lane < HDIM


def half_masks():
    lane = lax.broadcasted_iota(jnp.int32, (1, 128), 1)
    low = (lane < HDIM).astype(f32)
    return low.astype(bf16), (1.0 - low).astype(bf16)


def attn_forward(n, shifted, *refs):
    order_c, order_r, x_ref = refs[:3]
    refs = refs[3:]
    if shifted:
        mask_ref, refs = refs[0], refs[1:]
    unit, refs = refs[: n[0][0]], refs[n[0][0] :]
    h_ref, qkv_ref, p_ref, o_ref, part_ref, gain_ref, w_in, w_out, mixed, hidden, sem0, sem1 = refs
    tokens = x_ref.shape[1]
    own = o_ref.shape[1]
    lo = (tokens - own) // 2

    @pl.when(pl.program_id(0) == 0)
    def _():
        fetch_columns(w_in, unit, n[0], order_c, 0, sem0)
        fetch_rows(w_out, unit, n[0], order_r, OUT_AT, 0, sem1)
        end_fetch(w_in, sem0)
        end_fetch(w_out, sem1)
        gain_ref[...] = w_in[:, :128].astype(f32).T[0:8]

    direction, _ = norm_parts(x_ref[0].astype(f32))
    hidden[...] = direction * gain_ref[0:1]
    h_ref[0] = hidden[lo : lo + own].astype(bf16)
    qkv_ref[0] = nn(hidden[...].astype(bf16), w_in[:, 128:]).astype(bf16)
    first_half = lane_halves(CELLS)
    masks = half_masks()
    for block in range(tokens // CELLS):
        rows = slice(block * CELLS, (block + 1) * CELLS)
        for pair in range(PAIRS):
            q2 = qkv_ref[0, rows, pair * 128 : pair * 128 + 128]
            k2 = qkv_ref[0, rows, HALF + pair * 128 : HALF + pair * 128 + 128]
            v2 = qkv_ref[0, rows, 2 * HALF + pair * 128 : 2 * HALF + pair * 128 + 128]
            mixed_two = []
            for side in range(2):
                scores = nt(q2 * masks[side], k2) * scaling
                if shifted:
                    scores = scores + mask_ref[block]
                weights = jnp.exp(scores - jnp.max(scores, axis=-1, keepdims=True))
                probs = (weights / jnp.sum(weights, axis=-1, keepdims=True)).astype(bf16)
                p_ref[0, block * HH + pair * 2 + side] = probs
                mixed_two.append(nn(probs, v2))
            mixed[rows, pair * 128 : pair * 128 + 128] = jnp.where(
                first_half, mixed_two[0], mixed_two[1]
            )
    out = mixed[lo : lo + own].astype(bf16)
    o_ref[0] = out
    part_ref[0] = nn(out, w_out[...]).astype(bf16)


def mlp_forward(n, *refs):
    order_c, order_r, x_ref, pa_ref, pb_ref, gain_ref, cq_ref, valid_ref = refs[:8]
    refs = refs[8:]
    upper, lower, refs = refs[: n[1][0]], refs[n[1][0] : n[1][0] + n[2][0]], refs[n[1][0] + n[2][0] :]
    first_ref, h_ref, slope_ref, act_ref, part_ref, ckv_ref, e_ref, o_ref = refs[:8]
    w_up, w_down, sem0, sem1 = refs[8:]
    hid = slope_ref.shape[2]
    tokens = x_ref.shape[1]

    @pl.when(pl.program_id(0) == 0)
    def _():
        fetch_columns(w_up, upper, n[1], order_c, 0, sem0)
        fetch_rows(w_down, lower, n[2], order_r, 0, 0, sem1)
        end_fetch(w_up, sem0)
        end_fetch(w_down, sem1)

    first = x_ref[0].astype(f32) + (pa_ref[0].astype(f32) + pb_ref[0].astype(f32))
    first_ref[0] = first
    unit, _ = norm_parts(first)
    hidden = (unit * gain_ref[1:2]).astype(bf16)
    h_ref[0] = hidden
    ckv_ref[0] = nn(hidden, w_up[:, hid:]).astype(bf16)
    step = 512
    for at in range(0, hid, step):
        lifted = nn(hidden, w_up[:, at : at + step])
        cdf = 0.5 + 0.5 * lax.erf(lifted * math.sqrt(0.5))
        act_ref[0, :, at : at + step] = (lifted * cdf).astype(bf16)
        pdf = jnp.exp(lifted * lifted * -0.5) * (1.0 / math.sqrt(2.0 * math.pi))
        slope_ref[0, :, at : at + step] = (cdf + lifted * pdf).astype(bf16)
    part_ref[0] = nn(act_ref[0], w_down[...]).astype(bf16)

    valid = jnp.broadcast_to(valid_ref[0], (NQ, tokens)) > 0.5
    first_half = lane_halves(NQ)
    masks = half_masks()
    lane = lax.broadcasted_iota(jnp.int32, (NQ, 128), 1)
    stats = jnp.zeros((NQ, 128), f32)
    for pair in range(PAIRS):
        q2 = cq_ref[0, :, pair * 128 : pair * 128 + 128]
        k2 = ckv_ref[0, :, pair * 128 : pair * 128 + 128]
        v2 = ckv_ref[0, :, HALF + pair * 128 : HALF + pair * 128 + 128]
        mixed_two = []
        for side in range(2):
            head = pair * 2 + side
            scores = jnp.where(valid, nt(q2 * masks[side], k2) * scaling, hidden_value)
            peak = jnp.max(scores, axis=-1, keepdims=True)
            weights = jnp.where(valid, jnp.exp(scores - peak), 0.0)
            total = jnp.sum(weights, axis=-1, keepdims=True)
            for at, value in ((0, peak), (16, total)):
                high = value.astype(bf16).astype(f32)
                stats = jnp.where(lane == at + head, high, stats)
                stats = jnp.where(lane == at + 8 + head, value - high, stats)
            low = weights.astype(bf16)
            e_ref[0, head] = low
            mixed_two.append(nn(low, v2))
        o_ref[0, :, pair * 128 : pair * 128 + 128] = jnp.where(
            first_half, mixed_two[0], mixed_two[1]
        ).astype(bf16)
    o_ref[0, :, HALF:] = stats.astype(bf16)


def query_in(n, has_parts, *refs):
    order_c, q_ref, gain_ref = refs[:3]
    refs = refs[3:]
    if has_parts:
        pa_ref, pb_ref, live_ref, refs = refs[0], refs[1], refs[2], refs[3:]
    unit, refs = refs[: n[0][0]], refs[n[0][0] :]
    if has_parts:
        new_ref, refs = refs[0], refs[1:]
    h_ref, cq_ref, w_q, sem = refs
    fetch_columns(w_q, unit, n[0], order_c, CQ_AT, sem)
    end_fetch(w_q, sem)
    for m in range(q_ref.shape[0]):
        query = q_ref[m].astype(f32)
        if has_parts:
            query = query + live_ref[m] * (pa_ref[m].astype(f32) + pb_ref[m].astype(f32))
            low = query.astype(bf16)
            new_ref[m] = low
            query = low.astype(f32)
        direction, _ = norm_parts(query)
        hidden = (direction * gain_ref[2:3]).astype(bf16)
        h_ref[m] = hidden
        cq_ref[m] = nn(hidden, w_q[...]).astype(bf16)


def query_out(n, ns, *refs):
    order_r, order_s = refs[:2]
    refs = refs[2:]
    os, refs = refs[:ns], refs[ns:]
    lower, refs = refs[: n[2][0]], refs[n[2][0] :]
    att_ref, low_ref, coef_ref, part_ref, w_co, o_all, sem = refs
    fetch_rows(w_co, lower, n[2], order_r, *co_at(lower), sem)
    for p in range(ns):
        o_all[order_s[p]] = os[p][...]
    first_half = lane_halves(NQ)
    end_fetch(w_co, sem)

    def stat(block, at):
        wide = block.astype(f32)
        return wide[:, at : at + 8] + wide[:, at + 8 : at + 16]

    for m in range(att_ref.shape[0]):
        stats = [o_all[s, m, :, HALF:] for s in range(ns)]
        peaks = [stat(block, 0) for block in stats]
        peak = peaks[0]
        for other in peaks[1:]:
            peak = jnp.maximum(peak, other)
        scales = [jnp.exp(p - peak) for p in peaks]
        total = scales[0] * stat(stats[0], 16)
        for scale, block in zip(scales[1:], stats[1:]):
            total = total + scale * stat(block, 16)
        inverse = 1.0 / jnp.where(total > 0.0, total, 1.0)
        coef_ref[m, :, 0:8] = jnp.exp(stat(os[0][m, :, HALF:], 0) - peak) * inverse
        factors = [scale * inverse for scale in scales]
        for pair in range(PAIRS):
            mixed = jnp.zeros((NQ, 128), f32)
            for s in range(ns):
                at = pair * 2
                factor = jnp.where(
                    first_half, factors[s][:, at : at + 1], factors[s][:, at + 1 : at + 2]
                )
                mixed = mixed + factor * o_all[s, m, :, pair * 128 : pair * 128 + 128].astype(f32)
            att_ref[m, :, pair * 128 : pair * 128 + 128] = mixed
        low = att_ref[m].astype(bf16)
        low_ref[m] = low
        part_ref[m] = nn(low, w_co[...]).astype(bf16)


def mlp_backward(n, *refs):
    order_c, order_r, ds_ref, slope_ref = refs[:4]
    refs = refs[4:]
    upper, lower, refs = refs[: n[1][0]], refs[n[1][0] : n[1][0] + n[2][0]], refs[n[1][0] + n[2][0] :]
    du_ref, part_ref, w_up, w_down, sem0, sem1 = refs
    hid = slope_ref.shape[2]

    @pl.when(pl.program_id(0) == 0)
    def _():
        fetch_rows(w_down, lower, n[2], order_r, 0, 0, sem1)
        fetch_columns(w_up, upper, n[1], order_c, 0, sem0)
        end_fetch(w_down, sem1)
        end_fetch(w_up, sem0)

    grad_second = ds_ref[0]
    step = 512
    for at in range(0, hid, step):
        grad_act = nt(grad_second, w_down[at : at + step, :])
        du_ref[0, :, at : at + step] = (
            grad_act * slope_ref[0, :, at : at + step].astype(f32)
        ).astype(bf16)
    part_ref[0] = nt(du_ref[0], w_up[...])


def cross_backward(n, hid, *refs):
    order_c, order_r, before_ref, e_ref, coef_ref, dq_ref, live_ref, att_ref, cq_ref, ckv_ref = refs[:10]
    refs = refs[10:]
    upper, lower, refs = refs[: n[1][0]], refs[n[1][0] : n[1][0] + n[2][0]], refs[n[1][0] + n[2][0] :]
    dckv_ref, dcq_ref, part_ref, dc_ref, w_pair, w_co, sem0, sem1 = refs
    tokens = before_ref.shape[1]

    @pl.when(pl.program_id(0) == 0)
    def _():
        fetch_rows(w_co, lower, n[2], order_r, *co_at(lower), sem1)
        fetch_columns(w_pair, upper, n[1], order_c, hid, sem0)
        end_fetch(w_co, sem1)
        end_fetch(w_pair, sem0)

    grad_cross = (live_ref[0] * dq_ref[0].astype(f32)).astype(bf16)
    dc_ref[0] = grad_cross
    grad_att = nt(grad_cross, w_co[...]).astype(bf16)
    first_q = lane_halves(NQ)
    first_k = lane_halves(tokens)
    masks = half_masks()
    for pair in range(PAIRS):
        lanes = slice(pair * 128, pair * 128 + 128)
        upper = slice(HALF + pair * 128, HALF + pair * 128 + 128)
        a2 = grad_att[:, lanes]
        q2 = cq_ref[0, :, lanes]
        k2 = ckv_ref[0, :, lanes]
        v2 = ckv_ref[0, :, upper]
        inner = a2.astype(f32) * att_ref[0, :, lanes]
        dq_two, dk_two, dv_two = [], [], []
        for side in range(2):
            head = pair * 2 + side
            keep = first_q if side == 0 else jnp.logical_not(first_q)
            delta = jnp.sum(jnp.where(keep, inner, 0.0), axis=-1, keepdims=True)
            probs = e_ref[0, head].astype(f32) * coef_ref[0, :, head : head + 1]
            grad_probs = nt(a2 * masks[side], v2)
            grad_scores = (probs * (grad_probs - delta)).astype(bf16)
            dq_two.append(nn(grad_scores, k2))
            dk_two.append(tn(grad_scores, q2))
            dv_two.append(tn(probs.astype(bf16), a2))
        dcq_ref[0, :, lanes] = (jnp.where(first_q, dq_two[0], dq_two[1]) * scaling).astype(bf16)
        dckv_ref[0, :, lanes] = (jnp.where(first_k, dk_two[0], dk_two[1]) * scaling).astype(bf16)
        dckv_ref[0, :, upper] = jnp.where(first_k, dv_two[0], dv_two[1]).astype(bf16)
    part_ref[0] = (before_ref[0] + nt(dckv_ref[0], w_pair[...])).astype(bf16)


def first_backward(n, *refs):
    order_r, ds_ref, da_ref, db_ref, first_ref, gain_ref = refs[:6]
    source, refs = refs[6 : 6 + n[0][0]], refs[6 + n[0][0] :]
    df_ref, low_ref, do_ref, dg_ref, w_out, sem = refs

    @pl.when(pl.program_id(0) == 0)
    def _():
        fetch_rows(w_out, source, n[0], order_r, OUT_AT, 0, sem)
        dg_ref[...] = jnp.zeros_like(dg_ref)
        end_fetch(w_out, sem)

    grad = da_ref[0].astype(f32) + db_ref[0].astype(f32)
    unit, inv = norm_parts(first_ref[0])
    dg_ref[0:1] += jnp.sum(grad * unit, axis=0, keepdims=True)
    grad_first = ds_ref[0].astype(f32) + norm_back(unit, inv, gain_ref[1:2], grad)
    df_ref[0] = grad_first
    low = grad_first.astype(bf16)
    low_ref[0] = low
    do_ref[0] = nt(low, w_out[...]).astype(bf16)


def attn_backward(n, *refs):
    order_c, do_ref, qkv_ref, p_ref = refs[:4]
    unit, refs = refs[4 : 4 + n[0][0]], refs[4 + n[0][0] :]
    dqkv_ref, part_ref, w_in, wide, sem = refs
    tokens = do_ref.shape[1]
    own = dqkv_ref.shape[1]
    lo = (tokens - own) // 2

    @pl.when(pl.program_id(0) == 0)
    def _():
        fetch_columns(w_in, unit, n[0], order_c, 128, sem)
        end_fetch(w_in, sem)

    first_half = lane_halves(CELLS)
    masks = half_masks()
    for block in range(tokens // CELLS):
        rows = slice(block * CELLS, (block + 1) * CELLS)
        for pair in range(PAIRS):
            lanes = slice(pair * 128, pair * 128 + 128)
            q2 = qkv_ref[0, rows, lanes]
            k2 = qkv_ref[0, rows, HALF + pair * 128 : HALF + pair * 128 + 128]
            v2 = qkv_ref[0, rows, 2 * HALF + pair * 128 : 2 * HALF + pair * 128 + 128]
            g2 = do_ref[0, rows, lanes]
            dq_two, dk_two, dv_two = [], [], []
            for side in range(2):
                probs = p_ref[0, block * HH + pair * 2 + side]
                wide_probs = probs.astype(f32)
                grad_probs = nt(g2 * masks[side], v2)
                delta = jnp.sum(wide_probs * grad_probs, axis=-1, keepdims=True)
                grad_scores = (wide_probs * (grad_probs - delta)).astype(bf16)
                dq_two.append(nn(grad_scores, k2))
                dk_two.append(tn(grad_scores, q2))
                dv_two.append(tn(probs, g2))
            wide[rows, lanes] = jnp.where(first_half, dq_two[0], dq_two[1]) * scaling
            wide[rows, HALF + pair * 128 : HALF + pair * 128 + 128] = (
                jnp.where(first_half, dk_two[0], dk_two[1]) * scaling
            )
            wide[rows, 2 * HALF + pair * 128 : 2 * HALF + pair * 128 + 128] = jnp.where(
                first_half, dv_two[0], dv_two[1]
            )
    low = wide[lo : lo + own].astype(bf16)
    dqkv_ref[0] = low
    part_ref[0] = nt(low, w_in[...]).astype(bf16)


def input_backward(x_ref, df_ref, da_ref, db_ref, gain_ref, dx_ref, dg_ref):
    @pl.when(pl.program_id(0) == 0)
    def _():
        dg_ref[...] = jnp.zeros_like(dg_ref)

    grad = da_ref[0].astype(f32) + db_ref[0].astype(f32)
    unit, inv = norm_parts(x_ref[0].astype(f32))
    dg_ref[0:1] += jnp.sum(grad * unit, axis=0, keepdims=True)
    dx_ref[0] = (df_ref[0] + norm_back(unit, inv, gain_ref[0:1], grad)).astype(bf16)


def query_back_one(n, *refs):
    order_c, one_ref, two_ref = refs[:3]
    unit, refs = refs[3 : 3 + n[0][0]], refs[3 + n[0][0] :]
    dcq_ref, part_ref, w_q, sem = refs
    fetch_columns(w_q, unit, n[0], order_c, CQ_AT, sem)
    end_fetch(w_q, sem)
    for m in range(dcq_ref.shape[0]):
        low = (one_ref[m].astype(f32) + two_ref[m].astype(f32)).astype(bf16)
        dcq_ref[m] = low
        part_ref[m] = nt(low, w_q[...]).astype(bf16)


def query_back_two(q_ref, dq_ref, da_ref, db_ref, gain_ref, out_ref, dg_ref):
    total = jnp.zeros((1, D), f32)
    for m in range(q_ref.shape[0]):
        grad = da_ref[m].astype(f32) + db_ref[m].astype(f32)
        unit, inv = norm_parts(q_ref[m].astype(f32))
        total = total + jnp.sum(grad * unit, axis=0, keepdims=True)
        out_ref[m] = (dq_ref[m].astype(f32) + norm_back(unit, inv, gain_ref[2:3], grad)).astype(bf16)
    dg_ref[...] = jnp.broadcast_to(total, dg_ref.shape)


def weight_grads(n, plan, *refs):
    order_c, order_r = refs[:2]
    count = 1 + max(max(item[0], item[1]) for item in plan)
    sides, refs = refs[2 : 2 + count], refs[2 + count :]
    outs = []
    for k in n:
        outs.append(refs[:k])
        refs = refs[k:]
    acc = refs[0]
    for left, right, unit, by_rows, col0, row0 in plan:
        height, width = sides[left].shape[1], sides[right].shape[1]
        if left == right:
            turned = jnp.concatenate([sides[left][...], jnp.zeros((120, height), f32)], axis=0).T
            acc[0:height, 0:128] = turned
            spread_columns(acc.at[:, 0:128], outs[unit], order_c, col0)
            continue
        for at in range(0, width, HALF):
            acc[0:height] = tn(sides[left][...], sides[right][:, at : at + HALF])
            if by_rows:
                spread_rows(acc, outs[unit], order_r, height, at // HALF, col0, row0)
            else:
                spread_columns(acc, outs[unit], order_c, col0 + at)


def per_device(
    patches,
    queries,
    page_rows,
    window_mask,
    query_lengths,
    plan,
    norm_attn,
    norm_mlp,
    norm_query,
    attn_input,
    attn_output,
    mlp_up,
    mlp_down,
    cross_query,
    cross_pair,
    cross_output,
    patch_cotangent,
    query_cotangent,
):
    core = lax.axis_index("section")
    zi = lax.axis_index("dp")
    qi = lax.axis_index("seq")
    nz, ns = lax.axis_size("dp"), lax.axis_size("seq")
    rows = attn_input.shape[1]
    hid = mlp_up.shape[2] // 2
    manual = rows % 16 == 0 and ns == 4 and nz & (nz - 1) == 0
    near = nz // 2
    batches, row_count, col_count = patches.shape[:3]
    tokens = row_count * col_count
    core_zero = core == 0

    def swap(x):
        return lax.ppermute(x, "section", SWAP)

    def across(x, r):
        return lax.ppermute(x, "seq", [(j, j ^ r) for j in range(ns)])

    def tied(x, after):
        return x if after is None else lax.optimization_barrier((x, after))[0]

    far = (zi // near) ^ core
    if manual:
        order_c = [((zi ^ r) * ns + (qi ^ p)) for p in range(ns) for r in range(nz)]
        order_r = [
            ((zi ^ (far * near + k)) - core * near) * ns + (qi ^ p)
            for p in range(ns)
            for k in range(near)
        ]
    else:
        order_c = order_r = [zi]
    order_s = [qi ^ p for p in range(ns)]
    order_c, order_r, order_s = (
        jnp.stack(o).astype(jnp.int32) for o in (order_c, order_r, order_s)
    )

    gain_block = jnp.stack([norm_attn[0], norm_mlp[0], norm_query[0]], axis=1)
    gain_block = jnp.pad(gain_block, ((0, 0), (0, 125)))
    win, up, cq, cp = attn_input[0], mlp_up[0], cross_query[0], cross_pair[0]

    def half_columns(side):
        def half(a, w):
            return a[:, side * w : (side + 1) * w]

        first = [half(win[:, k * D : (k + 1) * D], HALF) for k in range(3)]
        return [
            jnp.concatenate([gain_block] + first + [half(cq, HALF)], axis=1),
            jnp.concatenate([half(up, hid), half(cp[:, :D], HALF), half(cp[:, D:], HALF)], axis=1),
        ]

    halves = [half_columns(side) for side in range(2)]

    def fold(w):
        return jnp.stack(
            [
                jnp.concatenate(
                    [
                        w[b * rows : (b + 1) * rows, side * HALF : (side + 1) * HALF]
                        for b in range(w.shape[0] // rows)
                    ],
                    axis=1,
                )
                for side in range(2)
            ]
        )

    down_co = jnp.concatenate([mlp_down[0], cross_output[0]], axis=0)

    def z_pairs(bit):
        return [
            (c * nz + j, c * nz + (j ^ bit))
            for c in range(2)
            for j in range(c * near, (c + 1) * near)
        ]

    def z_step(parts, bit, after):
        out = []
        for stack, by_rows in parts:
            stack = tied(stack, after)
            if not by_rows:
                got = lax.ppermute(stack, "dp", [(j, j ^ bit) for j in range(nz)])
                out.append((jnp.concatenate([stack, got]), False, got))
                continue
            got = lax.ppermute(stack, ("section", "dp"), z_pairs(bit))
            if bit < near:
                stack = jnp.concatenate([stack, got])
            else:
                stack = jnp.where(far == 0, stack, got)
                stack = stack.reshape((nz,) + stack.shape[2:])
            out.append((stack, True, got))
        return [o[:2] for o in out], tuple(o[2] for o in out)

    units = [[None] * 3 for _ in range(2)]
    counts = [[None] * 3 for _ in range(2)]
    if manual:
        col_send = [jnp.where(core_zero, b, a) for a, b in zip(*halves)]
        col_mine = [jnp.where(core_zero, a, b) for a, b in zip(*halves)]
        row_mine = [fold(attn_output[0]), fold(down_co)]
        col_recv = [swap(col_send[0])]
        row_recv = [swap(row_mine[0])]
        col_recv.append(swap(tied(col_send[1], (col_recv[0], row_recv[0]))))
        row_recv.append(swap(tied(row_mine[1], (col_recv[0], row_recv[0]))))

        queue = []
        for layer in range(2):
            own_layer = core == layer
            cols = [jnp.where(own_layer, a, b)[None] for a, b in zip(col_mine, col_recv)]
            folded = [jnp.where(own_layer, a, b)[None] for a, b in zip(row_mine, row_recv)]
            queue += [[(cols[0], False), (folded[0], True)], [(cols[1], False)], [(folded[1], True)]]
        bits = []
        while 2 ** len(bits) < nz:
            bits.append(2 ** len(bits))
        last_rows = queue.pop()[0][0][0]
        count = len(queue)

        def early_steps(k, after):
            tokens_of = ()
            for bit in bits[:-1]:
                queue[k], after = z_step(queue[k], bit, after)
                tokens_of += after
            return tokens_of

        lead = early_steps(0, None)
        queue[0], _ = z_step(queue[0], bits[-1], lead)
        ahead = early_steps(1, lead)
        token = ()
        corners = [across(last_rows, r) for r in range(1, ns)]
        messages = []
        from_x = from_y = jnp.zeros((nz, rows, 0), bf16)
        cut = 0
        before = None
        for k in range(count + 1):
            low, high = from_x[..., :cut], from_y[..., cut:]
            x_parts, y_parts = [high], [low]
            own = None
            if k < count:
                parts = [stack for stack, _ in queue[k]]
                own = parts[0] if len(parts) == 1 else jnp.concatenate(parts, axis=2)
                own = tied(own, token)
                x_parts.append(own)
                y_parts.append(own)
            sent_x, sent_y = jnp.concatenate(x_parts, axis=2), jnp.concatenate(y_parts, axis=2)
            messages.append((sent_x, sent_y))
            got_x, got_y = across(sent_x, 1), across(sent_y, 2)
            if k + 1 < count:
                queue[k + 1], got = z_step(queue[k + 1], bits[-1], (token, ahead))
                ahead = early_steps(k + 2, got) if k + 2 < count else got
            if before is not None:
                b = k - 1
                units[b // 3][b % 3] = before[0] + [got_y, got_x]
                counts[b // 3][b % 3] = (5,) + before[1] + (cut,)
            if own is None:
                break
            before = ([own, got_x, got_y], (high.shape[2], low.shape[2]))
            from_x, from_y = got_x[..., high.shape[2] :], got_y[..., low.shape[2] :]
            cut = own.shape[2] // 256 * 128
            token = (got_x, got_y) + (tuple(corners) if k == 0 else ())
        stack = jnp.stack([last_rows] + corners)[None]
        stack = tied(stack, ahead)
        for bit in bits:
            got = lax.ppermute(stack, ("section", "dp"), z_pairs(bit))
            stack = jnp.concatenate([stack, got]) if bit < near else jnp.where(far == 0, stack, got)
        units[1][2] = [stack]
        counts[1][2] = (1, 0, 0, 0)
        counts = tuple(tuple(c) for c in counts)
    else:

        def gather_all(x):
            return lax.all_gather(
                lax.all_gather(x, ("dp", "seq"), axis=0, tiled=True), "section", axis=0
            )

        whole_cols = [[gather_all(h[k]) for h in halves] for k in range(2)]
        whole_rows = [gather_all(x) for x in (attn_output[0], mlp_down[0], cross_output[0])]
        for layer in range(2):
            cols = [jnp.where(core_zero, a[layer], b[layer]) for a, b in whole_cols]
            mine = [
                lax.dynamic_slice_in_dim(w[layer], core * (w.shape[1] // 2), w.shape[1] // 2, 0)
                for w in whole_rows
            ]
            units[layer] = [[cols[0], mine[0]], [cols[1]], [jnp.concatenate(mine[1:], axis=0)]]
        counts = (((2, 0, 0, 0), (1, 0, 0, 0), (1, 0, 0, 0)),) * 2
        messages = [()] * 7

    order = jnp.arange(batches)
    inverse = jnp.sum(jnp.where(plan[0][None, :] == order[:, None], order[None, :], 0), axis=1)
    query_start = jnp.take(queries, inverse, axis=0)
    query_given = jnp.take(query_cotangent, inverse, axis=0)
    lengths = jnp.take(query_lengths, inverse)
    live = (jnp.arange(NQ)[None, :] < lengths[:, None]).astype(f32)[:, :, None]
    window_rows = qi * (row_count // WIN) + jnp.arange(row_count // WIN)
    marks = (window_rows[None, :, None] < page_rows[:, None, None]) & (window_mask == 1)
    valid = jnp.repeat(jnp.repeat(marks, WIN, axis=1), WIN, axis=2)
    valid = valid.reshape(batches, 1, tokens).astype(f32)
    blocks_wide = (row_count + WIN) // WIN
    cell = jnp.arange(CELLS)
    frame_row = qi * row_count - WIN // 2 + jnp.arange(blocks_wide)[:, None] * WIN + cell // WIN
    inside = (frame_row >= 0) & (frame_row < row_count * ns)
    side_of = (cell % WIN) < WIN // 2
    same = side_of[:, None] == side_of[None, :]
    mask = jnp.where(inside[:, None, :] & same[None], 0.0, hidden_value).astype(f32)

    pages = patches.reshape(batches, tokens, D)
    given = patch_cotangent.reshape(batches, tokens, D)

    def widened(edge_source):
        top = lax.ppermute(
            edge_source[:, tokens - RIM :], "seq", [(j, j + 1) for j in range(ns - 1)]
        )
        bottom = lax.ppermute(edge_source[:, :RIM], "seq", [(j + 1, j) for j in range(ns - 1)])
        return jnp.concatenate([top, edge_source, bottom], axis=1)

    def pieces(unit):
        return [(piece, ANY) for piece in unit]

    def shaped(shape, dtype, batched=True):
        return (shape, dtype, per_batch(shape) if batched else whole(shape))

    def batched(a):
        return (a, per_batch(a.shape))

    def full(a):
        return (a, whole(a.shape))

    dma = pltpu.SemaphoreType.DMA

    def forward(layer, x, query, query_parts):
        u, n = units[layer], counts[layer]
        shifted = layer == 1
        wide_x = wide_x1 if shifted else x
        wide = wide_x.shape[1]
        blocks = wide // CELLS
        wide_x = tied(wide_x, messages[2 + 3 * layer])
        ins = [(order_c, SMEM), (order_r, SMEM), batched(wide_x)]
        if shifted:
            ins.append(full(mask))
        h1, qkv, probs, mixed, part, gains = run(
            partial(attn_forward, n, shifted),
            "attn_forward",
            (batches,),
            ins + pieces(u[0]),
            [
                shaped((batches, tokens, D), bf16),
                shaped((batches, wide, 3 * HALF), bf16),
                shaped((batches, blocks * HH, CELLS, CELLS), bf16),
                shaped((batches, tokens, HALF), bf16),
                shaped((batches, tokens, D), bf16),
                shaped((8, D), f32, False),
            ],
            [
                pltpu.VMEM((D, 128 + 3 * HALF), bf16),
                pltpu.VMEM((HALF, D), bf16),
                pltpu.VMEM((wide, HALF), f32),
                pltpu.VMEM((wide, D), f32),
                dma,
                dma,
            ],
            10,
        )
        other = swap(part)
        if query_parts is not None:
            query_parts = query_parts(wide_x, part)
        q_ins = [(order_c, SMEM), full(query), full(gains)]
        q_outs = [
            shaped((batches, NQ, D), bf16, False),
            shaped((batches, NQ, HALF), bf16, False),
        ]
        if query_parts is not None:
            q_ins += [full(query_parts[0]), full(query_parts[1]), full(live)]
            q_outs = [shaped((batches, NQ, D), bf16, False)] + q_outs
        got = run(
            partial(query_in, n, query_parts is not None),
            "query_in",
            (),
            q_ins + pieces(u[0]),
            q_outs,
            [pltpu.VMEM((D, HALF), bf16), dma],
            2.5,
        )
        if query_parts is not None:
            query, got = got[0], got[1:]
        hq, cq_now = got
        first, h2, slope, act, second_part, ckv, e, o = run(
            partial(mlp_forward, n),
            "mlp_forward",
            (batches,),
            [
                (order_c, SMEM),
                (order_r, SMEM),
                batched(tied(x, messages[min(4 + 2 * layer, len(messages) - 1)])),
                batched(part),
                batched(other),
                full(gains),
                batched(cq_now),
                batched(valid),
            ]
            + pieces(u[1])
            + pieces(u[2]),
            [
                shaped((batches, tokens, D), f32),
                shaped((batches, tokens, D), bf16),
                shaped((batches, tokens, hid), bf16),
                shaped((batches, tokens, hid), bf16),
                shaped((batches, tokens, D), bf16),
                shaped((batches, tokens, D), bf16),
                shaped((batches, HH, NQ, tokens), bf16),
                shaped((batches, NQ, HALF + 128), bf16),
            ],
            [pltpu.VMEM((D, hid + D), bf16), pltpu.VMEM((hid, D), bf16), dma, dma],
            14,
        )
        second_other = swap(second_part)
        x_next = (first + (second_part.astype(f32) + second_other.astype(f32))).astype(bf16)
        kept = dict(
            x=x, query=query, h1=h1, qkv=qkv, probs=probs, mixed=mixed, gains=gains, hq=hq,
            cq=cq_now, first=first, h2=h2, slope=slope, act=act, ckv=ckv, e=e,
        )

        def query_rest(start, finish):
            sent = tied(o, start)
            os = [sent] + [across(sent, r) for r in range(1, ns)]
            os[1:] = tied(os[1:], finish)
            att, att_low, coef, q_part = run(
                partial(query_out, n, ns),
                "query_out",
                (),
                [(order_r, SMEM), (order_s, SMEM)]
                + [full(a) for a in os]
                + pieces(u[2]),
                [
                    shaped((batches, NQ, HALF), f32, False),
                    shaped((batches, NQ, HALF), bf16, False),
                    shaped((batches, NQ, 128), f32, False),
                    shaped((batches, NQ, D), bf16, False),
                ],
                [
                    pltpu.VMEM((HALF, D), bf16),
                    pltpu.VMEM((ns, batches, NQ, HALF + 128), bf16),
                    dma,
                ],
                4.5,
            )
            kept.update(att=att, att_low=att_low, coef=coef)
            return q_part, swap(q_part)

        return x_next, query_rest, kept

    def sums(kernel_plan, sides, shapes, height, name, after=None):
        flat = run(
            partial(weight_grads, tuple(len(unit) for unit in shapes), kernel_plan),
            name,
            (),
            [(order_c, SMEM), (order_r, SMEM)] + [full(s) for s in sides],
            [shaped(shape, bf16, False) for unit in shapes for shape in unit],
            [pltpu.VMEM((height, HALF), f32)],
            12 if height > D else 6,
        )
        out = []
        for unit in shapes:
            out.append(flat[: len(unit)])
            flat = flat[len(unit) :]
        return out

    def unit_shapes(cols, row_height):
        if not manual:
            shapes = [(D, cols)] if cols else []
            return shapes + ([(row_height, D)] if row_height else [])
        width = cols + row_height // (rows * nz * ns // 2) * HALF
        return [(nz, rows, width)] * 3 + [(near, rows, width)] * 2

    operands = {}

    def reduce_one(unit, after):
        own, one, two, low, high = unit
        low, high = tied((low, high), after)
        low, high = across(low, 2), across(high, 1)
        return (own, one, two, low, high), (low, high)

    def reduce_two(unit, after):
        own, one, two, low, high = tied(unit, after)
        one = jnp.concatenate([one[:near] + low, one[near:]])
        two = jnp.concatenate([two[:near], two[near:] + high])
        operands[2] = (one, two)
        one, two = across(one, 1), across(two, 2)
        return (own, one, two), (one, two)

    def reduce_three(unit, cols, after):
        own, one, two = tied(unit, after)
        total = own.astype(f32) + one.astype(f32) + two.astype(f32)
        col, row = total[..., :cols], total[..., cols:]
        sent = col[near:].astype(bf16)
        operands[3] = sent
        got_col = lax.ppermute(sent, "dp", [(j, j ^ near) for j in range(nz)])
        sent = row.astype(bf16)
        got_row = lax.ppermute(sent, ("section", "dp"), [(b, a) for a, b in z_pairs(near)])
        return [(col[:near], got_col), (row, got_row)], (got_col, got_row)

    def reduce_four(parts, after):
        out = []
        token = ()
        for by_rows, (total, got) in enumerate(tied(parts, after)):
            total = total + got.astype(f32)
            if by_rows:
                total = total.reshape((near, 2) + total.shape[1:])
            bit = near // 2
            while bit:
                sent = total[bit:].astype(bf16)
                pairs = [(b, a) for a, b in z_pairs(bit)] if by_rows else [
                    (j, j ^ bit) for j in range(nz)
                ]
                got = lax.ppermute(sent, ("section", "dp") if by_rows else "dp", pairs)
                token += (got,)
                total = total[:bit] + got.astype(f32)
                bit //= 2
            out.append(total[0])
        return out, token

    def unfold(row):
        blocks = row.shape[2] // HALF
        return jnp.concatenate(
            [
                jnp.concatenate([row[side, :, b * HALF : (b + 1) * HALF] for side in range(2)], axis=1)
                for b in range(blocks)
            ],
            axis=0,
        )

    def reduce_plain(unit, cols, heights):
        out = []
        if cols:
            out.append(lax.psum_scatter(unit[0], ("dp", "seq"), scatter_dimension=0, tiled=True))
        if len(unit) > 1 or not cols:
            cut = heights[0] * nz * ns // 2
            pieces_of = [unit[-1][:cut], unit[-1][cut:]]
            out += [
                lax.psum_scatter(
                    lax.all_gather(piece, "section", axis=0, tiled=True),
                    ("dp", "seq"),
                    scatter_dimension=0,
                    tiled=True,
                )
                for piece in pieces_of
            ]
        return [o.astype(f32) for o in out]

    share = 1.0 / ns

    def mlp_gradient(layer, grad_patch, slope):
        u, n = units[layer], counts[layer]
        return run(
            partial(mlp_backward, n),
            "mlp_backward",
            (batches,),
            [(order_c, SMEM), (order_r, SMEM), batched(grad_patch), batched(slope)]
            + pieces(u[1])
            + pieces(u[2]),
            [shaped((batches, tokens, hid), bf16), shaped((batches, tokens, D), f32)],
            [pltpu.VMEM((D, hid), bf16), pltpu.VMEM((hid, D), bf16), dma, dma],
            9,
        )

    def backward(layer, grad_patch, grad_query, kept, emit, mlp_part):
        u, n = units[layer], counts[layer]
        shifted = layer == 1
        gains = kept["gains"]
        du, before = mlp_part
        dckv, dcq_part, part, dcross = run(
            partial(cross_backward, n, hid),
            "cross_backward",
            (batches,),
            [(order_c, SMEM), (order_r, SMEM)]
            + [
                batched(a)
                for a in (
                    before, kept["e"], kept["coef"], grad_query, live, kept["att"], kept["cq"],
                    kept["ckv"],
                )
            ]
            + pieces(u[1])
            + pieces(u[2]),
            [
                shaped((batches, tokens, D), bf16),
                shaped((batches, NQ, HALF), bf16),
                shaped((batches, tokens, D), bf16),
                shaped((batches, NQ, D), bf16),
            ],
            [pltpu.VMEM((D, D), bf16), pltpu.VMEM((HALF, D), bf16), dma, dma],
            6,
        )
        emit("mlp", part)
        other = swap(part)
        dcq_got = across(dcq_part, 1)

        def flat(a):
            return a.reshape(-1, a.shape[-1])

        row_at = hid + D if manual else 0
        row_base = hid // (nz * ns // 2) // rows * HALF if manual else 0
        early = sums(
            (
                (0, 1, 0, False, 0, 0),
                (0, 2, 0, False, hid, 0),
                (3, 4, 0, True, row_at, 0),
                (5, 6, 0, True, row_at + row_base, hid),
            ),
            [
                flat(kept["h2"]), flat(du), flat(dckv), flat(kept["act"]), flat(grad_patch),
                flat(kept["att_low"]), flat(dcross * jnp.asarray(share, bf16)),
            ],
            [unit_shapes(hid + D, hid + HALF)],
            hid,
            "early_grads",
        )
        part = tied(part, early[0][0])
        def dcq_steps(part_of, got, after):
            bit = 2
            while bit < ns:
                got = tied(got, after)
                part_of = (part_of.astype(f32) + got.astype(f32)).astype(bf16)
                got = across(part_of, bit)
                bit *= 2
            return part_of, got

        if shifted:
            dcq_part, dcq_got = dcq_steps(dcq_part, dcq_got, early[0][0])
        emit("early", (early[0], dcq_part if shifted else early[0][0]))
        if not shifted:
            part = tied(part, operands.get(3, ()))
        grad_first, first_low, grad_mixed, dg_mlp = run(
            partial(first_backward, n),
            "first_backward",
            (batches,),
            [(order_r, SMEM)]
            + [batched(a) for a in (grad_patch, part, other, kept["first"])]
            + [full(gains)]
            + pieces(u[0]),
            [
                shaped((batches, tokens, D), f32),
                shaped((batches, tokens, D), bf16),
                shaped((batches, tokens, HALF), bf16),
                shaped((8, D), f32, False),
            ],
            [pltpu.VMEM((HALF, D), bf16), dma],
            5.6,
        )
        wide_grad = widened(grad_mixed) if shifted else grad_mixed
        emit("first", grad_mixed)
        wide = wide_grad.shape[1]
        dqkv, part = run(
            partial(attn_backward, n),
            "attn_backward",
            (batches,),
            [(order_c, SMEM)]
            + [batched(a) for a in (wide_grad, kept["qkv"], kept["probs"])]
            + pieces(u[0]),
            [shaped((batches, tokens, 3 * HALF), bf16), shaped((batches, tokens, D), bf16)],
            [pltpu.VMEM((D, 3 * HALF), bf16), pltpu.VMEM((wide, 3 * HALF), f32), dma],
            15,
        )
        emit("attn", part)
        other = swap(part)
        if not shifted:
            dcq_part, dcq_got = dcq_steps(dcq_part, dcq_got, dqkv)
            emit("dcq", dcq_part)
            dcq_got = tied(dcq_got, operands.get(2, ()))
        dcq_got = tied(dcq_got, dqkv)
        dcq, q_part = run(
            partial(query_back_one, n),
            "query_back_one",
            (),
            [(order_c, SMEM), full(dcq_part), full(dcq_got)] + pieces(u[0]),
            [shaped((batches, NQ, HALF), bf16, False), shaped((batches, NQ, D), bf16, False)],
            [pltpu.VMEM((D, HALF), bf16), dma],
            2.5,
        )
        q_other = swap(q_part)
        last_x = kept["x"]
        dx, dg_attn = run(
            input_backward,
            "input_backward",
            (batches,),
            [batched(a) for a in (last_x, grad_first, part, other)] + [full(gains)],
            [shaped((batches, tokens, D), bf16), shaped((8, D), f32, False)],
            [],
            3,
        )
        dq, dg_query = run(
            query_back_two,
            "query_back_two",
            (),
            [full(a) for a in (kept["query"], grad_query, q_part, q_other, gains)],
            [shaped((batches, NQ, D), bf16, False), shaped((8, D), f32, False)],
            [],
            1,
        )
        dgains = jnp.concatenate([dg_attn[0:1], dg_mlp[0:1], dg_query[0:1] * share], axis=0)
        emit(
            "late",
            ([
                flat(kept["h1"]), flat(dqkv), flat(kept["hq"]), flat(dcq * jnp.asarray(share, bf16)),
                flat(kept["mixed"]), flat(first_low),
            ], dgains),
        )
        return dx, dq

    x1, q_parts, kept0 = forward(0, pages, query_start, None)
    wide_x1 = widened(x1)
    x2, q_rest, kept1 = forward(1, x1, query_start, q_parts)
    mlp_part = mlp_gradient(1, given, kept1["slope"])
    q_parts_two = q_rest((), mlp_part[0])
    query_last = (
        kept1["query"].astype(f32)
        + live * (q_parts_two[0].astype(f32) + q_parts_two[1].astype(f32))
    ).astype(bf16)

    widths = (hid + D, hid + D, 8 * HALF + 128)
    out_rows = attn_output.shape[1]
    heights = [(mlp_down.shape[1], cross_output.shape[1])] * 2 + [(out_rows, out_rows)]
    state = [None] * 3
    late_sides = []

    rounds = [()]

    def one_round(*items, after=()):
        for unit, step in items:
            now = state[unit]
            if not manual:
                if step == 4:
                    now = reduce_plain(now, widths[unit], heights[unit])
            elif step == 1:
                now, got = reduce_one(now, after)
            elif step == 2:
                now, got = reduce_two(now, after)
            elif step == 3:
                now, got = reduce_three(now, widths[unit], after)
            else:
                now, got = reduce_four(now, after)
                rows_of = unfold(now[1])
                cut = heights[unit][0]
                now = [now[0], rows_of[:cut], rows_of[cut:]]
            state[unit] = now
            rounds[unit, step] = got if manual else ()

    rounds = {}

    def emit_late_layer(what, value):
        if what == "early":
            state[1] = value[0]
            one_round((1, 1), after=value[1])
        elif what == "attn":
            one_round((1, 2), after=value)
        elif what == "late":
            late_sides.extend(value)

    def emit_first_layer(what, value):
        if what == "early":
            state[0] = value[0]
            one_round((0, 1), after=value[1])
            one_round((1, 3), after=value[1])
        elif what == "dcq":
            one_round((0, 2), after=value)
        elif what == "late":
            sides = late_sides[0] + value[0]
            gain_sums = jnp.concatenate(
                [value[1], late_sides[1], jnp.zeros((2, D), f32)], axis=0
            )
            row_at = 8 * HALF + 128
            (state[2],) = sums(
                [
                    item
                    for k in range(2)
                    for item in (
                        (6 * k, 6 * k + 1, 0, False, 4 * HALF * k, 0),
                        (6 * k + 2, 6 * k + 3, 0, False, 4 * HALF * k + 3 * HALF, 0),
                        (6 * k + 4, 6 * k + 5, 0, True, row_at + HALF * k, HALF * k),
                    )
                ]
                + [(12, 12, 0, False, 8 * HALF, 0)],
                sides + [gain_sums],
                [unit_shapes(8 * HALF + 128, 2 * HALF)],
                D,
                "late_grads",
            )
            one_round((2, 1))

    query_given = tied(query_given, x2)
    kept1["h2"] = tied(kept1["h2"], query_last)
    dx1, dq1 = backward(1, given, query_given, kept1, emit_late_layer, mlp_part)
    dx0, dq0 = backward(
        0, dx1, dq1, kept0, emit_first_layer, mlp_gradient(0, dx1, kept0["slope"])
    )
    one_round((1, 4), after=state[2][0])
    one_round((0, 3), after=(state[2][0], rounds[1, 3]))
    one_round((2, 2), after=(rounds[0, 2], operands.get(3, ())))
    one_round((2, 3), after=rounds[0, 3])
    one_round((0, 4), after=rounds[2, 2])

    def handed(low, high):
        return [swap(jnp.where(core_zero, b, a)) for a, b in zip(low, high)]

    got_early = handed(
        [state[0][0], jnp.concatenate(state[0][1:], axis=0)],
        [state[1][0], jnp.concatenate(state[1][1:], axis=0)],
    )
    one_round((2, 4), after=(rounds[0, 4], got_early))
    cols, rows_of = state[2][0], state[2][1:]
    low_cols, high_cols = cols[:, : 4 * HALF], cols[:, 4 * HALF : 8 * HALF]
    got_late = handed([high_cols, rows_of[1]], [low_cols, rows_of[0]])
    own_early = [jnp.where(core_zero, a, b) for a, b in zip(state[0], state[1])]
    own_late = [jnp.where(core_zero, high_cols, low_cols)]
    own_late.append(jnp.where(core_zero, rows_of[1], rows_of[0]))
    cut = heights[0][0]
    mine = own_early + own_late
    theirs = [got_early[0], got_early[1][:cut], got_early[1][cut:]] + got_late

    def col_halves(k):
        low = jnp.where(core_zero, mine[k], theirs[k])
        high = jnp.where(core_zero, theirs[k], mine[k])
        return low, high

    holder = zi // near if manual else core

    def row_block(k):
        return jnp.where(holder == core, mine[k], theirs[k])

    low, high = col_halves(0)
    grad_up = jnp.concatenate([low[:, :hid], high[:, :hid]], axis=1)
    grad_pair = jnp.concatenate(
        [
            low[:, hid : hid + HALF], high[:, hid : hid + HALF],
            low[:, hid + HALF :], high[:, hid + HALF :],
        ],
        axis=1,
    )
    low, high = col_halves(3)
    grad_in = jnp.concatenate(
        [side[:, k * HALF : (k + 1) * HALF] for k in range(3) for side in (low, high)], axis=1
    )
    grad_cq = jnp.concatenate([low[:, 3 * HALF :], high[:, 3 * HALF :]], axis=1)
    grad_down, grad_co, grad_out = row_block(1), row_block(2), row_block(4)

    gain_rows = jnp.where(core_zero, cols[:, 8 * HALF : 8 * HALF + 3], cols[:, 8 * HALF + 3 : 8 * HALF + 6])
    own_gains = gain_rows.T

    patch_ends = jnp.where(core_zero, dx0, x2).reshape(1, batches, row_count, col_count, D)
    query_ends = jnp.take(jnp.where(core_zero, dq0, query_last), plan[0], axis=0)[None]
    return (
        patch_ends,
        query_ends,
        own_gains[0:1],
        own_gains[1:2],
        own_gains[2:3],
        grad_in[None],
        grad_out[None],
        grad_up[None],
        grad_down[None],
        grad_cq[None],
        grad_pair[None],
        grad_co[None],
    )


def solution(mesh):
    return jax.shard_map(
        per_device,
        mesh=mesh,
        in_specs=(
            P("dp", "seq", None, None),
            P("dp", None, None),
            P("dp"),
            P("dp", "seq", None),
            P("dp"),
            P("dp", None),
            P("section", ("dp", "seq")),
            P("section", ("dp", "seq")),
            P("section", ("dp", "seq")),
            P("section", ("dp", "seq"), None),
            P("section", ("dp", "seq"), None),
            P("section", ("dp", "seq"), None),
            P("section", ("dp", "seq"), None),
            P("section", ("dp", "seq"), None),
            P("section", ("dp", "seq"), None),
            P("section", ("dp", "seq"), None),
            P("dp", "seq", None, None),
            P("dp", None, None),
        ),
        out_specs=(
            P("section", "dp", "seq", None, None),
            P("section", "dp", None, None),
            P("section", ("dp", "seq")),
            P("section", ("dp", "seq")),
            P("section", ("dp", "seq")),
            P("section", ("dp", "seq"), None),
            P("section", ("dp", "seq"), None),
            P("section", ("dp", "seq"), None),
            P("section", ("dp", "seq"), None),
            P("section", ("dp", "seq"), None),
            P("section", ("dp", "seq"), None),
            P("section", ("dp", "seq"), None),
        ),
        check_vma=False,
    )
```
